32 devices in a mesh: grp: 2 (over x), shell: 16 (over z, y, core).
Axes of the slice: x: 2, y: 2, z: 4, core: 2. Of those that a mesh axis runs over, the one named last changes fastest.
Arguments:
- pair_coef: bfloat16 [1024, 8, 16, 1024], P(('grp', 'shell')), parts along dimension 0, may hold values from -6 to 6
- panel_pool: bfloat16 [16, 512, 512], P('shell'), may hold values from -0.0625 to 0.0625
- degree_owner: int32 [16], replicated, may hold values from 0 to 15, as said below
- batch_order: int32 [8], replicated, may hold values from 0 to 7, each once
Outputs:
- scores: float32 [2, 1024, 4, 2, 512], P(None, ('grp', 'shell')), parts along dimension 1
The draws below stay inside these ranges and needn't reach their ends.
There are 2 independent parts, one for each index of `grp`. The reference program is written for one: setup_inputs(seed, part) draws one part's arguments, and reference() takes and returns one part's arrays. A program takes and returns all parts, laid end to end along the dimension named above; an argument that names none is the same for every part. Nothing has to cross between parts.
Inputs may be any that keep to these rules, and one draw needn't show every extreme that they name: `degree_owner`: the entries are distinct slot numbers; slots that no degree names are not read.
All inputs are finite; a program needn't handle non-finite values.
Results may differ from the reference program's by a relative error of at most 0.0003.
Values may be sent and summed in bfloat16 or wider, within the bound.
No kernel may reach another device: no remote copies, remote signals or barrier semaphores. Data moves between devices by JAX's collectives and lax.ppermute only.
A program may use at most 128 MiB of HBM per device.

```python
import jax
import jax.numpy as jnp
import numpy as np

ORD = 512
K = 512
NDEG = 16
TB = 4
SHELLS = 8
N_SHELL = 16


def draw_degree_owner(key, part):
    return jax.random.permutation(key, N_SHELL)[:NDEG].astype(jnp.int32)


def steps_of(key, extent, shards, smallest, high):
    factor_of = 1.0
    for axis_at, shards_of in shards:
        heights = jax.random.uniform(jax.random.fold_in(jax.random.fold_in(key, 6), axis_at), (shards_of,), jnp.float32, smallest / len(shards), high / len(shards))
        factor_of = factor_of * jnp.repeat(jnp.exp(heights), extent[axis_at] // shards_of).reshape((-1,) + (1,) * (len(extent) - 1 - axis_at))
    return factor_of


def gaussian(key, extent, spread, bound, pieces=(), held_as=jnp.bfloat16):
    drawn = spread * jax.random.normal(key, extent, jnp.float32)
    if pieces:
        drawn = drawn * steps_of(key, extent, pieces, -0.22, 0.18)
    return jnp.clip(drawn, -bound, bound).astype(held_as)


def setup_inputs(seed: int = 0, part: int = 0) -> dict:
    splits = jax.random.split(jax.random.key(seed), 5)
    own_keys = jax.random.split(jax.random.fold_in(splits[4], part), 5)
    pair_coef = gaussian(own_keys[0], (K, SHELLS, NDEG, 2 * ORD), 1.0, 6.0, ((0, 16),))
    panel_pool = gaussian(splits[1], (N_SHELL, ORD, ORD), (ORD * NDEG) ** -0.5, 0.0625, ((0, 16),))
    degree_owner = draw_degree_owner(jax.random.fold_in(splits[4], 71), part)
    batch_order = jax.random.permutation(splits[3], SHELLS).astype(jnp.int32)
    return {"pair_coef": pair_coef, "panel_pool": panel_pool, "degree_owner": degree_owner, "batch_order": batch_order}


def reference(pair_coef, panel_pool, degree_owner, batch_order):
    rows = pair_coef[:, batch_order]
    rows = rows.reshape(K, 2, TB, NDEG, 2 * ORD).transpose(1, 0, 2, 3, 4)
    total = jnp.zeros((2 * K * TB * 2, ORD), jnp.float32)
    for degree in range(NDEG):
        panel = panel_pool[degree_owner[degree]]
        piece = rows[:, :, :, degree, :].reshape(-1, ORD)
        total = total + jnp.dot(piece, panel, preferred_element_type=jnp.float32)
    proj = total.reshape(2, K, TB, 2, ORD)
    wave = proj[:, :, :, 0, :] + 1j * proj[:, :, :, 1, :]
    spec = jnp.fft.fft(wave, axis=1) / np.sqrt(K)
    nbits = N_SHELL.bit_length() - 1
    order_list = []
    for device in range(N_SHELL):
        flipped = 0
        for bit in range(nbits):
            flipped = flipped | (device >> bit & 1) << nbits - 1 - bit
        for inner in range(K // N_SHELL):
            order_list.append(flipped + N_SHELL * inner)
    spec = spec[:, np.array(order_list)]
    return jnp.stack([jnp.real(spec), jnp.imag(spec)], axis=3).astype(jnp.float32)
```

```python
import functools
import math

import jax
import jax.numpy as jnp
from jax import lax
from jax.experimental import pallas as pl
from jax.experimental.pallas import tpu as pltpu
from jax.sharding import PartitionSpec as P


def broadcast(value, axis, root):
    mine = lax.axis_index(axis) == root
    return lax.psum(jnp.where(mine, value, jnp.zeros_like(value)), axis)


def partner(value, axis, distance):
    mask = 2**distance
    pairs = [(source, source ^ mask) for source in range(lax.axis_size(axis))]
    return lax.ppermute(value, axis, pairs)


def rotate(real_part, imag_part, cosine, sine):
    return (real_part * cosine - imag_part * sine, real_part * sine + imag_part * cosine)


def general(pair_coef, panel_pool, degree_owner, batch_order):
    local_orders = pair_coef.shape[0]
    degrees = pair_coef.shape[2]
    width = pair_coef.shape[3] // 2
    batch_rows = batch_order.shape[0] // 2
    devices = lax.axis_size("shell")
    total_orders = local_orders * devices
    first = jnp.take(pair_coef, batch_order[:batch_rows], axis=1)
    second = jnp.take(pair_coef, batch_order[batch_rows:], axis=1)
    rows = jnp.stack([first, second])

    def add_degree(degree, total):
        panel = broadcast(panel_pool[0], "shell", degree_owner[degree])
        piece = lax.dynamic_index_in_dim(rows, degree, axis=3, keepdims=False).reshape(-1, width)
        return total + jnp.dot(piece, panel, preferred_element_type=jnp.float32)

    total = lax.fori_loop(
        0, degrees, add_degree, jnp.zeros((2 * local_orders * batch_rows * 2, width), jnp.float32)
    )
    proj = total.reshape(2, local_orders, batch_rows, 2, width)
    nbits = devices.bit_length() - 1
    high = lax.Precision.HIGHEST
    me = lax.axis_index("shell")
    blocks = proj
    for bit in reversed(range(nbits)):
        other = partner(blocks, "shell", bit)
        upper = me >> bit & 1 == 1
        lower_val = jnp.where(upper, other, blocks)
        upper_val = jnp.where(upper, blocks, other)
        summed = lower_val + upper_val
        differ = lower_val - upper_val
        twist = (me % (1 << bit)).astype(jnp.float32)
        angle = -2.0 * math.pi * twist / float(2 << bit)
        new_real, new_imag = rotate(
            differ[:, :, :, 0], differ[:, :, :, 1], jnp.cos(angle), jnp.sin(angle)
        )
        turned = jnp.stack([new_real, new_imag], axis=3)
        blocks = jnp.where(upper, turned, summed)
    flipped = jnp.zeros((), jnp.int32)
    for bit in range(nbits):
        flipped = flipped | (me >> bit & 1) << nbits - 1 - bit
    inner = lax.iota(jnp.int32, local_orders)
    freq = flipped + devices * inner
    phase = inner[None, :] * freq[:, None] % total_orders
    angle = -2.0 * math.pi * phase.astype(jnp.float32) / float(total_orders)
    cosine = jnp.cos(angle)
    sine = jnp.sin(angle)
    real_part = blocks[:, :, :, 0]
    imag_part = blocks[:, :, :, 1]
    out_real = jnp.einsum("gr,brtj->bgtj", cosine, real_part, precision=high) - jnp.einsum(
        "gr,brtj->bgtj", sine, imag_part, precision=high
    )
    out_imag = jnp.einsum("gr,brtj->bgtj", sine, real_part, precision=high) + jnp.einsum(
        "gr,brtj->bgtj", cosine, imag_part, precision=high
    )
    result = jnp.stack([out_real, out_imag], axis=3)
    return result * (1.0 / math.sqrt(total_orders))


STEPS = 16.0
TOP = 32000.0
LANES = 128


def bit_reverse(value, nbits):
    flipped = 0
    for bit in range(nbits):
        flipped = flipped | (value >> bit & 1) << nbits - 1 - bit
    return flipped


def sort_kernel(perm_ref, coef_ref, out_ref):
    moved = jnp.dot(perm_ref[...], coef_ref[...], preferred_element_type=jnp.float32)
    out_ref[...] = moved.astype(out_ref.dtype).reshape(out_ref.shape)


def sort_rows(pair_coef, batch_order):
    orders, shells, degrees, width = pair_coef.shape
    group = 16 // shells
    rows = group * shells * degrees
    out_at = lax.iota(jnp.int32, rows)
    in_at = out_at
    out_degree, out_order, out_t = out_at // (group * shells), out_at // shells % group, out_at % shells
    in_degree, in_order, in_shell = in_at % degrees, in_at // (degrees * shells), in_at // degrees % shells
    wanted = jnp.zeros((rows,), jnp.int32)
    for t in range(shells):
        wanted = jnp.where(out_t == t, batch_order[t], wanted)
    perm = (
        (out_degree[:, None] == in_degree[None, :])
        & (out_order[:, None] == in_order[None, :])
        & (wanted[:, None] == in_shell[None, :])
    ).astype(jnp.bfloat16)
    return pl.pallas_call(
        sort_kernel,
        grid=(orders // group,),
        in_specs=[
            pl.BlockSpec((rows, rows), lambda i: (0, 0)),
            pl.BlockSpec((rows, width), lambda i: (i, 0)),
        ],
        out_specs=pl.BlockSpec((degrees, group * shells, width), lambda i: (0, i, 0)),
        out_shape=jax.ShapeDtypeStruct((degrees, orders * shells, width), pair_coef.dtype),
        compiler_params=pltpu.CompilerParams(vmem_limit_bytes=24 * 2**20),
        cost_estimate=pl.CostEstimate(
            flops=2 * orders * shells * degrees * rows * width,
            bytes_accessed=4 * orders * shells * degrees * width,
            transcendentals=0,
        ),
    )(perm, pair_coef.reshape(orders * shells * degrees, width))


def scale_code(largest):
    return jnp.ceil(jnp.log2(jnp.maximum(largest, 1e-30)) * STEPS) + 1.0


def encode(real_part, imag_part):
    largest = jnp.max(jnp.maximum(jnp.abs(real_part), jnp.abs(imag_part)), axis=0, keepdims=True)
    code = scale_code(largest)
    gain = jnp.exp2(code * (-1.0 / STEPS)) * TOP
    coded = [
        jnp.floor(v * gain + 0.5).astype(jnp.int32).astype(jnp.int16) for v in (real_part, imag_part)
    ]
    return coded[0], coded[1], code


def gains(codes):
    return jnp.exp2(codes.astype(jnp.int32).astype(jnp.float32) * (1.0 / STEPS)) * (1.0 / TOP)


def widen(value):
    return value.astype(jnp.int32).astype(jnp.float32)


def project_kernel(offsets, n_acc, degree_ref, rows_ref, *refs):
    n = len(offsets)
    panels = refs[:n]
    acc_in = refs[n : n + n_acc]
    acc_out, lhs, rhs, sems = refs[n + n_acc :]
    width = rhs.shape[1]
    copies = []
    at = 0
    for i, (panel, offset) in enumerate(zip(panels, offsets)):
        depth = panel.shape[0]
        copies.append(pltpu.make_async_copy(panel, rhs.at[pl.ds(at, depth), :], sems.at[3 * i]))
        for c in range(2):
            copies.append(
                pltpu.make_async_copy(
                    rows_ref.at[degree_ref[i], :, pl.ds(c * width + offset, depth)],
                    lhs.at[c, :, pl.ds(at, depth)],
                    sems.at[3 * i + 1 + c],
                )
            )
        at += depth
    for copy in copies:
        copy.start()
    for copy in copies:
        copy.wait()
    for c in range(2):
        part = jnp.dot(lhs[c], rhs[...], preferred_element_type=jnp.float32)
        acc_out[c] = part + acc_in[0][c] if n_acc else part


def project(acc, rows, degrees, panels, offsets):
    count, width = rows.shape[1], panels[0].shape[1]
    depth = sum(p.shape[0] for p in panels)
    n_acc = 0 if acc is None else 1
    return pl.pallas_call(
        functools.partial(project_kernel, tuple(offsets), n_acc),
        in_specs=[pl.BlockSpec(memory_space=pltpu.SMEM)]
        + [pl.BlockSpec(memory_space=pl.ANY)] * (1 + len(panels))
        + [pl.BlockSpec(memory_space=pltpu.VMEM)] * n_acc,
        out_specs=pl.BlockSpec(memory_space=pltpu.VMEM),
        out_shape=jax.ShapeDtypeStruct((2, count, width), jnp.float32),
        scratch_shapes=[
            pltpu.VMEM((2, count, depth), rows.dtype),
            pltpu.VMEM((depth, width), rows.dtype),
            pltpu.SemaphoreType.DMA((3 * len(panels),)),
        ],
        compiler_params=pltpu.CompilerParams(vmem_limit_bytes=24 * 2**20),
        cost_estimate=pl.CostEstimate(
            flops=4 * count * depth * width,
            bytes_accessed=2 * depth * (width + 2 * count) + 8 * count * width * (1 + n_acc),
            transcendentals=0,
        ),
    )(degrees, rows, *panels, *([acc] if n_acc else []))


def pack_kernel(proj_ref, out_ref):
    width = proj_ref.shape[2]
    blocks = width // LANES
    line = lax.broadcasted_iota(jnp.int32, (16, LANES), 0)
    for d in range(out_ref.shape[0]):
        codes = jnp.zeros((16, LANES), jnp.float32)
        for jb in range(blocks):
            lanes = pl.ds(jb * LANES, LANES)
            real_part, imag_part, code = encode(
                proj_ref[0, pl.ds(16 * d, 16), lanes], proj_ref[1, pl.ds(16 * d, 16), lanes]
            )
            out_ref[d, pl.ds(32 * jb, 16), :] = real_part
            out_ref[d, pl.ds(32 * jb + 16, 16), :] = imag_part
            codes = jnp.where(line == jb, code, codes)
        out_ref[d, pl.ds(32 * blocks, 16), :] = codes.astype(jnp.int32).astype(jnp.int16)


def radix2(real_parts, imag_parts):
    n = len(real_parts)
    re, im = list(real_parts), list(imag_parts)
    half = n // 2
    while half:
        for start in range(0, n, 2 * half):
            for k in range(half):
                a, b = start + k, start + k + half
                dr, di = re[a] - re[b], im[a] - im[b]
                re[a], im[a] = re[a] + re[b], im[a] + im[b]
                angle = -math.pi * k / half
                if k == 0:
                    re[b], im[b] = dr, di
                elif 2 * k == half:
                    re[b], im[b] = di, -dr
                elif 4 * k == half:
                    re[b], im[b] = (dr + di) * math.cos(angle), (di - dr) * math.cos(angle)
                elif 4 * k == 3 * half:
                    re[b], im[b] = (di - dr) * math.cos(math.pi / 4), (dr + di) * -math.cos(math.pi / 4)
                else:
                    c, s = math.cos(angle), math.sin(angle)
                    re[b], im[b] = dr * c - di * s, dr * s + di * c
        half //= 2
    return re, im


def outer_kernel(in_ref, out_ref, gain_ref, code_ref):
    n = in_ref.shape[0]
    blocks = in_ref.shape[1] // 32
    for q in range(n):
        gain_ref[q] = gains(in_ref[q, pl.ds(32 * blocks, 16), :])
    code_ref[...] = jnp.zeros_like(code_ref)
    for jb in range(blocks):
        re, im = [], []
        for q in range(n):
            gain = gain_ref[q, pl.ds(jb, 1), :]
            re.append(widen(in_ref[q, pl.ds(32 * jb, 16), :]) * gain)
            im.append(widen(in_ref[q, pl.ds(32 * jb + 16, 16), :]) * gain)
        re, im = radix2(re, im)
        for p in range(n):
            real_part, imag_part, code = encode(re[p], im[p])
            out_ref[p, pl.ds(32 * jb, 16), :] = real_part
            out_ref[p, pl.ds(32 * jb + 16, 16), :] = imag_part
            code_ref[p, pl.ds(jb, 1), :] = code
    for p in range(n):
        out_ref[p, pl.ds(32 * blocks, 16), :] = code_ref[p].astype(jnp.int32).astype(jnp.int16)


def inner_kernel(twist_ref, in_ref, out_ref, gain_ref):
    n = in_ref.shape[0]
    blocks = in_ref.shape[1] // 32
    orders = 2 * n
    nbits = orders.bit_length() - 1
    for d in range(n):
        gain_ref[d] = gains(in_ref[d, pl.ds(32 * blocks, 16), :])
    for jb in range(blocks):
        re, im = [], []
        for d in range(n):
            gain = gain_ref[d, pl.ds(jb, 1), :]
            both_re = widen(in_ref[d, pl.ds(32 * jb, 16), :]) * gain
            both_im = widen(in_ref[d, pl.ds(32 * jb + 16, 16), :]) * gain
            for r in range(2):
                a, b = both_re[8 * r : 8 * r + 8], both_im[8 * r : 8 * r + 8]
                c, s = twist_ref[0, 2 * d + r], twist_ref[1, 2 * d + r]
                re.append(a * c - b * s)
                im.append(a * s + b * c)
        re, im = radix2(re, im)
        for p in range(orders):
            h = bit_reverse(p, nbits)
            for part, value in enumerate((re[p], im[p])):
                for b in range(2):
                    first = (b * orders + h) * 32 + 2 * jb + part
                    out_ref[pl.ds(first, 4, stride=8), :] = value[4 * b : 4 * b + 4]


def local_call(kernel, out, scratch, *args, smem=0):
    return pl.pallas_call(
        kernel,
        in_specs=[pl.BlockSpec(memory_space=pltpu.SMEM)] * smem
        + [pl.BlockSpec(memory_space=pltpu.VMEM)] * (len(args) - smem),
        out_specs=pl.BlockSpec(memory_space=pltpu.VMEM),
        out_shape=out,
        scratch_shapes=scratch,
        compiler_params=pltpu.CompilerParams(vmem_limit_bytes=24 * 2**20),
    )(*args)


def ring_of(chips, columns):
    lines = chips // columns
    walk = [columns * z for z in range(lines)]
    if columns == 2:
        walk += [columns * z + 1 for z in reversed(range(lines))]
    return walk


def shards(pair_coef, panel_pool, degree_owner, batch_order):
    local_orders, shells = pair_coef.shape[:2]
    width = panel_pool.shape[2]
    devices = lax.axis_size("shell")
    total_orders = local_orders * devices
    chips = devices // 2
    me = lax.axis_index("shell")
    walk = jnp.array(ring_of(chips, 2), jnp.int32)
    place = jnp.argsort(walk)[me // 2]
    degree_of = jnp.argsort(degree_owner)
    steps = [ring_of(chips, 2)[i % chips] for i in range(chips + 1)]

    def around(value, forward):
        pairs = []
        for here, there in zip(steps[:-1], steps[1:]):
            for core in range(2):
                pair = (2 * here + core, 2 * there + core)
                pairs.append(pair if forward else pair[::-1])
        return lax.ppermute(value, "shell", pairs)

    def sibling(value):
        return lax.ppermute(value, "shell", [(s, s ^ 1) for s in range(devices)])

    def degrees_at(*shifts):
        slots = []
        for shift in shifts:
            chip = walk[(place + shift) % chips]
            slots += [2 * chip + me % 2, 2 * chip + 1 - me % 2]
        return degree_of[jnp.stack(slots)]

    rows = sort_rows(pair_coef, batch_order)
    own = panel_pool[0]
    acc = project(None, rows, degrees_at(0), [own, sibling(own)], [0, 0])
    fwd = bwd = own
    for step in range(1, chips // 2):
        fwd, bwd = around(fwd, True), around(bwd, False)
        acc = project(
            acc,
            rows,
            degrees_at(-step, step),
            [fwd, sibling(fwd), bwd, sibling(bwd)],
            [0] * 4,
        )
    half = own.shape[0] // 2
    upper, lower = around(fwd[:half], True), around(bwd[half:], False)
    far = degrees_at(chips // 2)
    proj = project(
        acc,
        rows,
        jnp.concatenate([far, far]),
        [upper, sibling(upper), lower, sibling(lower)],
        [0, 0, half, half],
    )
    blocks = width // LANES
    parcel = jax.ShapeDtypeStruct((devices, 32 * blocks + 16, LANES), jnp.int16)
    lines = pltpu.VMEM((devices, 16, LANES), jnp.float32)
    sent = local_call(pack_kernel, parcel, [], proj)
    sent = lax.all_to_all(sent, "shell", 0, 0)
    sent = local_call(outer_kernel, parcel, [lines, lines], sent)
    sent = lax.all_to_all(sent, "shell", 0, 0)
    first = bit_reverse(me, devices.bit_length() - 1)
    phase = lax.iota(jnp.int32, local_orders) * first % total_orders
    angle = -2.0 * math.pi * phase.astype(jnp.float32) / float(total_orders)
    twist = jnp.stack([jnp.cos(angle), jnp.sin(angle)]) * (1.0 / math.sqrt(total_orders))
    out = jax.ShapeDtypeStruct((2 * local_orders * shells // 2 * 2 * blocks, LANES), jnp.float32)
    scores = local_call(inner_kernel, out, [lines], twist, sent, smem=1)
    scores = scores.reshape(2, local_orders, shells // 2, blocks, 2, LANES)
    return scores.transpose(0, 1, 2, 4, 3, 5).reshape(2, local_orders, shells // 2, 2, width)


def solution(mesh):
    devices = mesh.shape["shell"]
    return jax.shard_map(
        shards if devices == 16 else general,
        mesh=mesh,
        in_specs=(P(("grp", "shell"), None, None, None), P("shell", None, None), P(), P()),
        out_specs=P(None, ("grp", "shell"), None, None, None),
        check_vma=False,
    )
```

```python
import functools
import math

import jax
import jax.numpy as jnp
from jax import lax
from jax.experimental import pallas as pl
from jax.experimental.pallas import tpu as pltpu
from jax.sharding import PartitionSpec as P


def broadcast(value, axis, root):
    mine = lax.axis_index(axis) == root
    return lax.psum(jnp.where(mine, value, jnp.zeros_like(value)), axis)


def partner(value, axis, distance):
    mask = 2**distance
    pairs = [(source, source ^ mask) for source in range(lax.axis_size(axis))]
    return lax.ppermute(value, axis, pairs)


def rotate(real_part, imag_part, cosine, sine):
    return (real_part * cosine - imag_part * sine, real_part * sine + imag_part * cosine)


def general(pair_coef, panel_pool, degree_owner, batch_order):
    local_orders = pair_coef.shape[0]
    degrees = pair_coef.shape[2]
    width = pair_coef.shape[3] // 2
    batch_rows = batch_order.shape[0] // 2
    devices = lax.axis_size("shell")
    total_orders = local_orders * devices
    first = jnp.take(pair_coef, batch_order[:batch_rows], axis=1)
    second = jnp.take(pair_coef, batch_order[batch_rows:], axis=1)
    rows = jnp.stack([first, second])

    def add_degree(degree, total):
        panel = broadcast(panel_pool[0], "shell", degree_owner[degree])
        piece = lax.dynamic_index_in_dim(rows, degree, axis=3, keepdims=False).reshape(-1, width)
        return total + jnp.dot(piece, panel, preferred_element_type=jnp.float32)

    total = lax.fori_loop(
        0, degrees, add_degree, jnp.zeros((2 * local_orders * batch_rows * 2, width), jnp.float32)
    )
    proj = total.reshape(2, local_orders, batch_rows, 2, width)
    nbits = devices.bit_length() - 1
    high = lax.Precision.HIGHEST
    me = lax.axis_index("shell")
    blocks = proj
    for bit in reversed(range(nbits)):
        other = partner(blocks, "shell", bit)
        upper = me >> bit & 1 == 1
        lower_val = jnp.where(upper, other, blocks)
        upper_val = jnp.where(upper, blocks, other)
        summed = lower_val + upper_val
        differ = lower_val - upper_val
        twist = (me % (1 << bit)).astype(jnp.float32)
        angle = -2.0 * math.pi * twist / float(2 << bit)
        new_real, new_imag = rotate(
            differ[:, :, :, 0], differ[:, :, :, 1], jnp.cos(angle), jnp.sin(angle)
        )
        turned = jnp.stack([new_real, new_imag], axis=3)
        blocks = jnp.where(upper, turned, summed)
    flipped = jnp.zeros((), jnp.int32)
    for bit in range(nbits):
        flipped = flipped | (me >> bit & 1) << nbits - 1 - bit
    inner = lax.iota(jnp.int32, local_orders)
    freq = flipped + devices * inner
    phase = inner[None, :] * freq[:, None] % total_orders
    angle = -2.0 * math.pi * phase.astype(jnp.float32) / float(total_orders)
    cosine = jnp.cos(angle)
    sine = jnp.sin(angle)
    real_part = blocks[:, :, :, 0]
    imag_part = blocks[:, :, :, 1]
    out_real = jnp.einsum("gr,brtj->bgtj", cosine, real_part, precision=high) - jnp.einsum(
        "gr,brtj->bgtj", sine, imag_part, precision=high
    )
    out_imag = jnp.einsum("gr,brtj->bgtj", sine, real_part, precision=high) + jnp.einsum(
        "gr,brtj->bgtj", cosine, imag_part, precision=high
    )
    result = jnp.stack([out_real, out_imag], axis=3)
    return result * (1.0 / math.sqrt(total_orders))


STEPS = 16.0
TOP = 32000.0
LANES = 128


def bit_reverse(value, nbits):
    flipped = 0
    for bit in range(nbits):
        flipped = flipped | (value >> bit & 1) << nbits - 1 - bit
    return flipped


def sort_kernel(shells, order_ref, coef_ref, out_ref, perm_ref):
    @pl.when(pl.program_id(0) == 0)
    def _():
        degrees, group = out_ref.shape[0], out_ref.shape[1] // shells
        shape = perm_ref.shape
        out_at = lax.broadcasted_iota(jnp.int32, shape, 0)
        in_at = lax.broadcasted_iota(jnp.int32, shape, 1)
        out_t = out_at % shells
        wanted = jnp.zeros(shape, jnp.int32)
        for t in range(shells):
            wanted = jnp.where(out_t == t, order_ref[t], wanted)
        source = (out_at // shells % group * shells + wanted) * degrees + out_at // (group * shells)
        perm_ref[...] = jnp.where(in_at == source, 1.0, 0.0).astype(perm_ref.dtype)

    moved = jnp.dot(perm_ref[...], coef_ref[...], preferred_element_type=jnp.float32)
    out_ref[...] = moved.astype(out_ref.dtype).reshape(out_ref.shape)


def sort_rows(pair_coef, batch_order):
    orders, shells, degrees, width = pair_coef.shape
    group = 16 // shells
    rows = group * shells * degrees
    return pl.pallas_call(
        functools.partial(sort_kernel, shells),
        grid=(orders // group,),
        in_specs=[
            pl.BlockSpec(memory_space=pltpu.SMEM),
            pl.BlockSpec((rows, width), lambda i: (i, 0)),
        ],
        out_specs=pl.BlockSpec((degrees, group * shells, width), lambda i: (0, i, 0)),
        out_shape=jax.ShapeDtypeStruct((degrees, orders * shells, width), pair_coef.dtype),
        scratch_shapes=[pltpu.VMEM((rows, rows), pair_coef.dtype)],
        compiler_params=pltpu.CompilerParams(vmem_limit_bytes=24 * 2**20),
        cost_estimate=pl.CostEstimate(
            flops=2 * orders * shells * degrees * rows * width,
            bytes_accessed=4 * orders * shells * degrees * width,
            transcendentals=0,
        ),
    )(batch_order, pair_coef.reshape(orders * shells * degrees, width))


def scale_code(largest):
    return jnp.ceil(jnp.log2(jnp.maximum(largest, 1e-30)) * STEPS) + 1.0


def encode(real_part, imag_part):
    largest = jnp.max(jnp.maximum(jnp.abs(real_part), jnp.abs(imag_part)), axis=0, keepdims=True)
    code = scale_code(largest)
    gain = jnp.exp2(code * (-1.0 / STEPS)) * TOP
    coded = [
        jnp.floor(v * gain + 0.5).astype(jnp.int32).astype(jnp.int16) for v in (real_part, imag_part)
    ]
    return coded[0], coded[1], code


def gains(codes):
    return jnp.exp2(codes.astype(jnp.int32).astype(jnp.float32) * (1.0 / STEPS)) * (1.0 / TOP)


def widen(value):
    return value.astype(jnp.int32).astype(jnp.float32)


def walk_at(place, chips):
    lines = chips // 2
    return jnp.where(place < lines, 2 * place, 2 * (chips - 1 - place) + 1)


def place_of(chip, chips):
    return jnp.where(chip % 2 == 0, chip // 2, chips - 1 - chip // 2)


def project_kernel(devices, sources, n_acc, owner_ref, rows_ref, *refs):
    n = len(sources)
    panels = refs[:n]
    acc_in = refs[n : n + n_acc]
    acc_out, lhs, rhs, sems = refs[n + n_acc :]
    width = rhs.shape[1]
    chips = devices // 2
    me = lax.axis_index("shell")
    copies = []
    at = 0
    part = lax.axis_index("grp")
    for i, (panel, (shift, flip, half)) in enumerate(zip(panels, sources)):
        depth = panel.shape[0]
        ahead = jnp.where(me % 2 == 0, shift, -shift)
        place = lax.rem(place_of(me // 2, chips) + ahead + chips, chips)
        slot = 2 * walk_at(place, chips) + (me + flip) % 2
        offset = 0 if half is None else pl.multiple_of(depth * (part + half) % (2 * depth), 128)
        degree = jnp.zeros((), jnp.int32)
        for l in range(rows_ref.shape[0]):
            degree = jnp.where(owner_ref[l] == slot, l, degree)
        copies.append(pltpu.make_async_copy(panel, rhs.at[pl.ds(at, depth), :], sems.at[3 * i]))
        for c in range(2):
            copies.append(
                pltpu.make_async_copy(
                    rows_ref.at[degree, :, pl.ds(pl.multiple_of(c * width + offset, 128), depth)],
                    lhs.at[c, :, pl.ds(at, depth)],
                    sems.at[3 * i + 1 + c],
                )
            )
        at += depth
    for copy in copies:
        copy.start()
    for copy in copies:
        copy.wait()
    for c in range(2):
        part = jnp.dot(lhs[c], rhs[...], preferred_element_type=jnp.float32)
        acc_out[c] = part + acc_in[0][c] if n_acc else part


def project(acc, rows, owner, panels, sources):
    count, width = rows.shape[1], panels[0].shape[1]
    depth = sum(p.shape[0] for p in panels)
    n_acc = 0 if acc is None else 1
    return pl.pallas_call(
        functools.partial(project_kernel, lax.axis_size("shell"), tuple(sources), n_acc),
        in_specs=[pl.BlockSpec(memory_space=pltpu.SMEM)]
        + [pl.BlockSpec(memory_space=pl.ANY)] * (1 + len(panels))
        + [pl.BlockSpec(memory_space=pltpu.VMEM)] * n_acc,
        out_specs=pl.BlockSpec(memory_space=pltpu.VMEM),
        out_shape=jax.ShapeDtypeStruct((2, count, width), jnp.float32),
        scratch_shapes=[
            pltpu.VMEM((2, count, depth), rows.dtype),
            pltpu.VMEM((depth, width), rows.dtype),
            pltpu.SemaphoreType.DMA((3 * len(panels),)),
        ],
        compiler_params=pltpu.CompilerParams(vmem_limit_bytes=24 * 2**20),
        cost_estimate=pl.CostEstimate(
            flops=4 * count * depth * width,
            bytes_accessed=2 * depth * (width + 2 * count) + 8 * count * width * (1 + n_acc),
            transcendentals=0,
        ),
    )(owner, rows, *panels, *([acc] if n_acc else []))


def pack_kernel(proj_ref, out_ref):
    width = proj_ref.shape[2]
    blocks = width // LANES
    line = lax.broadcasted_iota(jnp.int32, (16, LANES), 0)
    for d in range(out_ref.shape[0]):
        codes = jnp.zeros((16, LANES), jnp.float32)
        for jb in range(blocks):
            lanes = pl.ds(jb * LANES, LANES)
            real_part, imag_part, code = encode(
                proj_ref[0, pl.ds(16 * d, 16), lanes], proj_ref[1, pl.ds(16 * d, 16), lanes]
            )
            out_ref[d, pl.ds(32 * jb, 16), :] = real_part
            out_ref[d, pl.ds(32 * jb + 16, 16), :] = imag_part
            codes = jnp.where(line == jb, code, codes)
        out_ref[d, pl.ds(32 * blocks, 16), :] = codes.astype(jnp.int32).astype(jnp.int16)


def radix2(real_parts, imag_parts):
    n = len(real_parts)
    re, im = list(real_parts), list(imag_parts)
    half = n // 2
    while half:
        for start in range(0, n, 2 * half):
            for k in range(half):
                a, b = start + k, start + k + half
                dr, di = re[a] - re[b], im[a] - im[b]
                re[a], im[a] = re[a] + re[b], im[a] + im[b]
                angle = -math.pi * k / half
                if k == 0:
                    re[b], im[b] = dr, di
                elif 2 * k == half:
                    re[b], im[b] = di, -dr
                elif 4 * k == half:
                    re[b], im[b] = (dr + di) * math.cos(angle), (di - dr) * math.cos(angle)
                elif 4 * k == 3 * half:
                    re[b], im[b] = (di - dr) * math.cos(math.pi / 4), (dr + di) * -math.cos(math.pi / 4)
                else:
                    c, s = math.cos(angle), math.sin(angle)
                    re[b], im[b] = dr * c - di * s, dr * s + di * c
        half //= 2
    return re, im


def outer_kernel(in_ref, out_ref, gain_ref, code_ref):
    n = in_ref.shape[0]
    blocks = in_ref.shape[1] // 32
    for q in range(n):
        gain_ref[q] = gains(in_ref[q, pl.ds(32 * blocks, 16), :])
    code_ref[...] = jnp.zeros_like(code_ref)
    for jb in range(blocks):
        re, im = [], []
        for q in range(n):
            gain = gain_ref[q, pl.ds(jb, 1), :]
            re.append(widen(in_ref[q, pl.ds(32 * jb, 16), :]) * gain)
            im.append(widen(in_ref[q, pl.ds(32 * jb + 16, 16), :]) * gain)
        re, im = radix2(re, im)
        for p in range(n):
            real_part, imag_part, code = encode(re[p], im[p])
            out_ref[p, pl.ds(32 * jb, 16), :] = real_part
            out_ref[p, pl.ds(32 * jb + 16, 16), :] = imag_part
            code_ref[p, pl.ds(jb, 1), :] = code
    for p in range(n):
        out_ref[p, pl.ds(32 * blocks, 16), :] = code_ref[p].astype(jnp.int32).astype(jnp.int16)


def inner_kernel(twist_ref, in_ref, out_ref, gain_ref):
    n = in_ref.shape[0]
    blocks = in_ref.shape[1] // 32
    orders = 2 * n
    nbits = orders.bit_length() - 1
    for d in range(n):
        gain_ref[d] = gains(in_ref[d, pl.ds(32 * blocks, 16), :])
    for jb in range(blocks):
        re, im = [], []
        for d in range(n):
            gain = gain_ref[d, pl.ds(jb, 1), :]
            both_re = widen(in_ref[d, pl.ds(32 * jb, 16), :]) * gain
            both_im = widen(in_ref[d, pl.ds(32 * jb + 16, 16), :]) * gain
            for r in range(2):
                a, b = both_re[8 * r : 8 * r + 8], both_im[8 * r : 8 * r + 8]
                c, s = twist_ref[0, 2 * d + r], twist_ref[1, 2 * d + r]
                re.append(a * c - b * s)
                im.append(a * s + b * c)
        re, im = radix2(re, im)
        for p in range(orders):
            h = bit_reverse(p, nbits)
            for part, value in enumerate((re[p], im[p])):
                for b in range(2):
                    first = (b * orders + h) * 32 + 2 * jb + part
                    out_ref[pl.ds(first, 4, stride=8), :] = value[4 * b : 4 * b + 4]


def local_call(kernel, out, scratch, *args, smem=0):
    return pl.pallas_call(
        kernel,
        in_specs=[pl.BlockSpec(memory_space=pltpu.SMEM)] * smem
        + [pl.BlockSpec(memory_space=pltpu.VMEM)] * (len(args) - smem),
        out_specs=pl.BlockSpec(memory_space=pltpu.VMEM),
        out_shape=out,
        scratch_shapes=scratch,
        compiler_params=pltpu.CompilerParams(vmem_limit_bytes=24 * 2**20),
    )(*args)


def shards(pair_coef, panel_pool, degree_owner, batch_order):
    local_orders, shells = pair_coef.shape[:2]
    width = panel_pool.shape[2]
    devices = lax.axis_size("shell")
    total_orders = local_orders * devices
    chips = devices // 2
    me = lax.axis_index("shell")
    lines = chips // 2
    walk = [2 * z for z in range(lines)] + [2 * z + 1 for z in reversed(range(lines))]

    def around(value):
        pairs = []
        for here, there in zip(walk, walk[1:] + walk[:1]):
            pairs += [(2 * here, 2 * there), (2 * there + 1, 2 * here + 1)]
        return lax.ppermute(value, "shell", pairs)

    def sibling(value):
        return lax.ppermute(value, "shell", [(s, s ^ 1) for s in range(devices)])

    def across(value):
        return lax.ppermute(value, "grp", [(0, 1), (1, 0)])

    own = panel_pool[0]
    half = own.shape[0] // 2
    other = sibling(own)
    whole = around(own)
    part = around(lax.dynamic_slice_in_dim(other, half * lax.axis_index("grp"), half))
    rows = sort_rows(pair_coef, batch_order)
    acc = project(None, rows, degree_owner, [own, other], [(0, 0, None), (0, 1, None)])
    late, late_from = [], []
    for step in range(1, chips // 2):
        whole, acc = lax.optimization_barrier((whole, acc))
        next_whole = around(whole)
        next_part = around(part) if step + 1 < chips // 2 else None
        rest = across(part)
        acc = project(
            acc,
            rows,
            degree_owner,
            [whole, sibling(whole), part, sibling(part), *late],
            [(-step, 0, None), (step, 1, None), (-step, 1, 0), (step, 0, 0), *late_from],
        )
        late, late_from = [rest, sibling(rest)], [(-step, 1, 1), (step, 0, 1)]
        whole, part = next_whole, next_part
    whole, acc = lax.optimization_barrier((whole, acc))
    proj = project(
        acc,
        rows,
        degree_owner,
        [whole, sibling(whole), *late],
        [(-(chips // 2), 0, None), (chips // 2, 1, None), *late_from],
    )
    blocks = width // LANES
    parcel = jax.ShapeDtypeStruct((devices, 32 * blocks + 16, LANES), jnp.int16)
    lines = pltpu.VMEM((devices, 16, LANES), jnp.float32)
    sent = local_call(pack_kernel, parcel, [], proj)
    sent = lax.all_to_all(sent, "shell", 0, 0)
    sent = local_call(outer_kernel, parcel, [lines, lines], sent)
    sent = lax.all_to_all(sent, "shell", 0, 0)
    first = bit_reverse(me, devices.bit_length() - 1)
    phase = lax.iota(jnp.int32, local_orders) * first % total_orders
    angle = -2.0 * math.pi * phase.astype(jnp.float32) / float(total_orders)
    twist = jnp.stack([jnp.cos(angle), jnp.sin(angle)]) * (1.0 / math.sqrt(total_orders))
    out = jax.ShapeDtypeStruct((2 * local_orders * shells // 2 * 2 * blocks, LANES), jnp.float32)
    scores = local_call(inner_kernel, out, [lines], twist, sent, smem=1)
    scores = scores.reshape(2, local_orders, shells // 2, blocks, 2, LANES)
    return scores.transpose(0, 1, 2, 4, 3, 5).reshape(2, local_orders, shells // 2, 2, width)


def solution(mesh):
    devices = mesh.shape["shell"]
    return jax.shard_map(
        shards if (devices, mesh.shape["grp"]) == (16, 2) else general,
        mesh=mesh,
        in_specs=(P(("grp", "shell"), None, None, None), P("shell", None, None), P(), P()),
        out_specs=P(None, ("grp", "shell"), None, None, None),
        check_vma=False,
    )
```

```python
import functools
import math

import jax
import jax.numpy as jnp
from jax import lax
from jax.experimental import pallas as pl
from jax.experimental.pallas import tpu as pltpu
from jax.sharding import PartitionSpec as P


def broadcast(value, axis, root):
    mine = lax.axis_index(axis) == root
    return lax.psum(jnp.where(mine, value, jnp.zeros_like(value)), axis)


def partner(value, axis, distance):
    mask = 2**distance
    pairs = [(source, source ^ mask) for source in range(lax.axis_size(axis))]
    return lax.ppermute(value, axis, pairs)


def rotate(real_part, imag_part, cosine, sine):
    return (real_part * cosine - imag_part * sine, real_part * sine + imag_part * cosine)


def general(pair_coef, panel_pool, degree_owner, batch_order):
    local_orders = pair_coef.shape[0]
    degrees = pair_coef.shape[2]
    width = pair_coef.shape[3] // 2
    batch_rows = batch_order.shape[0] // 2
    devices = lax.axis_size("shell")
    total_orders = local_orders * devices
    first = jnp.take(pair_coef, batch_order[:batch_rows], axis=1)
    second = jnp.take(pair_coef, batch_order[batch_rows:], axis=1)
    rows = jnp.stack([first, second])

    def add_degree(degree, total):
        panel = broadcast(panel_pool[0], "shell", degree_owner[degree])
        piece = lax.dynamic_index_in_dim(rows, degree, axis=3, keepdims=False).reshape(-1, width)
        return total + jnp.dot(piece, panel, preferred_element_type=jnp.float32)

    total = lax.fori_loop(
        0, degrees, add_degree, jnp.zeros((2 * local_orders * batch_rows * 2, width), jnp.float32)
    )
    proj = total.reshape(2, local_orders, batch_rows, 2, width)
    nbits = devices.bit_length() - 1
    high = lax.Precision.HIGHEST
    me = lax.axis_index("shell")
    blocks = proj
    for bit in reversed(range(nbits)):
        other = partner(blocks, "shell", bit)
        upper = me >> bit & 1 == 1
        lower_val = jnp.where(upper, other, blocks)
        upper_val = jnp.where(upper, blocks, other)
        summed = lower_val + upper_val
        differ = lower_val - upper_val
        twist = (me % (1 << bit)).astype(jnp.float32)
        angle = -2.0 * math.pi * twist / float(2 << bit)
        new_real, new_imag = rotate(
            differ[:, :, :, 0], differ[:, :, :, 1], jnp.cos(angle), jnp.sin(angle)
        )
        turned = jnp.stack([new_real, new_imag], axis=3)
        blocks = jnp.where(upper, turned, summed)
    flipped = jnp.zeros((), jnp.int32)
    for bit in range(nbits):
        flipped = flipped | (me >> bit & 1) << nbits - 1 - bit
    inner = lax.iota(jnp.int32, local_orders)
    freq = flipped + devices * inner
    phase = inner[None, :] * freq[:, None] % total_orders
    angle = -2.0 * math.pi * phase.astype(jnp.float32) / float(total_orders)
    cosine = jnp.cos(angle)
    sine = jnp.sin(angle)
    real_part = blocks[:, :, :, 0]
    imag_part = blocks[:, :, :, 1]
    out_real = jnp.einsum("gr,brtj->bgtj", cosine, real_part, precision=high) - jnp.einsum(
        "gr,brtj->bgtj", sine, imag_part, precision=high
    )
    out_imag = jnp.einsum("gr,brtj->bgtj", sine, real_part, precision=high) + jnp.einsum(
        "gr,brtj->bgtj", cosine, imag_part, precision=high
    )
    result = jnp.stack([out_real, out_imag], axis=3)
    return result * (1.0 / math.sqrt(total_orders))


STEPS = 16.0
TOP = 32000.0
LANES = 128
SORT_LIMIT = 42


def bit_reverse(value, nbits):
    flipped = 0
    for bit in range(nbits):
        flipped = flipped | (value >> bit & 1) << nbits - 1 - bit
    return flipped


def sort_kernel(order_ref, coef_ref, out_ref, perm_ref, held_ref, sems):
    blocks, rows, _ = held_ref.shape
    degrees = out_ref.shape[0]
    shells = order_ref.shape[0]
    slab = rows // degrees

    def copy(i):
        block = coef_ref.at[pl.ds(i * rows, rows), :]
        return pltpu.make_async_copy(block, held_ref.at[i], sems.at[i])

    for i in range(blocks):
        copy(i).start()
    line = lax.broadcasted_iota(jnp.int32, (slab, rows), 0)
    in_at = lax.broadcasted_iota(jnp.int32, (slab, rows), 1)
    wanted = jnp.zeros(line.shape, jnp.int32)
    for at in range(slab):
        source = (at // shells * shells + order_ref[at % shells]) * degrees
        wanted = jnp.where(line == at, source, wanted)
    for l in range(degrees):
        chosen = jnp.where(in_at == wanted + l, 1.0, 0.0).astype(perm_ref.dtype)
        perm_ref[pl.ds(l * slab, slab), :] = chosen

    for i in range(blocks):
        copy(i).wait()
        moved = jnp.dot(perm_ref[...], held_ref[i], preferred_element_type=jnp.float32)
        out_ref[:, pl.ds(i * slab, slab), :] = moved.astype(out_ref.dtype).reshape(
            degrees, slab, moved.shape[1]
        )


def sort_rows(pair_coef, batch_order):
    orders, shells, degrees, width = pair_coef.shape
    group = 16 // shells
    rows = group * shells * degrees
    blocks = orders // group
    return pl.pallas_call(
        sort_kernel,
        in_specs=[pl.BlockSpec(memory_space=pltpu.SMEM), pl.BlockSpec(memory_space=pltpu.HBM)],
        out_specs=pl.BlockSpec(memory_space=pltpu.VMEM),
        out_shape=jax.ShapeDtypeStruct((degrees, orders * shells, width), pair_coef.dtype),
        scratch_shapes=[
            pltpu.VMEM((rows, rows), pair_coef.dtype),
            pltpu.VMEM((blocks, rows, width), pair_coef.dtype),
            pltpu.SemaphoreType.DMA((blocks,)),
        ],
        compiler_params=pltpu.CompilerParams(vmem_limit_bytes=SORT_LIMIT * 2**20),
        cost_estimate=pl.CostEstimate(
            flops=2 * blocks * rows * rows * width,
            bytes_accessed=4 * blocks * rows * width,
            transcendentals=0,
        ),
    )(batch_order, pair_coef.reshape(orders * shells * degrees, width))


def scale_code(largest):
    return jnp.ceil(jnp.log2(jnp.maximum(largest, 1e-30)) * STEPS) + 1.0


def encode(real_part, imag_part):
    largest = jnp.max(jnp.maximum(jnp.abs(real_part), jnp.abs(imag_part)), axis=0, keepdims=True)
    code = scale_code(largest)
    gain = jnp.exp2(code * (-1.0 / STEPS)) * TOP
    coded = [
        jnp.floor(v * gain + 0.5).astype(jnp.int32).astype(jnp.int16) for v in (real_part, imag_part)
    ]
    return coded[0], coded[1], code


def gains(codes):
    return jnp.exp2(codes.astype(jnp.int32).astype(jnp.float32) * (1.0 / STEPS)) * (1.0 / TOP)


def widen(value):
    return value.astype(jnp.int32).astype(jnp.float32)


def walk_at(place, chips):
    lines = chips // 2
    return jnp.where(place < lines, 2 * place, 2 * (chips - 1 - place) + 1)


def place_of(chip, chips):
    return jnp.where(chip % 2 == 0, chip // 2, chips - 1 - chip // 2)


def project_kernel(devices, sources, n_acc, packed, owner_ref, rows_ref, *refs):
    n = len(sources)
    panels = refs[:n]
    acc_in = refs[n : n + n_acc]
    acc_out = refs[-1]
    chips = devices // 2
    me = lax.axis_index("shell")
    part = lax.axis_index("grp")
    width = rows_ref.shape[2] // 2
    started = n_acc
    if n_acc:
        acc_out[...] = acc_in[0][...]
    for panel, (shift, flip, half) in zip(panels, sources):
        depth = panel.shape[0]
        ahead = jnp.where(me % 2 == 0, shift, -shift)
        place = lax.rem(place_of(me // 2, chips) + ahead + chips, chips)
        slot = 2 * walk_at(place, chips) + (me + flip) % 2
        degree = jnp.zeros((), jnp.int32)
        for l in range(rows_ref.shape[0]):
            degree = jnp.where(owner_ref[l] == slot, l, degree)
        offset = 0 if half is None else depth * (part + half) % (2 * depth)
        left = jnp.concatenate(
            [rows_ref[degree, :, pl.ds(pl.multiple_of(c * width + offset, 128), depth)] for c in range(2)]
        )
        product = jnp.dot(left, panel[...], preferred_element_type=jnp.float32)
        acc_out[...] = acc_out[...] + product if started else product
        started = 1
    if packed:
        pack(acc_out, refs[-2])


def project(acc, rows, owner, panels, sources, packed=None):
    count, width = rows.shape[1], panels[0].shape[1]
    depth = sum(p.shape[0] for p in panels)
    n_acc = 0 if acc is None else 1
    total = jax.ShapeDtypeStruct((2 * count, width), jnp.float32)
    return pl.pallas_call(
        functools.partial(
            project_kernel, lax.axis_size("shell"), tuple(sources), n_acc, packed is not None
        ),
        in_specs=[pl.BlockSpec(memory_space=pltpu.SMEM)]
        + [pl.BlockSpec(memory_space=pltpu.VMEM)] * (1 + len(panels) + n_acc),
        out_specs=pl.BlockSpec(memory_space=pltpu.VMEM),
        out_shape=total if packed is None else packed,
        scratch_shapes=[] if packed is None else [pltpu.VMEM(total.shape, total.dtype)],
        compiler_params=pltpu.CompilerParams(vmem_limit_bytes=24 * 2**20),
        cost_estimate=pl.CostEstimate(
            flops=4 * count * depth * width,
            bytes_accessed=2 * depth * (width + 2 * count) + 8 * count * width * (1 + n_acc),
            transcendentals=0,
        ),
    )(owner, rows, *panels, *([acc] if n_acc else []))


def pack(proj_ref, out_ref):
    count, width = proj_ref.shape[0] // 2, proj_ref.shape[1]
    blocks = width // LANES
    line = lax.broadcasted_iota(jnp.int32, (16, LANES), 0)
    for d in range(out_ref.shape[0]):
        codes = jnp.zeros((16, LANES), jnp.float32)
        for jb in range(blocks):
            lanes = pl.ds(jb * LANES, LANES)
            real_part, imag_part, code = encode(
                proj_ref[pl.ds(16 * d, 16), lanes], proj_ref[pl.ds(count + 16 * d, 16), lanes]
            )
            out_ref[d, pl.ds(32 * jb, 16), :] = real_part
            out_ref[d, pl.ds(32 * jb + 16, 16), :] = imag_part
            codes = jnp.where(line == jb, code, codes)
        out_ref[d, pl.ds(32 * blocks, 16), :] = codes.astype(jnp.int32).astype(jnp.int16)


def radix2(real_parts, imag_parts):
    n = len(real_parts)
    re, im = list(real_parts), list(imag_parts)
    half = n // 2
    while half:
        for start in range(0, n, 2 * half):
            for k in range(half):
                a, b = start + k, start + k + half
                dr, di = re[a] - re[b], im[a] - im[b]
                re[a], im[a] = re[a] + re[b], im[a] + im[b]
                angle = -math.pi * k / half
                if k == 0:
                    re[b], im[b] = dr, di
                elif 2 * k == half:
                    re[b], im[b] = di, -dr
                elif 4 * k == half:
                    re[b], im[b] = (dr + di) * math.cos(angle), (di - dr) * math.cos(angle)
                elif 4 * k == 3 * half:
                    re[b], im[b] = (di - dr) * math.cos(math.pi / 4), (dr + di) * -math.cos(math.pi / 4)
                else:
                    c, s = math.cos(angle), math.sin(angle)
                    re[b], im[b] = dr * c - di * s, dr * s + di * c
        half //= 2
    return re, im


def outer_kernel(in_ref, out_ref, gain_ref, code_ref):
    n = in_ref.shape[0]
    blocks = in_ref.shape[1] // 32
    for q in range(n):
        gain_ref[q] = gains(in_ref[q, pl.ds(32 * blocks, 16), :])
    code_ref[...] = jnp.zeros_like(code_ref)
    for jb in range(blocks):
        re, im = [], []
        for q in range(n):
            gain = gain_ref[q, pl.ds(jb, 1), :]
            re.append(widen(in_ref[q, pl.ds(32 * jb, 16), :]) * gain)
            im.append(widen(in_ref[q, pl.ds(32 * jb + 16, 16), :]) * gain)
        re, im = radix2(re, im)
        for p in range(n):
            real_part, imag_part, code = encode(re[p], im[p])
            out_ref[p, pl.ds(32 * jb, 16), :] = real_part
            out_ref[p, pl.ds(32 * jb + 16, 16), :] = imag_part
            code_ref[p, pl.ds(jb, 1), :] = code
    for p in range(n):
        out_ref[p, pl.ds(32 * blocks, 16), :] = code_ref[p].astype(jnp.int32).astype(jnp.int16)


def inner_kernel(twist_ref, in_ref, out_ref, gain_ref):
    n = in_ref.shape[0]
    blocks = in_ref.shape[1] // 32
    orders = 2 * n
    nbits = orders.bit_length() - 1
    for d in range(n):
        gain_ref[d] = gains(in_ref[d, pl.ds(32 * blocks, 16), :])
    for jb in range(blocks):
        re, im = [], []
        for d in range(n):
            gain = gain_ref[d, pl.ds(jb, 1), :]
            both_re = widen(in_ref[d, pl.ds(32 * jb, 16), :]) * gain
            both_im = widen(in_ref[d, pl.ds(32 * jb + 16, 16), :]) * gain
            for r in range(2):
                a, b = both_re[8 * r : 8 * r + 8], both_im[8 * r : 8 * r + 8]
                c, s = twist_ref[0, 2 * d + r], twist_ref[1, 2 * d + r]
                re.append(a * c - b * s)
                im.append(a * s + b * c)
        re, im = radix2(re, im)
        for p in range(orders):
            h = bit_reverse(p, nbits)
            for part, value in enumerate((re[p], im[p])):
                for b in range(2):
                    first = (b * orders + h) * 32 + 2 * jb + part
                    out_ref[pl.ds(first, 4, stride=8), :] = value[4 * b : 4 * b + 4]


def local_call(kernel, out, scratch, *args, smem=0):
    return pl.pallas_call(
        kernel,
        in_specs=[pl.BlockSpec(memory_space=pltpu.SMEM)] * smem
        + [pl.BlockSpec(memory_space=pltpu.VMEM)] * (len(args) - smem),
        out_specs=pl.BlockSpec(memory_space=pltpu.VMEM),
        out_shape=out,
        scratch_shapes=scratch,
        compiler_params=pltpu.CompilerParams(vmem_limit_bytes=24 * 2**20),
    )(*args)


def shards(pair_coef, panel_pool, degree_owner, batch_order):
    local_orders, shells = pair_coef.shape[:2]
    width = panel_pool.shape[2]
    devices = lax.axis_size("shell")
    total_orders = local_orders * devices
    chips = devices // 2
    me = lax.axis_index("shell")
    lines = chips // 2
    walk = [2 * z for z in range(lines)] + [2 * z + 1 for z in reversed(range(lines))]

    onward = []
    for here, there in zip(walk, walk[1:] + walk[:1]):
        onward += [(2 * here, 2 * there), (2 * there + 1, 2 * here + 1)]

    def around(value):
        return lax.ppermute(value, "shell", onward)

    def crosswise(value):
        return lax.ppermute(value, "shell", [(source ^ 1, target) for source, target in onward])

    def sibling(value):
        return lax.ppermute(value, "shell", [(s, s ^ 1) for s in range(devices)])

    def across(value):
        return lax.ppermute(value, "grp", [(0, 1), (1, 0)])

    blocks = width // LANES
    parcel = jax.ShapeDtypeStruct((devices, 32 * blocks + 16, LANES), jnp.int16)
    lines = pltpu.VMEM((devices, 16, LANES), jnp.float32)
    own = panel_pool[0]
    half = own.shape[0] // 2
    whole = around(own)
    part = crosswise(lax.dynamic_slice_in_dim(own, half * lax.axis_index("grp"), half))
    other = sibling(own)
    rows = sort_rows(pair_coef, batch_order)
    acc = project(None, rows, degree_owner, [own, other], [(0, 0, None), (0, 1, None)])
    whole, part, rows = lax.optimization_barrier((whole, part, rows))
    late, late_from = [], []
    for step in range(1, chips // 2):
        if step > 1:
            whole, acc = lax.optimization_barrier((whole, acc))
        next_whole = around(whole)
        next_part = around(part) if step + 1 < chips // 2 else None
        rest = across(part)
        acc = project(
            acc,
            rows,
            degree_owner,
            [whole, sibling(whole), part, sibling(part), *late],
            [(-step, 0, None), (step, 1, None), (-step, 1, 0), (step, 0, 0), *late_from],
        )
        late, late_from = [rest, sibling(rest)], [(-step, 1, 1), (step, 0, 1)]
        whole, part = next_whole, next_part
    whole, acc = lax.optimization_barrier((whole, acc))
    sent = project(
        acc,
        rows,
        degree_owner,
        [whole, sibling(whole), *late],
        [(-(chips // 2), 0, None), (chips // 2, 1, None), *late_from],
        packed=parcel,
    )
    sent = lax.all_to_all(sent, "shell", 0, 0)
    sent = local_call(outer_kernel, parcel, [lines, lines], sent)
    sent = lax.all_to_all(sent, "shell", 0, 0)
    first = bit_reverse(me, devices.bit_length() - 1)
    phase = lax.iota(jnp.int32, local_orders) * first % total_orders
    angle = -2.0 * math.pi * phase.astype(jnp.float32) / float(total_orders)
    twist = jnp.stack([jnp.cos(angle), jnp.sin(angle)]) * (1.0 / math.sqrt(total_orders))
    out = jax.ShapeDtypeStruct((2 * local_orders * shells // 2 * 2 * blocks, LANES), jnp.float32)
    scores = local_call(inner_kernel, out, [lines], twist, sent, smem=1)
    scores = scores.reshape(2, local_orders, shells // 2, blocks, 2, LANES)
    return scores.transpose(0, 1, 2, 4, 3, 5).reshape(2, local_orders, shells // 2, 2, width)


def solution(mesh):
    devices = mesh.shape["shell"]
    return jax.shard_map(
        shards if (devices, mesh.shape["grp"]) == (16, 2) else general,
        mesh=mesh,
        in_specs=(P(("grp", "shell"), None, None, None), P("shell", None, None), P(), P()),
        out_specs=P(None, ("grp", "shell"), None, None, None),
        check_vma=False,
    )
```

```python
import functools
import math

import jax
import jax.numpy as jnp
from jax import lax
from jax.experimental import pallas as pl
from jax.experimental.pallas import tpu as pltpu
from jax.sharding import PartitionSpec as P


def broadcast(value, axis, root):
    mine = lax.axis_index(axis) == root
    return lax.psum(jnp.where(mine, value, jnp.zeros_like(value)), axis)


def partner(value, axis, distance):
    mask = 2**distance
    pairs = [(source, source ^ mask) for source in range(lax.axis_size(axis))]
    return lax.ppermute(value, axis, pairs)


def rotate(real_part, imag_part, cosine, sine):
    return (real_part * cosine - imag_part * sine, real_part * sine + imag_part * cosine)


def general(pair_coef, panel_pool, degree_owner, batch_order):
    local_orders = pair_coef.shape[0]
    degrees = pair_coef.shape[2]
    width = pair_coef.shape[3] // 2
    batch_rows = batch_order.shape[0] // 2
    devices = lax.axis_size("shell")
    total_orders = local_orders * devices
    first = jnp.take(pair_coef, batch_order[:batch_rows], axis=1)
    second = jnp.take(pair_coef, batch_order[batch_rows:], axis=1)
    rows = jnp.stack([first, second])

    def add_degree(degree, total):
        panel = broadcast(panel_pool[0], "shell", degree_owner[degree])
        piece = lax.dynamic_index_in_dim(rows, degree, axis=3, keepdims=False).reshape(-1, width)
        return total + jnp.dot(piece, panel, preferred_element_type=jnp.float32)

    total = lax.fori_loop(
        0, degrees, add_degree, jnp.zeros((2 * local_orders * batch_rows * 2, width), jnp.float32)
    )
    proj = total.reshape(2, local_orders, batch_rows, 2, width)
    nbits = devices.bit_length() - 1
    high = lax.Precision.HIGHEST
    me = lax.axis_index("shell")
    blocks = proj
    for bit in reversed(range(nbits)):
        other = partner(blocks, "shell", bit)
        upper = me >> bit & 1 == 1
        lower_val = jnp.where(upper, other, blocks)
        upper_val = jnp.where(upper, blocks, other)
        summed = lower_val + upper_val
        differ = lower_val - upper_val
        twist = (me % (1 << bit)).astype(jnp.float32)
        angle = -2.0 * math.pi * twist / float(2 << bit)
        new_real, new_imag = rotate(
            differ[:, :, :, 0], differ[:, :, :, 1], jnp.cos(angle), jnp.sin(angle)
        )
        turned = jnp.stack([new_real, new_imag], axis=3)
        blocks = jnp.where(upper, turned, summed)
    flipped = jnp.zeros((), jnp.int32)
    for bit in range(nbits):
        flipped = flipped | (me >> bit & 1) << nbits - 1 - bit
    inner = lax.iota(jnp.int32, local_orders)
    freq = flipped + devices * inner
    phase = inner[None, :] * freq[:, None] % total_orders
    angle = -2.0 * math.pi * phase.astype(jnp.float32) / float(total_orders)
    cosine = jnp.cos(angle)
    sine = jnp.sin(angle)
    real_part = blocks[:, :, :, 0]
    imag_part = blocks[:, :, :, 1]
    out_real = jnp.einsum("gr,brtj->bgtj", cosine, real_part, precision=high) - jnp.einsum(
        "gr,brtj->bgtj", sine, imag_part, precision=high
    )
    out_imag = jnp.einsum("gr,brtj->bgtj", sine, real_part, precision=high) + jnp.einsum(
        "gr,brtj->bgtj", cosine, imag_part, precision=high
    )
    result = jnp.stack([out_real, out_imag], axis=3)
    return result * (1.0 / math.sqrt(total_orders))


STEPS = 16.0
TOP = 32000.0
LANES = 128
GROUP = 4
SORT_LIMIT = 42


def bit_reverse(value, nbits):
    flipped = 0
    for bit in range(nbits):
        flipped = flipped | (value >> bit & 1) << nbits - 1 - bit
    return flipped


def sort_kernel(order_ref, coef_ref, out_ref, perm_ref, held_ref, sems):
    rows = perm_ref.shape[0]
    blocks = held_ref.shape[0] // rows
    degrees = out_ref.shape[0]
    shells = order_ref.shape[0]
    slab = rows // degrees

    def copy(i):
        block = coef_ref.at[pl.ds(i * rows, GROUP * rows), :]
        return pltpu.make_async_copy(block, held_ref.at[pl.ds(i * rows, GROUP * rows), :], sems.at[i])

    for i in range(0, blocks, GROUP):
        copy(i).start()
    line = lax.broadcasted_iota(jnp.int32, (slab, rows), 0)
    in_at = lax.broadcasted_iota(jnp.int32, (slab, rows), 1)
    wanted = jnp.zeros(line.shape, jnp.int32)
    for at in range(slab):
        source = (at // shells * shells + order_ref[at % shells]) * degrees
        wanted = jnp.where(line == at, source, wanted)
    for l in range(degrees):
        chosen = jnp.where(in_at == wanted + l, 1.0, 0.0).astype(perm_ref.dtype)
        perm_ref[pl.ds(l * slab, slab), :] = chosen

    for i in range(blocks):
        if i % GROUP == 0:
            copy(i).wait()
        moved = jnp.dot(perm_ref[...], held_ref[pl.ds(i * rows, rows), :], preferred_element_type=jnp.float32)
        out_ref[:, pl.ds(i * slab, slab), :] = moved.astype(out_ref.dtype).reshape(
            degrees, slab, moved.shape[1]
        )


def sort_rows(pair_coef, batch_order):
    orders, shells, degrees, width = pair_coef.shape
    group = 16 // shells
    rows = group * shells * degrees
    blocks = orders // group
    return pl.pallas_call(
        sort_kernel,
        in_specs=[pl.BlockSpec(memory_space=pltpu.SMEM), pl.BlockSpec(memory_space=pltpu.HBM)],
        out_specs=pl.BlockSpec(memory_space=pltpu.VMEM),
        out_shape=jax.ShapeDtypeStruct((degrees, orders * shells, width), pair_coef.dtype),
        scratch_shapes=[
            pltpu.VMEM((rows, rows), pair_coef.dtype),
            pltpu.VMEM((blocks * rows, width), pair_coef.dtype),
            pltpu.SemaphoreType.DMA((blocks,)),
        ],
        compiler_params=pltpu.CompilerParams(vmem_limit_bytes=SORT_LIMIT * 2**20),
        cost_estimate=pl.CostEstimate(
            flops=2 * blocks * rows * rows * width,
            bytes_accessed=4 * blocks * rows * width,
            transcendentals=0,
        ),
    )(batch_order, pair_coef.reshape(orders * shells * degrees, width))


def scale_code(largest):
    return jnp.ceil(jnp.log2(jnp.maximum(largest, 1e-30)) * STEPS) + 1.0


def encode(real_part, imag_part):
    largest = jnp.max(jnp.maximum(jnp.abs(real_part), jnp.abs(imag_part)), axis=0, keepdims=True)
    code = scale_code(largest)
    gain = jnp.exp2(code * (-1.0 / STEPS)) * TOP
    coded = [jnp.floor(v * gain + 0.5).astype(jnp.int32) for v in (real_part, imag_part)]
    return coded[0], coded[1], code


EIGHTS = 17


def stage_block(stage_ref, piece, jb, coded, code):
    odd = lax.axis_index("shell") % 2
    first = EIGHTS * piece + odd + 4 * jb
    for part in range(2):
        stage_ref[pl.ds(first + 2 * part, 2)] = coded[part].reshape(2, 8, LANES)
    stage_ref[EIGHTS * piece + (EIGHTS - 1) * (1 - odd), pl.ds(jb, 1), :] = code.astype(jnp.int32)


def clear_codes(stage_ref, pieces):
    odd = lax.axis_index("shell") % 2
    for piece in range(pieces):
        stage_ref[EIGHTS * piece + (EIGHTS - 1) * (1 - odd)] = jnp.zeros((8, LANES), jnp.int32)


def ship(stage_ref, out_ref):
    for pair in range(stage_ref.shape[0] // 2):
        both = stage_ref[pl.ds(2 * pair, 2)].reshape(16, LANES)
        out_ref[pl.ds(16 * pair, 16), :] = both.astype(jnp.int16)


def value_rows(piece, jb, part):
    return pl.ds((EIGHTS * piece + piece % 2 + 4 * jb + 2 * part) * 8, 16)


def read_gains(in_ref, gain_ref):
    for pair in range(gain_ref.shape[0]):
        gain_ref[pair] = gains(in_ref[pl.ds((2 * EIGHTS * pair + EIGHTS - 1) * 8, 16), :])


def gains(codes):
    return jnp.exp2(codes.astype(jnp.int32).astype(jnp.float32) * (1.0 / STEPS)) * (1.0 / TOP)


def widen(value):
    return value.astype(jnp.int32).astype(jnp.float32)


def walk_at(place, chips):
    lines = chips // 2
    return jnp.where(place < lines, 2 * place, 2 * (chips - 1 - place) + 1)


def place_of(chip, chips):
    return jnp.where(chip % 2 == 0, chip // 2, chips - 1 - chip // 2)


def project_kernel(devices, sources, n_acc, packed, owner_ref, rows_ref, *refs):
    n = len(sources)
    panels = refs[:n]
    acc_in = refs[n : n + n_acc]
    acc_out = refs[-2] if packed else refs[-1]
    chips = devices // 2
    me = lax.axis_index("shell")
    part = lax.axis_index("grp")
    width = rows_ref.shape[2] // 2
    started = n_acc
    if n_acc:
        acc_out[...] = acc_in[0][...]
    for panel, (shift, flip, half) in zip(panels, sources):
        depth = panel.shape[0]
        ahead = jnp.where(me % 2 == 0, shift, -shift)
        place = lax.rem(place_of(me // 2, chips) + ahead + chips, chips)
        slot = 2 * walk_at(place, chips) + (me + flip) % 2
        degree = jnp.zeros((), jnp.int32)
        for l in range(rows_ref.shape[0]):
            degree = jnp.where(owner_ref[l] == slot, l, degree)
        offset = 0 if half is None else depth * (part + half) % (2 * depth)
        left = jnp.concatenate(
            [rows_ref[degree, :, pl.ds(pl.multiple_of(c * width + offset, 128), depth)] for c in range(2)]
        )
        product = jnp.dot(left, panel[...], preferred_element_type=jnp.float32)
        acc_out[...] = acc_out[...] + product if started else product
        started = 1
    if packed:
        pack(acc_out, refs[-1], refs[-3])


def project(acc, rows, owner, panels, sources, packed=None):
    count, width = rows.shape[1], panels[0].shape[1]
    depth = sum(p.shape[0] for p in panels)
    n_acc = 0 if acc is None else 1
    total = jax.ShapeDtypeStruct((2 * count, width), jnp.float32)
    return pl.pallas_call(
        functools.partial(
            project_kernel, lax.axis_size("shell"), tuple(sources), n_acc, packed is not None
        ),
        in_specs=[pl.BlockSpec(memory_space=pltpu.SMEM)]
        + [pl.BlockSpec(memory_space=pltpu.VMEM)] * (1 + len(panels) + n_acc),
        out_specs=pl.BlockSpec(memory_space=pltpu.VMEM),
        out_shape=total if packed is None else packed,
        scratch_shapes=[]
        if packed is None
        else [
            pltpu.VMEM(total.shape, total.dtype),
            pltpu.VMEM((packed.shape[0] // 8, 8, LANES), jnp.int32),
        ],
        compiler_params=pltpu.CompilerParams(vmem_limit_bytes=24 * 2**20),
        cost_estimate=pl.CostEstimate(
            flops=4 * count * depth * width,
            bytes_accessed=2 * depth * (width + 2 * count) + 8 * count * width * (1 + n_acc),
            transcendentals=0,
        ),
    )(owner, rows, *panels, *([acc] if n_acc else []))


def pack(proj_ref, stage_ref, out_ref):
    count, width = proj_ref.shape[0] // 2, proj_ref.shape[1]
    pieces = count // 16
    clear_codes(stage_ref, pieces)
    for d in range(pieces):
        for jb in range(width // LANES):
            lanes = pl.ds(jb * LANES, LANES)
            *coded, code = encode(
                proj_ref[pl.ds(16 * d, 16), lanes], proj_ref[pl.ds(count + 16 * d, 16), lanes]
            )
            stage_block(stage_ref, d, jb, coded, code)
    ship(stage_ref, out_ref)


def radix2(real_parts, imag_parts):
    n = len(real_parts)
    re, im = list(real_parts), list(imag_parts)
    half = n // 2
    while half:
        for start in range(0, n, 2 * half):
            for k in range(half):
                a, b = start + k, start + k + half
                dr, di = re[a] - re[b], im[a] - im[b]
                re[a], im[a] = re[a] + re[b], im[a] + im[b]
                angle = -math.pi * k / half
                if k == 0:
                    re[b], im[b] = dr, di
                elif 2 * k == half:
                    re[b], im[b] = di, -dr
                elif 4 * k == half:
                    re[b], im[b] = (dr + di) * math.cos(angle), (di - dr) * math.cos(angle)
                elif 4 * k == 3 * half:
                    re[b], im[b] = (di - dr) * math.cos(math.pi / 4), (dr + di) * -math.cos(math.pi / 4)
                else:
                    c, s = math.cos(angle), math.sin(angle)
                    re[b], im[b] = dr * c - di * s, dr * s + di * c
        half //= 2
    return re, im


def outer_kernel(in_ref, out_ref, gain_ref, stage_ref):
    n = 2 * gain_ref.shape[0]
    read_gains(in_ref, gain_ref)
    clear_codes(stage_ref, n)
    for jb in range((EIGHTS - 1) // 4):
        re, im = [], []
        for q in range(n):
            gain = gain_ref[q // 2, pl.ds(8 * (q % 2) + jb, 1), :]
            re.append(widen(in_ref[value_rows(q, jb, 0), :]) * gain)
            im.append(widen(in_ref[value_rows(q, jb, 1), :]) * gain)
        re, im = radix2(re, im)
        for p in range(n):
            *coded, code = encode(re[p], im[p])
            stage_block(stage_ref, p, jb, coded, code)
    ship(stage_ref, out_ref)


def inner_kernel(twist_ref, in_ref, out_ref, gain_ref):
    n = 2 * gain_ref.shape[0]
    orders = 2 * n
    nbits = orders.bit_length() - 1
    read_gains(in_ref, gain_ref)
    for jb in range((EIGHTS - 1) // 4):
        re, im = [], []
        for d in range(n):
            gain = gain_ref[d // 2, pl.ds(8 * (d % 2) + jb, 1), :]
            both_re = widen(in_ref[value_rows(d, jb, 0), :]) * gain
            both_im = widen(in_ref[value_rows(d, jb, 1), :]) * gain
            for r in range(2):
                a, b = both_re[8 * r : 8 * r + 8], both_im[8 * r : 8 * r + 8]
                c, s = twist_ref[0, 2 * d + r], twist_ref[1, 2 * d + r]
                re.append(a * c - b * s)
                im.append(a * s + b * c)
        re, im = radix2(re, im)
        for p in range(orders):
            h = bit_reverse(p, nbits)
            for part, value in enumerate((re[p], im[p])):
                for b in range(2):
                    first = (b * orders + h) * 32 + 2 * jb + part
                    out_ref[pl.ds(first, 4, stride=8), :] = value[4 * b : 4 * b + 4]


def local_call(kernel, out, scratch, *args, smem=0):
    return pl.pallas_call(
        kernel,
        in_specs=[pl.BlockSpec(memory_space=pltpu.SMEM)] * smem
        + [pl.BlockSpec(memory_space=pltpu.VMEM)] * (len(args) - smem),
        out_specs=pl.BlockSpec(memory_space=pltpu.VMEM),
        out_shape=out,
        scratch_shapes=scratch,
        compiler_params=pltpu.CompilerParams(vmem_limit_bytes=24 * 2**20),
    )(*args)


def shards(pair_coef, panel_pool, degree_owner, batch_order):
    local_orders, shells = pair_coef.shape[:2]
    width = panel_pool.shape[2]
    devices = lax.axis_size("shell")
    total_orders = local_orders * devices
    chips = devices // 2
    me = lax.axis_index("shell")
    lines = chips // 2
    walk = [2 * z for z in range(lines)] + [2 * z + 1 for z in reversed(range(lines))]

    onward = []
    for here, there in zip(walk, walk[1:] + walk[:1]):
        onward += [(2 * here, 2 * there), (2 * there + 1, 2 * here + 1)]

    def around(value):
        return lax.ppermute(value, "shell", onward)

    def crosswise(value):
        return lax.ppermute(value, "shell", [(source ^ 1, target) for source, target in onward])

    def sibling(value):
        return lax.ppermute(value, "shell", [(s, s ^ 1) for s in range(devices)])

    def across(value):
        return lax.ppermute(value, "grp", [(0, 1), (1, 0)])

    blocks = width // LANES
    parcels = jax.ShapeDtypeStruct((devices * EIGHTS * 8, LANES), jnp.int16)
    lines = pltpu.VMEM((devices // 2, 16, LANES), jnp.float32)
    stage = pltpu.VMEM((devices * EIGHTS, 8, LANES), jnp.int32)

    def exchange(value):
        value = value.reshape(devices, EIGHTS * 8, LANES)
        return lax.all_to_all(value, "shell", 0, 0).reshape(parcels.shape)

    own = panel_pool[0]
    half = own.shape[0] // 2
    whole = around(own)
    part = crosswise(lax.dynamic_slice_in_dim(own, half * lax.axis_index("grp"), half))
    other = sibling(own)
    rows = sort_rows(pair_coef, batch_order)
    acc = project(None, rows, degree_owner, [own, other], [(0, 0, None), (0, 1, None)])
    whole, part, rows = lax.optimization_barrier((whole, part, rows))
    late, late_from = [], []
    for step in range(1, chips // 2):
        if step > 1:
            whole, acc = lax.optimization_barrier((whole, acc))
        next_whole = around(whole)
        next_part = around(part) if step + 1 < chips // 2 else None
        rest = across(part)
        acc = project(
            acc,
            rows,
            degree_owner,
            [whole, sibling(whole), part, sibling(part), *late],
            [(-step, 0, None), (step, 1, None), (-step, 1, 0), (step, 0, 0), *late_from],
        )
        late, late_from = [rest, sibling(rest)], [(-step, 1, 1), (step, 0, 1)]
        whole, part = next_whole, next_part
    whole, acc = lax.optimization_barrier((whole, acc))
    sent = project(
        acc,
        rows,
        degree_owner,
        [whole, sibling(whole), *late],
        [(-(chips // 2), 0, None), (chips // 2, 1, None), *late_from],
        packed=parcels,
    )
    sent = local_call(outer_kernel, parcels, [lines, stage], exchange(sent))
    sent = exchange(sent)
    first = bit_reverse(me, devices.bit_length() - 1)
    phase = lax.iota(jnp.int32, local_orders) * first % total_orders
    angle = -2.0 * math.pi * phase.astype(jnp.float32) / float(total_orders)
    twist = jnp.stack([jnp.cos(angle), jnp.sin(angle)]) * (1.0 / math.sqrt(total_orders))
    out = jax.ShapeDtypeStruct((2 * local_orders * shells // 2 * 2 * blocks, LANES), jnp.float32)
    scores = local_call(inner_kernel, out, [lines], twist, sent, smem=1)
    scores = scores.reshape(2, local_orders, shells // 2, blocks, 2, LANES)
    return scores.transpose(0, 1, 2, 4, 3, 5).reshape(2, local_orders, shells // 2, 2, width)


def solution(mesh):
    devices = mesh.shape["shell"]
    return jax.shard_map(
        shards if (devices, mesh.shape["grp"]) == (16, 2) else general,
        mesh=mesh,
        in_specs=(P(("grp", "shell"), None, None, None), P("shell", None, None), P(), P()),
        out_specs=P(None, ("grp", "shell"), None, None, None),
        check_vma=False,
    )
```

```python
import functools
import math

import jax
import jax.numpy as jnp
from jax import lax
from jax.experimental import pallas as pl
from jax.experimental.pallas import tpu as pltpu
from jax.sharding import PartitionSpec as P


def broadcast(value, axis, root):
    mine = lax.axis_index(axis) == root
    return lax.psum(jnp.where(mine, value, jnp.zeros_like(value)), axis)


def partner(value, axis, distance):
    mask = 2**distance
    pairs = [(source, source ^ mask) for source in range(lax.axis_size(axis))]
    return lax.ppermute(value, axis, pairs)


def rotate(real_part, imag_part, cosine, sine):
    return (real_part * cosine - imag_part * sine, real_part * sine + imag_part * cosine)


def general(pair_coef, panel_pool, degree_owner, batch_order):
    local_orders = pair_coef.shape[0]
    degrees = pair_coef.shape[2]
    width = pair_coef.shape[3] // 2
    batch_rows = batch_order.shape[0] // 2
    devices = lax.axis_size("shell")
    total_orders = local_orders * devices
    first = jnp.take(pair_coef, batch_order[:batch_rows], axis=1)
    second = jnp.take(pair_coef, batch_order[batch_rows:], axis=1)
    rows = jnp.stack([first, second])

    def add_degree(degree, total):
        panel = broadcast(panel_pool[0], "shell", degree_owner[degree])
        piece = lax.dynamic_index_in_dim(rows, degree, axis=3, keepdims=False).reshape(-1, width)
        return total + jnp.dot(piece, panel, preferred_element_type=jnp.float32)

    total = lax.fori_loop(
        0, degrees, add_degree, jnp.zeros((2 * local_orders * batch_rows * 2, width), jnp.float32)
    )
    proj = total.reshape(2, local_orders, batch_rows, 2, width)
    nbits = devices.bit_length() - 1
    high = lax.Precision.HIGHEST
    me = lax.axis_index("shell")
    blocks = proj
    for bit in reversed(range(nbits)):
        other = partner(blocks, "shell", bit)
        upper = me >> bit & 1 == 1
        lower_val = jnp.where(upper, other, blocks)
        upper_val = jnp.where(upper, blocks, other)
        summed = lower_val + upper_val
        differ = lower_val - upper_val
        twist = (me % (1 << bit)).astype(jnp.float32)
        angle = -2.0 * math.pi * twist / float(2 << bit)
        new_real, new_imag = rotate(
            differ[:, :, :, 0], differ[:, :, :, 1], jnp.cos(angle), jnp.sin(angle)
        )
        turned = jnp.stack([new_real, new_imag], axis=3)
        blocks = jnp.where(upper, turned, summed)
    flipped = jnp.zeros((), jnp.int32)
    for bit in range(nbits):
        flipped = flipped | (me >> bit & 1) << nbits - 1 - bit
    inner = lax.iota(jnp.int32, local_orders)
    freq = flipped + devices * inner
    phase = inner[None, :] * freq[:, None] % total_orders
    angle = -2.0 * math.pi * phase.astype(jnp.float32) / float(total_orders)
    cosine = jnp.cos(angle)
    sine = jnp.sin(angle)
    real_part = blocks[:, :, :, 0]
    imag_part = blocks[:, :, :, 1]
    out_real = jnp.einsum("gr,brtj->bgtj", cosine, real_part, precision=high) - jnp.einsum(
        "gr,brtj->bgtj", sine, imag_part, precision=high
    )
    out_imag = jnp.einsum("gr,brtj->bgtj", sine, real_part, precision=high) + jnp.einsum(
        "gr,brtj->bgtj", cosine, imag_part, precision=high
    )
    result = jnp.stack([out_real, out_imag], axis=3)
    return result * (1.0 / math.sqrt(total_orders))


STEPS = 16.0
TOP = 32000.0
LANES = 128
GROUP = 4
SORT_LIMIT = 42


def bit_reverse(value, nbits):
    flipped = 0
    for bit in range(nbits):
        flipped = flipped | (value >> bit & 1) << nbits - 1 - bit
    return flipped


def sort_kernel(order_ref, coef_ref, out_ref, perm_ref, held_ref, sems):
    rows = perm_ref.shape[0]
    blocks = held_ref.shape[0] // rows
    degrees = out_ref.shape[0]
    shells = order_ref.shape[0]
    slab = rows // degrees

    def copy(i):
        block = coef_ref.at[pl.ds(i * rows, GROUP * rows), :]
        return pltpu.make_async_copy(block, held_ref.at[pl.ds(i * rows, GROUP * rows), :], sems.at[i])

    for i in range(0, blocks, GROUP):
        copy(i).start()
    line = lax.broadcasted_iota(jnp.int32, (slab, rows), 0)
    in_at = lax.broadcasted_iota(jnp.int32, (slab, rows), 1)
    wanted = jnp.zeros(line.shape, jnp.int32)
    for at in range(slab):
        source = (at // shells * shells + order_ref[at % shells]) * degrees
        wanted = jnp.where(line == at, source, wanted)
    for l in range(degrees):
        chosen = jnp.where(in_at == wanted + l, 1.0, 0.0).astype(perm_ref.dtype)
        perm_ref[pl.ds(l * slab, slab), :] = chosen

    for i in range(blocks):
        if i % GROUP == 0:
            copy(i).wait()
        moved = jnp.dot(perm_ref[...], held_ref[pl.ds(i * rows, rows), :], preferred_element_type=jnp.float32)
        out_ref[:, pl.ds(i * slab, slab), :] = moved.astype(out_ref.dtype).reshape(
            degrees, slab, moved.shape[1]
        )


def sort_rows(pair_coef, batch_order):
    orders, shells, degrees, width = pair_coef.shape
    group = 16 // shells
    rows = group * shells * degrees
    blocks = orders // group
    return pl.pallas_call(
        sort_kernel,
        in_specs=[pl.BlockSpec(memory_space=pltpu.SMEM), pl.BlockSpec(memory_space=pltpu.HBM)],
        out_specs=pl.BlockSpec(memory_space=pltpu.VMEM),
        out_shape=jax.ShapeDtypeStruct((degrees, orders * shells, width), pair_coef.dtype),
        scratch_shapes=[
            pltpu.VMEM((rows, rows), pair_coef.dtype),
            pltpu.VMEM((blocks * rows, width), pair_coef.dtype),
            pltpu.SemaphoreType.DMA((blocks,)),
        ],
        compiler_params=pltpu.CompilerParams(vmem_limit_bytes=SORT_LIMIT * 2**20),
        cost_estimate=pl.CostEstimate(
            flops=2 * blocks * rows * rows * width,
            bytes_accessed=4 * blocks * rows * width,
            transcendentals=0,
        ),
    )(batch_order, pair_coef.reshape(orders * shells * degrees, width))


def scale_code(largest):
    return jnp.ceil(jnp.log2(jnp.maximum(largest, 1e-30)) * STEPS) + 1.0


def encode(real_part, imag_part):
    largest = jnp.max(jnp.maximum(jnp.abs(real_part), jnp.abs(imag_part)), axis=0, keepdims=True)
    code = scale_code(largest)
    gain = jnp.exp2(code * (-1.0 / STEPS)) * TOP
    coded = [jnp.floor(v * gain + 0.5).astype(jnp.int32) for v in (real_part, imag_part)]
    return coded[0], coded[1], code


EIGHTS = 17


def stage_block(stage_ref, piece, jb, coded, code):
    odd = lax.axis_index("shell") % 2
    first = EIGHTS * piece + odd + 4 * jb
    for part in range(2):
        stage_ref[pl.ds(first + 2 * part, 2)] = coded[part].reshape(2, 8, LANES)
    stage_ref[EIGHTS * piece + (EIGHTS - 1) * (1 - odd), pl.ds(jb, 1), :] = code.astype(jnp.int32)


def clear_codes(stage_ref, pieces):
    odd = lax.axis_index("shell") % 2
    for piece in range(pieces):
        stage_ref[EIGHTS * piece + (EIGHTS - 1) * (1 - odd)] = jnp.zeros((8, LANES), jnp.int32)


def ship(stage_ref, out_ref):
    for pair in range(stage_ref.shape[0] // 2):
        both = stage_ref[pl.ds(2 * pair, 2)].reshape(16, LANES)
        out_ref[pl.ds(16 * pair, 16), :] = both.astype(jnp.int16)


def value_rows(piece, jb, part):
    return pl.ds((EIGHTS * piece + piece % 2 + 4 * jb + 2 * part) * 8, 16)


def read_gains(in_ref, gain_ref):
    for pair in range(gain_ref.shape[0]):
        gain_ref[pair] = gains(in_ref[pl.ds((2 * EIGHTS * pair + EIGHTS - 1) * 8, 16), :])


def gains(codes):
    return jnp.exp2(codes.astype(jnp.int32).astype(jnp.float32) * (1.0 / STEPS)) * (1.0 / TOP)


def widen(value):
    return value.astype(jnp.int32).astype(jnp.float32)


def walk_at(place, chips):
    lines = chips // 2
    return jnp.where(place < lines, 2 * place, 2 * (chips - 1 - place) + 1)


def place_of(chip, chips):
    return jnp.where(chip % 2 == 0, chip // 2, chips - 1 - chip // 2)


def project_kernel(devices, sources, n_acc, packed, owner_ref, rows_ref, *refs):
    n = len(sources)
    panels = refs[:n]
    acc_in = refs[n : n + n_acc]
    acc_out = refs[-2] if packed else refs[-1]
    chips = devices // 2
    me = lax.axis_index("shell")
    part = lax.axis_index("grp")
    width = rows_ref.shape[2] // 2
    started = n_acc
    if n_acc:
        acc_out[...] = acc_in[0][...]
    for panel, (shift, flip, half) in zip(panels, sources):
        depth = panel.shape[0]
        ahead = jnp.where(me % 2 == 0, shift, -shift)
        place = lax.rem(place_of(me // 2, chips) + ahead + chips, chips)
        slot = 2 * walk_at(place, chips) + (me + flip) % 2
        degree = jnp.zeros((), jnp.int32)
        for l in range(rows_ref.shape[0]):
            degree = jnp.where(owner_ref[l] == slot, l, degree)
        offset = 0 if half is None else depth * (part + half) % (2 * depth)
        left = jnp.concatenate(
            [rows_ref[degree, :, pl.ds(pl.multiple_of(c * width + offset, 128), depth)] for c in range(2)]
        )
        product = jnp.dot(left, panel[...], preferred_element_type=jnp.float32)
        acc_out[...] = acc_out[...] + product if started else product
        started = 1
    if packed:
        pack(acc_out, refs[-1], refs[-3])


def project(acc, rows, owner, panels, sources, packed=None):
    count, width = rows.shape[1], panels[0].shape[1]
    depth = sum(p.shape[0] for p in panels)
    n_acc = 0 if acc is None else 1
    total = jax.ShapeDtypeStruct((2 * count, width), jnp.float32)
    return pl.pallas_call(
        functools.partial(
            project_kernel, lax.axis_size("shell"), tuple(sources), n_acc, packed is not None
        ),
        in_specs=[pl.BlockSpec(memory_space=pltpu.SMEM)]
        + [pl.BlockSpec(memory_space=pltpu.VMEM)] * (1 + len(panels) + n_acc),
        out_specs=pl.BlockSpec(memory_space=pltpu.VMEM),
        out_shape=total if packed is None else packed,
        scratch_shapes=[]
        if packed is None
        else [
            pltpu.VMEM(total.shape, total.dtype),
            pltpu.VMEM((packed.shape[0] // 8, 8, LANES), jnp.int32),
        ],
        compiler_params=pltpu.CompilerParams(vmem_limit_bytes=24 * 2**20),
        cost_estimate=pl.CostEstimate(
            flops=4 * count * depth * width,
            bytes_accessed=2 * depth * (width + 2 * count) + 8 * count * width * (1 + n_acc),
            transcendentals=0,
        ),
    )(owner, rows, *panels, *([acc] if n_acc else []))


def pack(proj_ref, stage_ref, out_ref):
    count, width = proj_ref.shape[0] // 2, proj_ref.shape[1]
    pieces = count // 16
    clear_codes(stage_ref, pieces)
    for d in range(pieces):
        for jb in range(width // LANES):
            lanes = pl.ds(jb * LANES, LANES)
            *coded, code = encode(
                proj_ref[pl.ds(16 * d, 16), lanes], proj_ref[pl.ds(count + 16 * d, 16), lanes]
            )
            stage_block(stage_ref, d, jb, coded, code)
    ship(stage_ref, out_ref)


def radix2(real_parts, imag_parts):
    n = len(real_parts)
    re, im = list(real_parts), list(imag_parts)
    half = n // 2
    while half:
        for start in range(0, n, 2 * half):
            for k in range(half):
                a, b = start + k, start + k + half
                dr, di = re[a] - re[b], im[a] - im[b]
                re[a], im[a] = re[a] + re[b], im[a] + im[b]
                angle = -math.pi * k / half
                if k == 0:
                    re[b], im[b] = dr, di
                elif 2 * k == half:
                    re[b], im[b] = di, -dr
                elif 4 * k == half:
                    re[b], im[b] = (dr + di) * math.cos(angle), (di - dr) * math.cos(angle)
                elif 4 * k == 3 * half:
                    re[b], im[b] = (di - dr) * math.cos(math.pi / 4), (dr + di) * -math.cos(math.pi / 4)
                else:
                    c, s = math.cos(angle), math.sin(angle)
                    re[b], im[b] = dr * c - di * s, dr * s + di * c
        half //= 2
    return re, im


def outer_kernel(in_ref, out_ref, gain_ref, stage_ref):
    n = 2 * gain_ref.shape[0]
    read_gains(in_ref, gain_ref)
    clear_codes(stage_ref, n)
    for jb in range((EIGHTS - 1) // 4):
        re, im = [], []
        for q in range(n):
            gain = gain_ref[q // 2, pl.ds(8 * (q % 2) + jb, 1), :]
            re.append(widen(in_ref[value_rows(q, jb, 0), :]) * gain)
            im.append(widen(in_ref[value_rows(q, jb, 1), :]) * gain)
        re, im = radix2(re, im)
        for p in range(n):
            *coded, code = encode(re[p], im[p])
            stage_block(stage_ref, p, jb, coded, code)
    ship(stage_ref, out_ref)


def inner_kernel(twist_ref, in_ref, out_ref, gain_ref):
    n = 2 * gain_ref.shape[0]
    orders = 2 * n
    nbits = orders.bit_length() - 1
    read_gains(in_ref, gain_ref)
    for jb in range((EIGHTS - 1) // 4):
        re, im = [], []
        for d in range(n):
            gain = gain_ref[d // 2, pl.ds(8 * (d % 2) + jb, 1), :]
            both_re = widen(in_ref[value_rows(d, jb, 0), :]) * gain
            both_im = widen(in_ref[value_rows(d, jb, 1), :]) * gain
            for r in range(2):
                a, b = both_re[8 * r : 8 * r + 8], both_im[8 * r : 8 * r + 8]
                c, s = twist_ref[0, 2 * d + r], twist_ref[1, 2 * d + r]
                re.append(a * c - b * s)
                im.append(a * s + b * c)
        re, im = radix2(re, im)
        for p in range(orders):
            h = bit_reverse(p, nbits)
            for part, value in enumerate((re[p], im[p])):
                for b in range(2):
                    first = (b * orders + h) * 32 + 2 * jb + part
                    out_ref[pl.ds(first, 4, stride=8), :] = value[4 * b : 4 * b + 4]


def local_call(kernel, out, scratch, *args, smem=0):
    return pl.pallas_call(
        kernel,
        in_specs=[pl.BlockSpec(memory_space=pltpu.SMEM)] * smem
        + [pl.BlockSpec(memory_space=pltpu.VMEM)] * (len(args) - smem),
        out_specs=pl.BlockSpec(memory_space=pltpu.VMEM),
        out_shape=out,
        scratch_shapes=scratch,
        compiler_params=pltpu.CompilerParams(vmem_limit_bytes=24 * 2**20),
    )(*args)


def shards(pair_coef, panel_pool, degree_owner, batch_order):
    local_orders, shells = pair_coef.shape[:2]
    width = panel_pool.shape[2]
    devices = lax.axis_size("shell")
    total_orders = local_orders * devices
    chips = devices // 2
    me = lax.axis_index("shell")
    lines = chips // 2
    walk = [2 * z for z in range(lines)] + [2 * z + 1 for z in reversed(range(lines))]

    onward = []
    for here, there in zip(walk, walk[1:] + walk[:1]):
        onward += [(2 * here, 2 * there), (2 * there + 1, 2 * here + 1)]

    def around(value):
        return lax.ppermute(value, "shell", onward)

    def crosswise(value):
        return lax.ppermute(value, "shell", [(source ^ 1, target) for source, target in onward])

    def sibling(value):
        return lax.ppermute(value, "shell", [(s, s ^ 1) for s in range(devices)])

    def across(value):
        return lax.ppermute(value, "grp", [(0, 1), (1, 0)])

    blocks = width // LANES
    parcels = jax.ShapeDtypeStruct((devices * EIGHTS * 8, LANES), jnp.int16)
    lines = pltpu.VMEM((devices // 2, 16, LANES), jnp.float32)
    stage = pltpu.VMEM((devices * EIGHTS, 8, LANES), jnp.int32)

    def exchange(value):
        value = value.reshape(devices, EIGHTS * 8, LANES)
        return lax.all_to_all(value, "shell", 0, 0).reshape(parcels.shape)

    own = panel_pool[0]
    half = own.shape[0] // 2
    whole = around(own)
    part = crosswise(lax.dynamic_slice_in_dim(own, half * lax.axis_index("grp"), half))
    other = sibling(own)
    rows = sort_rows(pair_coef, batch_order)
    acc = project(None, rows, degree_owner, [own, other], [(0, 0, None), (0, 1, None)])
    whole, part, rows = lax.optimization_barrier((whole, part, rows))
    late, late_from = [], []
    for step in range(1, chips // 2):
        if step > 1:
            whole, acc = lax.optimization_barrier((whole, acc))
        next_whole = around(whole)
        next_part = around(part) if step + 1 < chips // 2 else None
        rest = across(part) if next_part is not None else around(late[0])
        acc = project(
            acc,
            rows,
            degree_owner,
            [whole, sibling(whole), part, sibling(part), *late],
            [(-step, 0, None), (step, 1, None), (-step, 1, 0), (step, 0, 0), *late_from],
        )
        late, late_from = [rest, sibling(rest)], [(-step, 1, 1), (step, 0, 1)]
        whole, part = next_whole, next_part
    whole, acc = lax.optimization_barrier((whole, acc))
    sent = project(
        acc,
        rows,
        degree_owner,
        [whole, sibling(whole), *late],
        [(-(chips // 2), 0, None), (chips // 2, 1, None), *late_from],
        packed=parcels,
    )
    sent = local_call(outer_kernel, parcels, [lines, stage], exchange(sent))
    sent = exchange(sent)
    first = bit_reverse(me, devices.bit_length() - 1)
    phase = lax.iota(jnp.int32, local_orders) * first % total_orders
    angle = -2.0 * math.pi * phase.astype(jnp.float32) / float(total_orders)
    twist = jnp.stack([jnp.cos(angle), jnp.sin(angle)]) * (1.0 / math.sqrt(total_orders))
    out = jax.ShapeDtypeStruct((2 * local_orders * shells // 2 * 2 * blocks, LANES), jnp.float32)
    scores = local_call(inner_kernel, out, [lines], twist, sent, smem=1)
    scores = scores.reshape(2, local_orders, shells // 2, blocks, 2, LANES)
    return scores.transpose(0, 1, 2, 4, 3, 5).reshape(2, local_orders, shells // 2, 2, width)


def solution(mesh):
    devices = mesh.shape["shell"]
    return jax.shard_map(
        shards if (devices, mesh.shape["grp"]) == (16, 2) else general,
        mesh=mesh,
        in_specs=(P(("grp", "shell"), None, None, None), P("shell", None, None), P(), P()),
        out_specs=P(None, ("grp", "shell"), None, None, None),
        check_vma=False,
    )
```

```python
import functools
import math

import jax
import jax.numpy as jnp
from jax import lax
from jax.experimental import pallas as pl
from jax.experimental.pallas import tpu as pltpu
from jax.sharding import PartitionSpec as P


def broadcast(value, axis, root):
    mine = lax.axis_index(axis) == root
    return lax.psum(jnp.where(mine, value, jnp.zeros_like(value)), axis)


def partner(value, axis, distance):
    mask = 2**distance
    pairs = [(source, source ^ mask) for source in range(lax.axis_size(axis))]
    return lax.ppermute(value, axis, pairs)


def rotate(real_part, imag_part, cosine, sine):
    return (real_part * cosine - imag_part * sine, real_part * sine + imag_part * cosine)


def general(pair_coef, panel_pool, degree_owner, batch_order):
    local_orders = pair_coef.shape[0]
    degrees = pair_coef.shape[2]
    width = pair_coef.shape[3] // 2
    batch_rows = batch_order.shape[0] // 2
    devices = lax.axis_size("shell")
    total_orders = local_orders * devices
    first = jnp.take(pair_coef, batch_order[:batch_rows], axis=1)
    second = jnp.take(pair_coef, batch_order[batch_rows:], axis=1)
    rows = jnp.stack([first, second])

    def add_degree(degree, total):
        panel = broadcast(panel_pool[0], "shell", degree_owner[degree])
        piece = lax.dynamic_index_in_dim(rows, degree, axis=3, keepdims=False).reshape(-1, width)
        return total + jnp.dot(piece, panel, preferred_element_type=jnp.float32)

    total = lax.fori_loop(
        0, degrees, add_degree, jnp.zeros((2 * local_orders * batch_rows * 2, width), jnp.float32)
    )
    proj = total.reshape(2, local_orders, batch_rows, 2, width)
    nbits = devices.bit_length() - 1
    high = lax.Precision.HIGHEST
    me = lax.axis_index("shell")
    blocks = proj
    for bit in reversed(range(nbits)):
        other = partner(blocks, "shell", bit)
        upper = me >> bit & 1 == 1
        lower_val = jnp.where(upper, other, blocks)
        upper_val = jnp.where(upper, blocks, other)
        summed = lower_val + upper_val
        differ = lower_val - upper_val
        twist = (me % (1 << bit)).astype(jnp.float32)
        angle = -2.0 * math.pi * twist / float(2 << bit)
        new_real, new_imag = rotate(
            differ[:, :, :, 0], differ[:, :, :, 1], jnp.cos(angle), jnp.sin(angle)
        )
        turned = jnp.stack([new_real, new_imag], axis=3)
        blocks = jnp.where(upper, turned, summed)
    flipped = jnp.zeros((), jnp.int32)
    for bit in range(nbits):
        flipped = flipped | (me >> bit & 1) << nbits - 1 - bit
    inner = lax.iota(jnp.int32, local_orders)
    freq = flipped + devices * inner
    phase = inner[None, :] * freq[:, None] % total_orders
    angle = -2.0 * math.pi * phase.astype(jnp.float32) / float(total_orders)
    cosine = jnp.cos(angle)
    sine = jnp.sin(angle)
    real_part = blocks[:, :, :, 0]
    imag_part = blocks[:, :, :, 1]
    out_real = jnp.einsum("gr,brtj->bgtj", cosine, real_part, precision=high) - jnp.einsum(
        "gr,brtj->bgtj", sine, imag_part, precision=high
    )
    out_imag = jnp.einsum("gr,brtj->bgtj", sine, real_part, precision=high) + jnp.einsum(
        "gr,brtj->bgtj", cosine, imag_part, precision=high
    )
    result = jnp.stack([out_real, out_imag], axis=3)
    return result * (1.0 / math.sqrt(total_orders))


STEPS = 16.0
TOP = 32000.0
LANES = 128
GROUP = 4
SORT_LIMIT = 42


def bit_reverse(value, nbits):
    flipped = 0
    for bit in range(nbits):
        flipped = flipped | (value >> bit & 1) << nbits - 1 - bit
    return flipped


def sort_kernel(order_ref, coef_ref, out_ref, perm_ref, held_ref, sems):
    rows = perm_ref.shape[0]
    blocks = held_ref.shape[0] // rows
    degrees = out_ref.shape[0]
    shells = order_ref.shape[0]
    slab = rows // degrees

    def copy(i):
        block = coef_ref.at[pl.ds(i * rows, GROUP * rows), :]
        return pltpu.make_async_copy(block, held_ref.at[pl.ds(i * rows, GROUP * rows), :], sems.at[i])

    for i in range(0, blocks, GROUP):
        copy(i).start()
    line = lax.broadcasted_iota(jnp.int32, (slab, rows), 0)
    in_at = lax.broadcasted_iota(jnp.int32, (slab, rows), 1)
    wanted = jnp.zeros(line.shape, jnp.int32)
    for at in range(slab):
        source = (at // shells * shells + order_ref[at % shells]) * degrees
        wanted = jnp.where(line == at, source, wanted)
    for l in range(degrees):
        chosen = jnp.where(in_at == wanted + l, 1.0, 0.0).astype(perm_ref.dtype)
        perm_ref[pl.ds(l * slab, slab), :] = chosen

    for i in range(blocks):
        if i % GROUP == 0:
            copy(i).wait()
        moved = jnp.dot(perm_ref[...], held_ref[pl.ds(i * rows, rows), :], preferred_element_type=jnp.float32)
        out_ref[:, pl.ds(i * slab, slab), :] = moved.astype(out_ref.dtype).reshape(
            degrees, slab, moved.shape[1]
        )


def sort_rows(pair_coef, batch_order):
    orders, shells, degrees, width = pair_coef.shape
    group = 16 // shells
    rows = group * shells * degrees
    blocks = orders // group
    return pl.pallas_call(
        sort_kernel,
        in_specs=[pl.BlockSpec(memory_space=pltpu.SMEM), pl.BlockSpec(memory_space=pltpu.HBM)],
        out_specs=pl.BlockSpec(memory_space=pltpu.VMEM),
        out_shape=jax.ShapeDtypeStruct((degrees, orders * shells, width), pair_coef.dtype),
        scratch_shapes=[
            pltpu.VMEM((rows, rows), pair_coef.dtype),
            pltpu.VMEM((blocks * rows, width), pair_coef.dtype),
            pltpu.SemaphoreType.DMA((blocks,)),
        ],
        compiler_params=pltpu.CompilerParams(vmem_limit_bytes=SORT_LIMIT * 2**20),
        cost_estimate=pl.CostEstimate(
            flops=2 * blocks * rows * rows * width,
            bytes_accessed=4 * blocks * rows * width,
            transcendentals=0,
        ),
    )(batch_order, pair_coef.reshape(orders * shells * degrees, width))


def scale_code(largest):
    return jnp.ceil(jnp.log2(jnp.maximum(largest, 1e-30)) * STEPS) + 1.0


def encode(real_part, imag_part):
    largest = jnp.max(jnp.maximum(jnp.abs(real_part), jnp.abs(imag_part)), axis=0, keepdims=True)
    code = scale_code(largest)
    gain = jnp.exp2(code * (-1.0 / STEPS)) * TOP
    coded = [jnp.floor(v * gain + 0.5).astype(jnp.int32) for v in (real_part, imag_part)]
    return coded[0], coded[1], code


EIGHTS = 17


def stage_block(stage_ref, piece, jb, coded, code):
    odd = lax.axis_index("shell") % 2
    first = EIGHTS * piece + odd + 4 * jb
    for part in range(2):
        stage_ref[pl.ds(first + 2 * part, 2)] = coded[part].reshape(2, 8, LANES)
    stage_ref[EIGHTS * piece + (EIGHTS - 1) * (1 - odd), pl.ds(jb, 1), :] = code.astype(jnp.int32)


def clear_codes(stage_ref, pieces):
    odd = lax.axis_index("shell") % 2
    for piece in range(pieces):
        stage_ref[EIGHTS * piece + (EIGHTS - 1) * (1 - odd)] = jnp.zeros((8, LANES), jnp.int32)


def ship(stage_ref, out_ref):
    for pair in range(stage_ref.shape[0] // 2):
        both = stage_ref[pl.ds(2 * pair, 2)].reshape(16, LANES)
        out_ref[pl.ds(16 * pair, 16), :] = both.astype(jnp.int16)


def value_rows(piece, jb, part):
    return pl.ds((EIGHTS * piece + piece % 2 + 4 * jb + 2 * part) * 8, 16)


def read_gains(in_ref, gain_ref):
    for pair in range(gain_ref.shape[0]):
        gain_ref[pair] = gains(in_ref[pl.ds((2 * EIGHTS * pair + EIGHTS - 1) * 8, 16), :])


def gains(codes):
    return jnp.exp2(codes.astype(jnp.int32).astype(jnp.float32) * (1.0 / STEPS)) * (1.0 / TOP)


def widen(value):
    return value.astype(jnp.int32).astype(jnp.float32)


def walk_at(place, chips):
    lines = chips // 2
    return jnp.where(place < lines, 2 * place, 2 * (chips - 1 - place) + 1)


def place_of(chip, chips):
    return jnp.where(chip % 2 == 0, chip // 2, chips - 1 - chip // 2)


def project_kernel(devices, sources, n_acc, packed, owner_ref, rows_ref, *refs):
    n = len(sources)
    panels = refs[:n]
    acc_in = refs[n : n + n_acc]
    acc_out = refs[-2] if packed else refs[-1]
    chips = devices // 2
    me = lax.axis_index("shell")
    part = lax.axis_index("grp")
    width = rows_ref.shape[2] // 2
    started = n_acc
    if n_acc:
        acc_out[...] = acc_in[0][...]
    for panel, (shift, flip, half) in zip(panels, sources):
        depth = panel.shape[0]
        ahead = jnp.where(me % 2 == 0, shift, -shift)
        place = lax.rem(place_of(me // 2, chips) + ahead + chips, chips)
        slot = 2 * walk_at(place, chips) + (me + flip) % 2
        degree = jnp.zeros((), jnp.int32)
        for l in range(rows_ref.shape[0]):
            degree = jnp.where(owner_ref[l] == slot, l, degree)
        offset = 0 if half is None else depth * (part + half) % (2 * depth)
        left = jnp.concatenate(
            [rows_ref[degree, :, pl.ds(pl.multiple_of(c * width + offset, 128), depth)] for c in range(2)]
        )
        product = jnp.dot(left, panel[...], preferred_element_type=jnp.float32)
        acc_out[...] = acc_out[...] + product if started else product
        started = 1
    if packed:
        pack(acc_out, refs[-1], refs[-3])


def project(acc, rows, owner, panels, sources, packed=None):
    count, width = rows.shape[1], panels[0].shape[1]
    depth = sum(p.shape[0] for p in panels)
    n_acc = 0 if acc is None else 1
    total = jax.ShapeDtypeStruct((2 * count, width), jnp.float32)
    return pl.pallas_call(
        functools.partial(
            project_kernel, lax.axis_size("shell"), tuple(sources), n_acc, packed is not None
        ),
        in_specs=[pl.BlockSpec(memory_space=pltpu.SMEM)]
        + [pl.BlockSpec(memory_space=pltpu.VMEM)] * (1 + len(panels) + n_acc),
        out_specs=pl.BlockSpec(memory_space=pltpu.VMEM),
        out_shape=total if packed is None else packed,
        scratch_shapes=[]
        if packed is None
        else [
            pltpu.VMEM(total.shape, total.dtype),
            pltpu.VMEM((packed.shape[0] // 8, 8, LANES), jnp.int32),
        ],
        compiler_params=pltpu.CompilerParams(vmem_limit_bytes=24 * 2**20),
        cost_estimate=pl.CostEstimate(
            flops=4 * count * depth * width,
            bytes_accessed=2 * depth * (width + 2 * count) + 8 * count * width * (1 + n_acc),
            transcendentals=0,
        ),
    )(owner, rows, *panels, *([acc] if n_acc else []))


def pack(proj_ref, stage_ref, out_ref):
    count, width = proj_ref.shape[0] // 2, proj_ref.shape[1]
    pieces = count // 16
    clear_codes(stage_ref, pieces)
    for d in range(pieces):
        for jb in range(width // LANES):
            lanes = pl.ds(jb * LANES, LANES)
            *coded, code = encode(
                proj_ref[pl.ds(16 * d, 16), lanes], proj_ref[pl.ds(count + 16 * d, 16), lanes]
            )
            stage_block(stage_ref, d, jb, coded, code)
    ship(stage_ref, out_ref)


def radix2(real_parts, imag_parts):
    n = len(real_parts)
    re, im = list(real_parts), list(imag_parts)
    half = n // 2
    while half:
        for start in range(0, n, 2 * half):
            for k in range(half):
                a, b = start + k, start + k + half
                dr, di = re[a] - re[b], im[a] - im[b]
                re[a], im[a] = re[a] + re[b], im[a] + im[b]
                angle = -math.pi * k / half
                if k == 0:
                    re[b], im[b] = dr, di
                elif 2 * k == half:
                    re[b], im[b] = di, -dr
                elif 4 * k == half:
                    re[b], im[b] = (dr + di) * math.cos(angle), (di - dr) * math.cos(angle)
                elif 4 * k == 3 * half:
                    re[b], im[b] = (di - dr) * math.cos(math.pi / 4), (dr + di) * -math.cos(math.pi / 4)
                else:
                    c, s = math.cos(angle), math.sin(angle)
                    re[b], im[b] = dr * c - di * s, dr * s + di * c
        half //= 2
    return re, im


def outer_kernel(in_ref, out_ref, gain_ref, stage_ref):
    n = 2 * gain_ref.shape[0]
    read_gains(in_ref, gain_ref)
    clear_codes(stage_ref, n)
    for jb in range((EIGHTS - 1) // 4):
        re, im = [], []
        for q in range(n):
            gain = gain_ref[q // 2, pl.ds(8 * (q % 2) + jb, 1), :]
            re.append(widen(in_ref[value_rows(q, jb, 0), :]) * gain)
            im.append(widen(in_ref[value_rows(q, jb, 1), :]) * gain)
        re, im = radix2(re, im)
        for p in range(n):
            *coded, code = encode(re[p], im[p])
            stage_block(stage_ref, p, jb, coded, code)
    ship(stage_ref, out_ref)


def inner_kernel(twist_ref, in_ref, out_ref, gain_ref):
    n = 2 * gain_ref.shape[0]
    orders = 2 * n
    nbits = orders.bit_length() - 1
    read_gains(in_ref, gain_ref)
    for jb in range((EIGHTS - 1) // 4):
        re, im = [], []
        for d in range(n):
            gain = gain_ref[d // 2, pl.ds(8 * (d % 2) + jb, 1), :]
            both_re = widen(in_ref[value_rows(d, jb, 0), :]) * gain
            both_im = widen(in_ref[value_rows(d, jb, 1), :]) * gain
            for r in range(2):
                a, b = both_re[8 * r : 8 * r + 8], both_im[8 * r : 8 * r + 8]
                c, s = twist_ref[0, 2 * d + r], twist_ref[1, 2 * d + r]
                re.append(a * c - b * s)
                im.append(a * s + b * c)
        re, im = radix2(re, im)
        for p in range(orders):
            h = bit_reverse(p, nbits)
            for part, value in enumerate((re[p], im[p])):
                for b in range(2):
                    first = (b * orders + h) * 32 + 2 * jb + part
                    out_ref[pl.ds(first, 4, stride=8), :] = value[4 * b : 4 * b + 4]


def local_call(kernel, out, scratch, *args, smem=0):
    return pl.pallas_call(
        kernel,
        in_specs=[pl.BlockSpec(memory_space=pltpu.SMEM)] * smem
        + [pl.BlockSpec(memory_space=pltpu.VMEM)] * (len(args) - smem),
        out_specs=pl.BlockSpec(memory_space=pltpu.VMEM),
        out_shape=out,
        scratch_shapes=scratch,
        compiler_params=pltpu.CompilerParams(vmem_limit_bytes=24 * 2**20),
    )(*args)


def shards(pair_coef, panel_pool, degree_owner, batch_order):
    local_orders, shells = pair_coef.shape[:2]
    width = panel_pool.shape[2]
    devices = lax.axis_size("shell")
    total_orders = local_orders * devices
    chips = devices // 2
    me = lax.axis_index("shell")
    lines = chips // 2
    walk = [2 * z for z in range(lines)] + [2 * z + 1 for z in reversed(range(lines))]

    onward = []
    for here, there in zip(walk, walk[1:] + walk[:1]):
        onward += [(2 * here, 2 * there), (2 * there + 1, 2 * here + 1)]

    def around(value):
        return lax.ppermute(value, "shell", onward)

    def crosswise(value):
        return lax.ppermute(value, "shell", [(source ^ 1, target) for source, target in onward])

    def sibling(value):
        return lax.ppermute(value, "shell", [(s, s ^ 1) for s in range(devices)])

    def across(value):
        return lax.ppermute(value, "grp", [(0, 1), (1, 0)])

    blocks = width // LANES
    parcels = jax.ShapeDtypeStruct((devices * EIGHTS * 8, LANES), jnp.int16)
    lines = pltpu.VMEM((devices // 2, 16, LANES), jnp.float32)
    stage = pltpu.VMEM((devices * EIGHTS, 8, LANES), jnp.int32)

    def exchange(value):
        value = value.reshape(devices, EIGHTS * 8, LANES)
        return lax.all_to_all(value, "shell", 0, 0).reshape(parcels.shape)

    own = panel_pool[0]
    half = own.shape[0] // 2
    whole = around(own)
    part = crosswise(lax.dynamic_slice_in_dim(own, half * lax.axis_index("grp"), half))
    other = sibling(own)
    rows = sort_rows(pair_coef, batch_order)
    acc = project(None, rows, degree_owner, [own, other], [(0, 0, None), (0, 1, None)])
    whole, part, rows = lax.optimization_barrier((whole, part, rows))
    late, late_from = [], []
    for step in range(1, chips // 2):
        if step > 1:
            whole, acc = lax.optimization_barrier((whole, acc))
        next_whole = around(whole)
        next_part = around(part) if step + 1 < chips // 2 else None
        rest = across(part) if next_part is not None else around(late[0])
        acc = project(
            acc,
            rows,
            degree_owner,
            [whole, sibling(whole), part, sibling(part), *late],
            [(-step, 0, None), (step, 1, None), (-step, 1, 0), (step, 0, 0), *late_from],
        )
        late, late_from = [rest, sibling(rest)], [(-step, 1, 1), (step, 0, 1)]
        whole, part = next_whole, next_part
    whole, acc = lax.optimization_barrier((whole, acc))
    far = chips // 2
    acc = project(acc, rows, degree_owner, [whole, late[0]], [(-far, 0, None), late_from[0]])
    sent = project(
        acc,
        rows,
        degree_owner,
        [sibling(whole), late[1]],
        [(far, 1, None), late_from[1]],
        packed=parcels,
    )
    sent = local_call(outer_kernel, parcels, [lines, stage], exchange(sent))
    sent = exchange(sent)
    first = bit_reverse(me, devices.bit_length() - 1)
    phase = lax.iota(jnp.int32, local_orders) * first % total_orders
    angle = -2.0 * math.pi * phase.astype(jnp.float32) / float(total_orders)
    twist = jnp.stack([jnp.cos(angle), jnp.sin(angle)]) * (1.0 / math.sqrt(total_orders))
    out = jax.ShapeDtypeStruct((2 * local_orders * shells // 2 * 2 * blocks, LANES), jnp.float32)
    scores = local_call(inner_kernel, out, [lines], twist, sent, smem=1)
    scores = scores.reshape(2, local_orders, shells // 2, blocks, 2, LANES)
    return scores.transpose(0, 1, 2, 4, 3, 5).reshape(2, local_orders, shells // 2, 2, width)


def solution(mesh):
    devices = mesh.shape["shell"]
    return jax.shard_map(
        shards if (devices, mesh.shape["grp"]) == (16, 2) else general,
        mesh=mesh,
        in_specs=(P(("grp", "shell"), None, None, None), P("shell", None, None), P(), P()),
        out_specs=P(None, ("grp", "shell"), None, None, None),
        check_vma=False,
    )
```

```python
import functools
import math

import jax
import jax.numpy as jnp
from jax import lax
from jax.experimental import pallas as pl
from jax.experimental.pallas import tpu as pltpu
from jax.sharding import PartitionSpec as P


def broadcast(value, axis, root):
    mine = lax.axis_index(axis) == root
    return lax.psum(jnp.where(mine, value, jnp.zeros_like(value)), axis)


def partner(value, axis, distance):
    mask = 2**distance
    pairs = [(source, source ^ mask) for source in range(lax.axis_size(axis))]
    return lax.ppermute(value, axis, pairs)


def rotate(real_part, imag_part, cosine, sine):
    return (real_part * cosine - imag_part * sine, real_part * sine + imag_part * cosine)


def general(pair_coef, panel_pool, degree_owner, batch_order):
    local_orders = pair_coef.shape[0]
    degrees = pair_coef.shape[2]
    width = pair_coef.shape[3] // 2
    batch_rows = batch_order.shape[0] // 2
    devices = lax.axis_size("shell")
    total_orders = local_orders * devices
    first = jnp.take(pair_coef, batch_order[:batch_rows], axis=1)
    second = jnp.take(pair_coef, batch_order[batch_rows:], axis=1)
    rows = jnp.stack([first, second])

    def add_degree(degree, total):
        panel = broadcast(panel_pool[0], "shell", degree_owner[degree])
        piece = lax.dynamic_index_in_dim(rows, degree, axis=3, keepdims=False).reshape(-1, width)
        return total + jnp.dot(piece, panel, preferred_element_type=jnp.float32)

    total = lax.fori_loop(
        0, degrees, add_degree, jnp.zeros((2 * local_orders * batch_rows * 2, width), jnp.float32)
    )
    proj = total.reshape(2, local_orders, batch_rows, 2, width)
    nbits = devices.bit_length() - 1
    high = lax.Precision.HIGHEST
    me = lax.axis_index("shell")
    blocks = proj
    for bit in reversed(range(nbits)):
        other = partner(blocks, "shell", bit)
        upper = me >> bit & 1 == 1
        lower_val = jnp.where(upper, other, blocks)
        upper_val = jnp.where(upper, blocks, other)
        summed = lower_val + upper_val
        differ = lower_val - upper_val
        twist = (me % (1 << bit)).astype(jnp.float32)
        angle = -2.0 * math.pi * twist / float(2 << bit)
        new_real, new_imag = rotate(
            differ[:, :, :, 0], differ[:, :, :, 1], jnp.cos(angle), jnp.sin(angle)
        )
        turned = jnp.stack([new_real, new_imag], axis=3)
        blocks = jnp.where(upper, turned, summed)
    flipped = jnp.zeros((), jnp.int32)
    for bit in range(nbits):
        flipped = flipped | (me >> bit & 1) << nbits - 1 - bit
    inner = lax.iota(jnp.int32, local_orders)
    freq = flipped + devices * inner
    phase = inner[None, :] * freq[:, None] % total_orders
    angle = -2.0 * math.pi * phase.astype(jnp.float32) / float(total_orders)
    cosine = jnp.cos(angle)
    sine = jnp.sin(angle)
    real_part = blocks[:, :, :, 0]
    imag_part = blocks[:, :, :, 1]
    out_real = jnp.einsum("gr,brtj->bgtj", cosine, real_part, precision=high) - jnp.einsum(
        "gr,brtj->bgtj", sine, imag_part, precision=high
    )
    out_imag = jnp.einsum("gr,brtj->bgtj", sine, real_part, precision=high) + jnp.einsum(
        "gr,brtj->bgtj", cosine, imag_part, precision=high
    )
    result = jnp.stack([out_real, out_imag], axis=3)
    return result * (1.0 / math.sqrt(total_orders))


STEPS = 16.0
TOP = 32000.0
LANES = 128
GROUP = 4
SORT_LIMIT = 42


def bit_reverse(value, nbits):
    flipped = 0
    for bit in range(nbits):
        flipped = flipped | (value >> bit & 1) << nbits - 1 - bit
    return flipped


def sort_kernel(order_ref, coef_ref, out_ref, perm_ref, held_ref, sems):
    rows = perm_ref.shape[0]
    blocks = held_ref.shape[0] // rows
    degrees = out_ref.shape[0]
    shells = order_ref.shape[0]
    slab = rows // degrees

    def copy(i):
        block = coef_ref.at[pl.ds(i * rows, GROUP * rows), :]
        return pltpu.make_async_copy(block, held_ref.at[pl.ds(i * rows, GROUP * rows), :], sems.at[i])

    for i in range(0, blocks, GROUP):
        copy(i).start()
    line = lax.broadcasted_iota(jnp.int32, (slab, rows), 0)
    in_at = lax.broadcasted_iota(jnp.int32, (slab, rows), 1)
    wanted = jnp.zeros(line.shape, jnp.int32)
    for at in range(slab):
        source = (at // shells * shells + order_ref[at % shells]) * degrees
        wanted = jnp.where(line == at, source, wanted)
    for l in range(degrees):
        chosen = jnp.where(in_at == wanted + l, 1.0, 0.0).astype(perm_ref.dtype)
        perm_ref[pl.ds(l * slab, slab), :] = chosen

    for i in range(blocks):
        if i % GROUP == 0:
            copy(i).wait()
        moved = jnp.dot(perm_ref[...], held_ref[pl.ds(i * rows, rows), :], preferred_element_type=jnp.float32)
        out_ref[:, pl.ds(i * slab, slab), :] = moved.astype(out_ref.dtype).reshape(
            degrees, slab, moved.shape[1]
        )


def sort_rows(pair_coef, batch_order):
    orders, shells, degrees, width = pair_coef.shape
    group = 16 // shells
    rows = group * shells * degrees
    blocks = orders // group
    return pl.pallas_call(
        sort_kernel,
        in_specs=[pl.BlockSpec(memory_space=pltpu.SMEM), pl.BlockSpec(memory_space=pltpu.HBM)],
        out_specs=pl.BlockSpec(memory_space=pltpu.VMEM),
        out_shape=jax.ShapeDtypeStruct((degrees, orders * shells, width), pair_coef.dtype),
        scratch_shapes=[
            pltpu.VMEM((rows, rows), pair_coef.dtype),
            pltpu.VMEM((blocks * rows, width), pair_coef.dtype),
            pltpu.SemaphoreType.DMA((blocks,)),
        ],
        compiler_params=pltpu.CompilerParams(vmem_limit_bytes=SORT_LIMIT * 2**20),
        cost_estimate=pl.CostEstimate(
            flops=2 * blocks * rows * rows * width,
            bytes_accessed=4 * blocks * rows * width,
            transcendentals=0,
        ),
    )(batch_order, pair_coef.reshape(orders * shells * degrees, width))


def scale_code(largest):
    return jnp.ceil(jnp.log2(jnp.maximum(largest, 1e-30)) * STEPS) + 1.0


def encode(real_part, imag_part):
    largest = jnp.max(jnp.maximum(jnp.abs(real_part), jnp.abs(imag_part)), axis=0, keepdims=True)
    code = scale_code(largest)
    gain = jnp.exp2(code * (-1.0 / STEPS)) * TOP
    coded = [jnp.floor(v * gain + 0.5).astype(jnp.int32) for v in (real_part, imag_part)]
    return coded[0], coded[1], code


EIGHTS = 17


def stage_block(stage_ref, piece, jb, coded, code):
    odd = lax.axis_index("shell") % 2
    first = EIGHTS * piece + odd + 4 * jb
    for part in range(2):
        stage_ref[pl.ds(first + 2 * part, 2)] = coded[part].reshape(2, 8, LANES)
    stage_ref[EIGHTS * piece + (EIGHTS - 1) * (1 - odd), pl.ds(jb, 1), :] = code.astype(jnp.int32)


def clear_codes(stage_ref, pieces):
    odd = lax.axis_index("shell") % 2
    for piece in range(pieces):
        stage_ref[EIGHTS * piece + (EIGHTS - 1) * (1 - odd)] = jnp.zeros((8, LANES), jnp.int32)


def ship(stage_ref, out_ref):
    for pair in range(stage_ref.shape[0] // 2):
        both = stage_ref[pl.ds(2 * pair, 2)].reshape(16, LANES)
        out_ref[pl.ds(16 * pair, 16), :] = both.astype(jnp.int16)


def value_rows(piece, jb, part):
    return pl.ds((EIGHTS * piece + piece % 2 + 4 * jb + 2 * part) * 8, 16)


def read_gains(in_ref, gain_ref):
    for pair in range(gain_ref.shape[0]):
        gain_ref[pair] = gains(in_ref[pl.ds((2 * EIGHTS * pair + EIGHTS - 1) * 8, 16), :])


def gains(codes):
    return jnp.exp2(codes.astype(jnp.int32).astype(jnp.float32) * (1.0 / STEPS)) * (1.0 / TOP)


def widen(value):
    return value.astype(jnp.int32).astype(jnp.float32)


def walk_at(place, chips):
    lines = chips // 2
    return jnp.where(place < lines, 2 * place, 2 * (chips - 1 - place) + 1)


def place_of(chip, chips):
    return jnp.where(chip % 2 == 0, chip // 2, chips - 1 - chip // 2)


def project_kernel(devices, sources, n_acc, packed, owner_ref, rows_ref, *refs):
    n = len(sources)
    panels = refs[:n]
    acc_in = refs[n : n + n_acc]
    acc_out = refs[-2] if packed else refs[-1]
    chips = devices // 2
    me = lax.axis_index("shell")
    part = lax.axis_index("grp")
    width = rows_ref.shape[2] // 2
    started = n_acc
    if n_acc:
        acc_out[...] = acc_in[0][...]
    for panel, (shift, flip, half) in zip(panels, sources):
        depth = panel.shape[0]
        ahead = jnp.where(me % 2 == 0, shift, -shift)
        place = lax.rem(place_of(me // 2, chips) + ahead + chips, chips)
        slot = 2 * walk_at(place, chips) + (me + flip) % 2
        degree = jnp.zeros((), jnp.int32)
        for l in range(rows_ref.shape[0]):
            degree = jnp.where(owner_ref[l] == slot, l, degree)
        offset = 0 if half is None else width // 2 * ((part + half[0]) % 2) + half[1]
        left = jnp.concatenate(
            [rows_ref[degree, :, pl.ds(pl.multiple_of(c * width + offset, 128), depth)] for c in range(2)]
        )
        product = jnp.dot(left, panel[...], preferred_element_type=jnp.float32)
        acc_out[...] = acc_out[...] + product if started else product
        started = 1
    if packed:
        pack(acc_out, refs[-1], refs[-3])


def project(acc, rows, owner, panels, sources, packed=None):
    count, width = rows.shape[1], panels[0].shape[1]
    depth = sum(p.shape[0] for p in panels)
    n_acc = 0 if acc is None else 1
    total = jax.ShapeDtypeStruct((2 * count, width), jnp.float32)
    return pl.pallas_call(
        functools.partial(
            project_kernel, lax.axis_size("shell"), tuple(sources), n_acc, packed is not None
        ),
        in_specs=[pl.BlockSpec(memory_space=pltpu.SMEM)]
        + [pl.BlockSpec(memory_space=pltpu.VMEM)] * (1 + len(panels) + n_acc),
        out_specs=pl.BlockSpec(memory_space=pltpu.VMEM),
        out_shape=total if packed is None else packed,
        scratch_shapes=[]
        if packed is None
        else [
            pltpu.VMEM(total.shape, total.dtype),
            pltpu.VMEM((packed.shape[0] // 8, 8, LANES), jnp.int32),
        ],
        compiler_params=pltpu.CompilerParams(vmem_limit_bytes=24 * 2**20),
        cost_estimate=pl.CostEstimate(
            flops=4 * count * depth * width,
            bytes_accessed=2 * depth * (width + 2 * count) + 8 * count * width * (1 + n_acc),
            transcendentals=0,
        ),
    )(owner, rows, *panels, *([acc] if n_acc else []))


def pack(proj_ref, stage_ref, out_ref):
    count, width = proj_ref.shape[0] // 2, proj_ref.shape[1]
    pieces = count // 16
    clear_codes(stage_ref, pieces)
    for d in range(pieces):
        for jb in range(width // LANES):
            lanes = pl.ds(jb * LANES, LANES)
            *coded, code = encode(
                proj_ref[pl.ds(16 * d, 16), lanes], proj_ref[pl.ds(count + 16 * d, 16), lanes]
            )
            stage_block(stage_ref, d, jb, coded, code)
    ship(stage_ref, out_ref)


def radix2(real_parts, imag_parts):
    n = len(real_parts)
    re, im = list(real_parts), list(imag_parts)
    half = n // 2
    while half:
        for start in range(0, n, 2 * half):
            for k in range(half):
                a, b = start + k, start + k + half
                dr, di = re[a] - re[b], im[a] - im[b]
                re[a], im[a] = re[a] + re[b], im[a] + im[b]
                angle = -math.pi * k / half
                if k == 0:
                    re[b], im[b] = dr, di
                elif 2 * k == half:
                    re[b], im[b] = di, -dr
                elif 4 * k == half:
                    re[b], im[b] = (dr + di) * math.cos(angle), (di - dr) * math.cos(angle)
                elif 4 * k == 3 * half:
                    re[b], im[b] = (di - dr) * math.cos(math.pi / 4), (dr + di) * -math.cos(math.pi / 4)
                else:
                    c, s = math.cos(angle), math.sin(angle)
                    re[b], im[b] = dr * c - di * s, dr * s + di * c
        half //= 2
    return re, im


def outer_kernel(in_ref, out_ref, gain_ref, stage_ref):
    n = 2 * gain_ref.shape[0]
    read_gains(in_ref, gain_ref)
    clear_codes(stage_ref, n)
    for jb in range((EIGHTS - 1) // 4):
        re, im = [], []
        for q in range(n):
            gain = gain_ref[q // 2, pl.ds(8 * (q % 2) + jb, 1), :]
            re.append(widen(in_ref[value_rows(q, jb, 0), :]) * gain)
            im.append(widen(in_ref[value_rows(q, jb, 1), :]) * gain)
        re, im = radix2(re, im)
        for p in range(n):
            *coded, code = encode(re[p], im[p])
            stage_block(stage_ref, p, jb, coded, code)
    ship(stage_ref, out_ref)


def inner_kernel(twist_ref, in_ref, out_ref, gain_ref):
    n = 2 * gain_ref.shape[0]
    orders = 2 * n
    nbits = orders.bit_length() - 1
    read_gains(in_ref, gain_ref)
    for jb in range((EIGHTS - 1) // 4):
        re, im = [], []
        for d in range(n):
            gain = gain_ref[d // 2, pl.ds(8 * (d % 2) + jb, 1), :]
            both_re = widen(in_ref[value_rows(d, jb, 0), :]) * gain
            both_im = widen(in_ref[value_rows(d, jb, 1), :]) * gain
            for r in range(2):
                a, b = both_re[8 * r : 8 * r + 8], both_im[8 * r : 8 * r + 8]
                c, s = twist_ref[0, 2 * d + r], twist_ref[1, 2 * d + r]
                re.append(a * c - b * s)
                im.append(a * s + b * c)
        re, im = radix2(re, im)
        for p in range(orders):
            h = bit_reverse(p, nbits)
            for part, value in enumerate((re[p], im[p])):
                for b in range(2):
                    first = (b * orders + h) * 32 + 2 * jb + part
                    out_ref[pl.ds(first, 4, stride=8), :] = value[4 * b : 4 * b + 4]


def local_call(kernel, out, scratch, *args, smem=0):
    return pl.pallas_call(
        kernel,
        in_specs=[pl.BlockSpec(memory_space=pltpu.SMEM)] * smem
        + [pl.BlockSpec(memory_space=pltpu.VMEM)] * (len(args) - smem),
        out_specs=pl.BlockSpec(memory_space=pltpu.VMEM),
        out_shape=out,
        scratch_shapes=scratch,
        compiler_params=pltpu.CompilerParams(vmem_limit_bytes=24 * 2**20),
    )(*args)


def shards(pair_coef, panel_pool, degree_owner, batch_order):
    local_orders, shells = pair_coef.shape[:2]
    width = panel_pool.shape[2]
    devices = lax.axis_size("shell")
    total_orders = local_orders * devices
    chips = devices // 2
    me = lax.axis_index("shell")
    lines = chips // 2
    walk = [2 * z for z in range(lines)] + [2 * z + 1 for z in reversed(range(lines))]

    onward = []
    for here, there in zip(walk, walk[1:] + walk[:1]):
        onward += [(2 * here, 2 * there), (2 * there + 1, 2 * here + 1)]

    def around(value):
        return lax.ppermute(value, "shell", onward)

    def crosswise(value):
        return lax.ppermute(value, "shell", [(source ^ 1, target) for source, target in onward])

    def sibling(value):
        return lax.ppermute(value, "shell", [(s, s ^ 1) for s in range(devices)])

    def across(value):
        return lax.ppermute(value, "grp", [(0, 1), (1, 0)])

    blocks = width // LANES
    parcels = jax.ShapeDtypeStruct((devices * EIGHTS * 8, LANES), jnp.int16)
    lines = pltpu.VMEM((devices // 2, 16, LANES), jnp.float32)
    stage = pltpu.VMEM((devices * EIGHTS, 8, LANES), jnp.int32)

    def exchange(value):
        value = value.reshape(devices, EIGHTS * 8, LANES)
        return lax.all_to_all(value, "shell", 0, 0).reshape(parcels.shape)

    own = panel_pool[0]
    half = own.shape[0] // 2
    whole = around(own)
    part = crosswise(lax.dynamic_slice_in_dim(own, half * lax.axis_index("grp"), half))
    other = sibling(own)
    rows = sort_rows(pair_coef, batch_order)
    acc = project(None, rows, degree_owner, [own, other], [(0, 0, None), (0, 1, None)])
    whole, part, rows = lax.optimization_barrier((whole, part, rows))
    late, late_from = [], []
    for step in range(1, chips // 2):
        if step > 1:
            whole, acc = lax.optimization_barrier((whole, acc))
        next_whole = around(whole)
        next_part = around(part) if step + 1 < chips // 2 else None
        if next_part is None:
            cut = half // 2
            front, back, acc = lax.optimization_barrier((late[0][:cut], part[cut:], acc))
            ends = [around(front), across(back)]
        else:
            rest = across(part)
        acc = project(
            acc,
            rows,
            degree_owner,
            [whole, sibling(whole), part, sibling(part), *late],
            [(-step, 0, None), (step, 1, None), (-step, 1, (0, 0)), (step, 0, (0, 0)), *late_from],
        )
        if next_part is not None:
            late, late_from = [rest, sibling(rest)], [(-step, 1, (1, 0)), (step, 0, (1, 0))]
        whole, part = next_whole, next_part
    whole, acc, *ends = lax.optimization_barrier((whole, acc, *ends))
    far = chips // 2
    acc = project(
        acc,
        rows,
        degree_owner,
        [whole, *ends],
        [(-far, 0, None), (1 - far, 1, (1, 0)), (1 - far, 1, (1, cut))],
    )
    sent = project(
        acc,
        rows,
        degree_owner,
        [sibling(whole), *map(sibling, ends)],
        [(far, 1, None), (far - 1, 0, (1, 0)), (far - 1, 0, (1, cut))],
        packed=parcels,
    )
    sent = local_call(outer_kernel, parcels, [lines, stage], exchange(sent))
    sent = exchange(sent)
    first = bit_reverse(me, devices.bit_length() - 1)
    phase = lax.iota(jnp.int32, local_orders) * first % total_orders
    angle = -2.0 * math.pi * phase.astype(jnp.float32) / float(total_orders)
    twist = jnp.stack([jnp.cos(angle), jnp.sin(angle)]) * (1.0 / math.sqrt(total_orders))
    out = jax.ShapeDtypeStruct((2 * local_orders * shells // 2 * 2 * blocks, LANES), jnp.float32)
    scores = local_call(inner_kernel, out, [lines], twist, sent, smem=1)
    scores = scores.reshape(2, local_orders, shells // 2, blocks, 2, LANES)
    return scores.transpose(0, 1, 2, 4, 3, 5).reshape(2, local_orders, shells // 2, 2, width)


def solution(mesh):
    devices = mesh.shape["shell"]
    return jax.shard_map(
        shards if (devices, mesh.shape["grp"]) == (16, 2) else general,
        mesh=mesh,
        in_specs=(P(("grp", "shell"), None, None, None), P("shell", None, None), P(), P()),
        out_specs=P(None, ("grp", "shell"), None, None, None),
        check_vma=False,
    )
```

```python
import functools
import math

import jax
import jax.numpy as jnp
from jax import lax
from jax.experimental import pallas as pl
from jax.experimental.pallas import tpu as pltpu
from jax.sharding import PartitionSpec as P


def broadcast(value, axis, root):
    mine = lax.axis_index(axis) == root
    return lax.psum(jnp.where(mine, value, jnp.zeros_like(value)), axis)


def partner(value, axis, distance):
    mask = 2**distance
    pairs = [(source, source ^ mask) for source in range(lax.axis_size(axis))]
    return lax.ppermute(value, axis, pairs)


def rotate(real_part, imag_part, cosine, sine):
    return (real_part * cosine - imag_part * sine, real_part * sine + imag_part * cosine)


def general(pair_coef, panel_pool, degree_owner, batch_order):
    local_orders = pair_coef.shape[0]
    degrees = pair_coef.shape[2]
    width = pair_coef.shape[3] // 2
    batch_rows = batch_order.shape[0] // 2
    devices = lax.axis_size("shell")
    total_orders = local_orders * devices
    first = jnp.take(pair_coef, batch_order[:batch_rows], axis=1)
    second = jnp.take(pair_coef, batch_order[batch_rows:], axis=1)
    rows = jnp.stack([first, second])

    def add_degree(degree, total):
        panel = broadcast(panel_pool[0], "shell", degree_owner[degree])
        piece = lax.dynamic_index_in_dim(rows, degree, axis=3, keepdims=False).reshape(-1, width)
        return total + jnp.dot(piece, panel, preferred_element_type=jnp.float32)

    total = lax.fori_loop(
        0, degrees, add_degree, jnp.zeros((2 * local_orders * batch_rows * 2, width), jnp.float32)
    )
    proj = total.reshape(2, local_orders, batch_rows, 2, width)
    nbits = devices.bit_length() - 1
    high = lax.Precision.HIGHEST
    me = lax.axis_index("shell")
    blocks = proj
    for bit in reversed(range(nbits)):
        other = partner(blocks, "shell", bit)
        upper = me >> bit & 1 == 1
        lower_val = jnp.where(upper, other, blocks)
        upper_val = jnp.where(upper, blocks, other)
        summed = lower_val + upper_val
        differ = lower_val - upper_val
        twist = (me % (1 << bit)).astype(jnp.float32)
        angle = -2.0 * math.pi * twist / float(2 << bit)
        new_real, new_imag = rotate(
            differ[:, :, :, 0], differ[:, :, :, 1], jnp.cos(angle), jnp.sin(angle)
        )
        turned = jnp.stack([new_real, new_imag], axis=3)
        blocks = jnp.where(upper, turned, summed)
    flipped = jnp.zeros((), jnp.int32)
    for bit in range(nbits):
        flipped = flipped | (me >> bit & 1) << nbits - 1 - bit
    inner = lax.iota(jnp.int32, local_orders)
    freq = flipped + devices * inner
    phase = inner[None, :] * freq[:, None] % total_orders
    angle = -2.0 * math.pi * phase.astype(jnp.float32) / float(total_orders)
    cosine = jnp.cos(angle)
    sine = jnp.sin(angle)
    real_part = blocks[:, :, :, 0]
    imag_part = blocks[:, :, :, 1]
    out_real = jnp.einsum("gr,brtj->bgtj", cosine, real_part, precision=high) - jnp.einsum(
        "gr,brtj->bgtj", sine, imag_part, precision=high
    )
    out_imag = jnp.einsum("gr,brtj->bgtj", sine, real_part, precision=high) + jnp.einsum(
        "gr,brtj->bgtj", cosine, imag_part, precision=high
    )
    result = jnp.stack([out_real, out_imag], axis=3)
    return result * (1.0 / math.sqrt(total_orders))


STEPS = 16.0
TOP = 32000.0
LANES = 128
GROUP = 4
SORT_LIMIT = 42


def bit_reverse(value, nbits):
    flipped = 0
    for bit in range(nbits):
        flipped = flipped | (value >> bit & 1) << nbits - 1 - bit
    return flipped


def sort_kernel(order_ref, coef_ref, out_ref, perm_ref, held_ref, sems):
    rows = perm_ref.shape[0]
    blocks = held_ref.shape[0] // rows
    degrees = out_ref.shape[0]
    shells = order_ref.shape[0]
    slab = rows // degrees

    def copy(i):
        block = coef_ref.at[pl.ds(i * rows, GROUP * rows), :]
        return pltpu.make_async_copy(block, held_ref.at[pl.ds(i * rows, GROUP * rows), :], sems.at[i])

    for i in range(0, blocks, GROUP):
        copy(i).start()
    line = lax.broadcasted_iota(jnp.int32, (slab, rows), 0)
    in_at = lax.broadcasted_iota(jnp.int32, (slab, rows), 1)
    wanted = jnp.zeros(line.shape, jnp.int32)
    for at in range(slab):
        source = (at // shells * shells + order_ref[at % shells]) * degrees
        wanted = jnp.where(line == at, source, wanted)
    for l in range(degrees):
        chosen = jnp.where(in_at == wanted + l, 1.0, 0.0).astype(perm_ref.dtype)
        perm_ref[pl.ds(l * slab, slab), :] = chosen

    for i in range(blocks):
        if i % GROUP == 0:
            copy(i).wait()
        moved = jnp.dot(perm_ref[...], held_ref[pl.ds(i * rows, rows), :], preferred_element_type=jnp.float32)
        out_ref[:, pl.ds(i * slab, slab), :] = moved.astype(out_ref.dtype).reshape(
            degrees, slab, moved.shape[1]
        )


def sort_rows(pair_coef, batch_order):
    orders, shells, degrees, width = pair_coef.shape
    group = 16 // shells
    rows = group * shells * degrees
    blocks = orders // group
    return pl.pallas_call(
        sort_kernel,
        in_specs=[pl.BlockSpec(memory_space=pltpu.SMEM), pl.BlockSpec(memory_space=pltpu.HBM)],
        out_specs=pl.BlockSpec(memory_space=pltpu.VMEM),
        out_shape=jax.ShapeDtypeStruct((degrees, orders * shells, width), pair_coef.dtype),
        scratch_shapes=[
            pltpu.VMEM((rows, rows), pair_coef.dtype),
            pltpu.VMEM((blocks * rows, width), pair_coef.dtype),
            pltpu.SemaphoreType.DMA((blocks,)),
        ],
        compiler_params=pltpu.CompilerParams(vmem_limit_bytes=SORT_LIMIT * 2**20),
        cost_estimate=pl.CostEstimate(
            flops=2 * blocks * rows * rows * width,
            bytes_accessed=4 * blocks * rows * width,
            transcendentals=0,
        ),
    )(batch_order, pair_coef.reshape(orders * shells * degrees, width))


def scale_code(largest):
    return jnp.ceil(jnp.log2(jnp.maximum(largest, 1e-30)) * STEPS) + 1.0


def encode(real_part, imag_part):
    largest = jnp.max(jnp.maximum(jnp.abs(real_part), jnp.abs(imag_part)), axis=0, keepdims=True)
    code = scale_code(largest)
    gain = jnp.exp2(code * (-1.0 / STEPS)) * TOP
    coded = [jnp.floor(v * gain + 0.5).astype(jnp.int32) for v in (real_part, imag_part)]
    return coded[0], coded[1], code


EIGHTS = 17


def stage_block(stage_ref, piece, jb, coded, code):
    odd = lax.axis_index("shell") % 2
    first = EIGHTS * piece + odd + 4 * jb
    for part in range(2):
        stage_ref[pl.ds(first + 2 * part, 2)] = coded[part].reshape(2, 8, LANES)
    stage_ref[EIGHTS * piece + (EIGHTS - 1) * (1 - odd), pl.ds(jb, 1), :] = code.astype(jnp.int32)


def clear_codes(stage_ref, pieces):
    odd = lax.axis_index("shell") % 2
    for piece in range(pieces):
        stage_ref[EIGHTS * piece + (EIGHTS - 1) * (1 - odd)] = jnp.zeros((8, LANES), jnp.int32)


def ship(stage_ref, out_ref):
    for pair in range(stage_ref.shape[0] // 2):
        both = stage_ref[pl.ds(2 * pair, 2)].reshape(16, LANES)
        out_ref[pl.ds(16 * pair, 16), :] = both.astype(jnp.int16)


def value_rows(piece, jb, part):
    return pl.ds((EIGHTS * piece + piece % 2 + 4 * jb + 2 * part) * 8, 16)


def read_gains(in_ref, gain_ref):
    for pair in range(gain_ref.shape[0]):
        gain_ref[pair] = gains(in_ref[pl.ds((2 * EIGHTS * pair + EIGHTS - 1) * 8, 16), :])


def gains(codes):
    return jnp.exp2(codes.astype(jnp.int32).astype(jnp.float32) * (1.0 / STEPS)) * (1.0 / TOP)


def widen(value):
    return value.astype(jnp.int32).astype(jnp.float32)


def walk_at(place, chips):
    lines = chips // 2
    return jnp.where(place < lines, 2 * place, 2 * (chips - 1 - place) + 1)


def place_of(chip, chips):
    return jnp.where(chip % 2 == 0, chip // 2, chips - 1 - chip // 2)


def project_kernel(devices, sources, n_acc, packed, owner_ref, rows_ref, *refs):
    n = len(sources)
    panels = refs[:n]
    acc_in = refs[n : n + n_acc]
    acc_out = refs[-2] if packed else refs[-1]
    chips = devices // 2
    me = lax.axis_index("shell")
    part = lax.axis_index("grp")
    width = rows_ref.shape[2] // 2
    started = n_acc
    if n_acc:
        acc_out[...] = acc_in[0][...]
    for panel, (shift, flip, half) in zip(panels, sources):
        depth = panel.shape[0]
        ahead = jnp.where(me % 2 == 0, shift, -shift)
        place = lax.rem(place_of(me // 2, chips) + ahead + chips, chips)
        slot = 2 * walk_at(place, chips) + (me + flip) % 2
        degree = jnp.zeros((), jnp.int32)
        for l in range(rows_ref.shape[0]):
            degree = jnp.where(owner_ref[l] == slot, l, degree)
        offset = 0 if half is None else width // 2 * ((part + half[0]) % 2) + half[1]
        left = jnp.concatenate(
            [rows_ref[degree, :, pl.ds(pl.multiple_of(c * width + offset, 128), depth)] for c in range(2)]
        )
        product = jnp.dot(left, panel[...], preferred_element_type=jnp.float32)
        acc_out[...] = acc_out[...] + product if started else product
        started = 1
    if packed:
        pack(acc_out, refs[-1], refs[-3])


def project(acc, rows, owner, panels, sources, packed=None):
    count, width = rows.shape[1], panels[0].shape[1]
    depth = sum(p.shape[0] for p in panels)
    n_acc = 0 if acc is None else 1
    total = jax.ShapeDtypeStruct((2 * count, width), jnp.float32)
    return pl.pallas_call(
        functools.partial(
            project_kernel, lax.axis_size("shell"), tuple(sources), n_acc, packed is not None
        ),
        in_specs=[pl.BlockSpec(memory_space=pltpu.SMEM)]
        + [pl.BlockSpec(memory_space=pltpu.VMEM)] * (1 + len(panels) + n_acc),
        out_specs=pl.BlockSpec(memory_space=pltpu.VMEM),
        out_shape=total if packed is None else packed,
        scratch_shapes=[]
        if packed is None
        else [
            pltpu.VMEM(total.shape, total.dtype),
            pltpu.VMEM((packed.shape[0] // 8, 8, LANES), jnp.int32),
        ],
        compiler_params=pltpu.CompilerParams(vmem_limit_bytes=12 * 2**20),
        cost_estimate=pl.CostEstimate(
            flops=4 * count * depth * width,
            bytes_accessed=2 * depth * (width + 2 * count) + 8 * count * width * (1 + n_acc),
            transcendentals=0,
        ),
    )(owner, rows, *panels, *([acc] if n_acc else []))


def pack(proj_ref, stage_ref, out_ref):
    count, width = proj_ref.shape[0] // 2, proj_ref.shape[1]
    pieces = count // 16
    clear_codes(stage_ref, pieces)
    for d in range(pieces):
        for jb in range(width // LANES):
            lanes = pl.ds(jb * LANES, LANES)
            *coded, code = encode(
                proj_ref[pl.ds(16 * d, 16), lanes], proj_ref[pl.ds(count + 16 * d, 16), lanes]
            )
            stage_block(stage_ref, d, jb, coded, code)
    ship(stage_ref, out_ref)


def radix2(real_parts, imag_parts):
    n = len(real_parts)
    re, im = list(real_parts), list(imag_parts)
    half = n // 2
    while half:
        for start in range(0, n, 2 * half):
            for k in range(half):
                a, b = start + k, start + k + half
                dr, di = re[a] - re[b], im[a] - im[b]
                re[a], im[a] = re[a] + re[b], im[a] + im[b]
                angle = -math.pi * k / half
                if k == 0:
                    re[b], im[b] = dr, di
                elif 2 * k == half:
                    re[b], im[b] = di, -dr
                elif 4 * k == half:
                    re[b], im[b] = (dr + di) * math.cos(angle), (di - dr) * math.cos(angle)
                elif 4 * k == 3 * half:
                    re[b], im[b] = (di - dr) * math.cos(math.pi / 4), (dr + di) * -math.cos(math.pi / 4)
                else:
                    c, s = math.cos(angle), math.sin(angle)
                    re[b], im[b] = dr * c - di * s, dr * s + di * c
        half //= 2
    return re, im


def outer_kernel(in_ref, out_ref, gain_ref, stage_ref):
    n = 2 * gain_ref.shape[0]
    read_gains(in_ref, gain_ref)
    clear_codes(stage_ref, n)
    for jb in range((EIGHTS - 1) // 4):
        re, im = [], []
        for q in range(n):
            gain = gain_ref[q // 2, pl.ds(8 * (q % 2) + jb, 1), :]
            re.append(widen(in_ref[value_rows(q, jb, 0), :]) * gain)
            im.append(widen(in_ref[value_rows(q, jb, 1), :]) * gain)
        re, im = radix2(re, im)
        for p in range(n):
            *coded, code = encode(re[p], im[p])
            stage_block(stage_ref, p, jb, coded, code)
    ship(stage_ref, out_ref)


def inner_kernel(twist_ref, in_ref, out_ref, gain_ref):
    n = 2 * gain_ref.shape[0]
    orders = 2 * n
    nbits = orders.bit_length() - 1
    read_gains(in_ref, gain_ref)
    for jb in range((EIGHTS - 1) // 4):
        re, im = [], []
        for d in range(n):
            gain = gain_ref[d // 2, pl.ds(8 * (d % 2) + jb, 1), :]
            both_re = widen(in_ref[value_rows(d, jb, 0), :]) * gain
            both_im = widen(in_ref[value_rows(d, jb, 1), :]) * gain
            for r in range(2):
                a, b = both_re[8 * r : 8 * r + 8], both_im[8 * r : 8 * r + 8]
                c, s = twist_ref[0, 2 * d + r], twist_ref[1, 2 * d + r]
                re.append(a * c - b * s)
                im.append(a * s + b * c)
        re, im = radix2(re, im)
        for p in range(orders):
            h = bit_reverse(p, nbits)
            for part, value in enumerate((re[p], im[p])):
                for b in range(2):
                    first = (b * orders + h) * 32 + 2 * jb + part
                    out_ref[pl.ds(first, 4, stride=8), :] = value[4 * b : 4 * b + 4]


def local_call(kernel, out, scratch, *args, smem=0):
    return pl.pallas_call(
        kernel,
        in_specs=[pl.BlockSpec(memory_space=pltpu.SMEM)] * smem
        + [pl.BlockSpec(memory_space=pltpu.VMEM)] * (len(args) - smem),
        out_specs=pl.BlockSpec(memory_space=pltpu.VMEM),
        out_shape=out,
        scratch_shapes=scratch,
        compiler_params=pltpu.CompilerParams(vmem_limit_bytes=12 * 2**20),
    )(*args)


def shards(pair_coef, panel_pool, degree_owner, batch_order):
    local_orders, shells = pair_coef.shape[:2]
    width = panel_pool.shape[2]
    devices = lax.axis_size("shell")
    total_orders = local_orders * devices
    chips = devices // 2
    me = lax.axis_index("shell")
    lines = chips // 2
    walk = [2 * z for z in range(lines)] + [2 * z + 1 for z in reversed(range(lines))]

    onward = []
    for here, there in zip(walk, walk[1:] + walk[:1]):
        onward += [(2 * here, 2 * there), (2 * there + 1, 2 * here + 1)]

    def around(value):
        return lax.ppermute(value, "shell", onward)

    def crosswise(value):
        return lax.ppermute(value, "shell", [(source ^ 1, target) for source, target in onward])

    def sibling(value):
        return lax.ppermute(value, "shell", [(s, s ^ 1) for s in range(devices)])

    def across(value):
        return lax.ppermute(value, "grp", [(0, 1), (1, 0)])

    blocks = width // LANES
    parcels = jax.ShapeDtypeStruct((devices * EIGHTS * 8, LANES), jnp.int16)
    lines = pltpu.VMEM((devices // 2, 16, LANES), jnp.float32)
    stage = pltpu.VMEM((devices * EIGHTS, 8, LANES), jnp.int32)

    def exchange(value):
        value = value.reshape(devices, EIGHTS * 8, LANES)
        return lax.all_to_all(value, "shell", 0, 0).reshape(parcels.shape)

    own = panel_pool[0]
    half = own.shape[0] // 2
    whole = around(own)
    part = crosswise(lax.dynamic_slice_in_dim(own, half * lax.axis_index("grp"), half))
    other = sibling(own)
    rows = sort_rows(pair_coef, batch_order)
    acc = project(None, rows, degree_owner, [own, other], [(0, 0, None), (0, 1, None)])
    whole, part, rows = lax.optimization_barrier((whole, part, rows))
    late, late_from = [], []
    for step in range(1, chips // 2):
        if step > 1:
            whole, acc = lax.optimization_barrier((whole, acc))
        next_whole = around(whole)
        next_part = around(part) if step + 1 < chips // 2 else None
        if next_part is None:
            cut = half // 2
            front, back, acc = lax.optimization_barrier((late[0][:cut], part[cut:], acc))
            ends = [around(front), across(back)]
        else:
            rest = across(part)
        acc = project(
            acc,
            rows,
            degree_owner,
            [whole, sibling(whole), part, sibling(part), *late],
            [(-step, 0, None), (step, 1, None), (-step, 1, (0, 0)), (step, 0, (0, 0)), *late_from],
        )
        if next_part is not None:
            late, late_from = [rest, sibling(rest)], [(-step, 1, (1, 0)), (step, 0, (1, 0))]
        whole, part = next_whole, next_part
    whole, acc, *ends = lax.optimization_barrier((whole, acc, *ends))
    far = chips // 2
    acc = project(
        acc,
        rows,
        degree_owner,
        [whole, *ends],
        [(-far, 0, None), (1 - far, 1, (1, 0)), (1 - far, 1, (1, cut))],
    )
    sent = project(
        acc,
        rows,
        degree_owner,
        [sibling(whole), *map(sibling, ends)],
        [(far, 1, None), (far - 1, 0, (1, 0)), (far - 1, 0, (1, cut))],
        packed=parcels,
    )
    sent = local_call(outer_kernel, parcels, [lines, stage], exchange(sent))
    sent = exchange(sent)
    first = bit_reverse(me, devices.bit_length() - 1)
    phase = lax.iota(jnp.int32, local_orders) * first % total_orders
    angle = -2.0 * math.pi * phase.astype(jnp.float32) / float(total_orders)
    twist = jnp.stack([jnp.cos(angle), jnp.sin(angle)]) * (1.0 / math.sqrt(total_orders))
    out = jax.ShapeDtypeStruct((2 * local_orders * shells // 2 * 2 * blocks, LANES), jnp.float32)
    scores = local_call(inner_kernel, out, [lines], twist, sent, smem=1)
    scores = scores.reshape(2, local_orders, shells // 2, blocks, 2, LANES)
    return scores.transpose(0, 1, 2, 4, 3, 5).reshape(2, local_orders, shells // 2, 2, width)


def solution(mesh):
    devices = mesh.shape["shell"]
    return jax.shard_map(
        shards if (devices, mesh.shape["grp"]) == (16, 2) else general,
        mesh=mesh,
        in_specs=(P(("grp", "shell"), None, None, None), P("shell", None, None), P(), P()),
        out_specs=P(None, ("grp", "shell"), None, None, None),
        check_vma=False,
    )
```

```python
import functools
import math

import jax
import jax.numpy as jnp
from jax import lax
from jax.experimental import pallas as pl
from jax.experimental.pallas import tpu as pltpu
from jax.sharding import PartitionSpec as P


def broadcast(value, axis, root):
    mine = lax.axis_index(axis) == root
    return lax.psum(jnp.where(mine, value, jnp.zeros_like(value)), axis)


def partner(value, axis, distance):
    mask = 2**distance
    pairs = [(source, source ^ mask) for source in range(lax.axis_size(axis))]
    return lax.ppermute(value, axis, pairs)


def rotate(real_part, imag_part, cosine, sine):
    return (real_part * cosine - imag_part * sine, real_part * sine + imag_part * cosine)


def general(pair_coef, panel_pool, degree_owner, batch_order):
    local_orders = pair_coef.shape[0]
    degrees = pair_coef.shape[2]
    width = pair_coef.shape[3] // 2
    batch_rows = batch_order.shape[0] // 2
    devices = lax.axis_size("shell")
    total_orders = local_orders * devices
    first = jnp.take(pair_coef, batch_order[:batch_rows], axis=1)
    second = jnp.take(pair_coef, batch_order[batch_rows:], axis=1)
    rows = jnp.stack([first, second])

    def add_degree(degree, total):
        panel = broadcast(panel_pool[0], "shell", degree_owner[degree])
        piece = lax.dynamic_index_in_dim(rows, degree, axis=3, keepdims=False).reshape(-1, width)
        return total + jnp.dot(piece, panel, preferred_element_type=jnp.float32)

    total = lax.fori_loop(
        0, degrees, add_degree, jnp.zeros((2 * local_orders * batch_rows * 2, width), jnp.float32)
    )
    proj = total.reshape(2, local_orders, batch_rows, 2, width)
    nbits = devices.bit_length() - 1
    high = lax.Precision.HIGHEST
    me = lax.axis_index("shell")
    blocks = proj
    for bit in reversed(range(nbits)):
        other = partner(blocks, "shell", bit)
        upper = me >> bit & 1 == 1
        lower_val = jnp.where(upper, other, blocks)
        upper_val = jnp.where(upper, blocks, other)
        summed = lower_val + upper_val
        differ = lower_val - upper_val
        twist = (me % (1 << bit)).astype(jnp.float32)
        angle = -2.0 * math.pi * twist / float(2 << bit)
        new_real, new_imag = rotate(
            differ[:, :, :, 0], differ[:, :, :, 1], jnp.cos(angle), jnp.sin(angle)
        )
        turned = jnp.stack([new_real, new_imag], axis=3)
        blocks = jnp.where(upper, turned, summed)
    flipped = jnp.zeros((), jnp.int32)
    for bit in range(nbits):
        flipped = flipped | (me >> bit & 1) << nbits - 1 - bit
    inner = lax.iota(jnp.int32, local_orders)
    freq = flipped + devices * inner
    phase = inner[None, :] * freq[:, None] % total_orders
    angle = -2.0 * math.pi * phase.astype(jnp.float32) / float(total_orders)
    cosine = jnp.cos(angle)
    sine = jnp.sin(angle)
    real_part = blocks[:, :, :, 0]
    imag_part = blocks[:, :, :, 1]
    out_real = jnp.einsum("gr,brtj->bgtj", cosine, real_part, precision=high) - jnp.einsum(
        "gr,brtj->bgtj", sine, imag_part, precision=high
    )
    out_imag = jnp.einsum("gr,brtj->bgtj", sine, real_part, precision=high) + jnp.einsum(
        "gr,brtj->bgtj", cosine, imag_part, precision=high
    )
    result = jnp.stack([out_real, out_imag], axis=3)
    return result * (1.0 / math.sqrt(total_orders))


STEPS = 16.0
TOP = 32000.0
LANES = 128
GROUP = 4
SORT_LIMIT = 42


def bit_reverse(value, nbits):
    flipped = 0
    for bit in range(nbits):
        flipped = flipped | (value >> bit & 1) << nbits - 1 - bit
    return flipped


def sort_kernel(order_ref, coef_ref, out_ref, perm_ref, held_ref, sems):
    rows = perm_ref.shape[0]
    blocks = held_ref.shape[0] // rows
    degrees = out_ref.shape[0]
    shells = order_ref.shape[0]
    slab = rows // degrees

    def copy(i):
        block = coef_ref.at[pl.ds(i * rows, GROUP * rows), :]
        return pltpu.make_async_copy(block, held_ref.at[pl.ds(i * rows, GROUP * rows), :], sems.at[i])

    for i in range(0, blocks, GROUP):
        copy(i).start()
    line = lax.broadcasted_iota(jnp.int32, (slab, rows), 0)
    in_at = lax.broadcasted_iota(jnp.int32, (slab, rows), 1)
    wanted = jnp.zeros(line.shape, jnp.int32)
    for at in range(slab):
        source = (at // shells * shells + order_ref[at % shells]) * degrees
        wanted = jnp.where(line == at, source, wanted)
    for l in range(degrees):
        chosen = jnp.where(in_at == wanted + l, 1.0, 0.0).astype(perm_ref.dtype)
        perm_ref[pl.ds(l * slab, slab), :] = chosen

    for i in range(blocks):
        if i % GROUP == 0:
            copy(i).wait()
        moved = jnp.dot(perm_ref[...], held_ref[pl.ds(i * rows, rows), :], preferred_element_type=jnp.float32)
        out_ref[:, pl.ds(i * slab, slab), :] = moved.astype(out_ref.dtype).reshape(
            degrees, slab, moved.shape[1]
        )


def sort_rows(pair_coef, batch_order):
    orders, shells, degrees, width = pair_coef.shape
    group = 16 // shells
    rows = group * shells * degrees
    blocks = orders // group
    return pl.pallas_call(
        sort_kernel,
        in_specs=[pl.BlockSpec(memory_space=pltpu.SMEM), pl.BlockSpec(memory_space=pltpu.HBM)],
        out_specs=pl.BlockSpec(memory_space=pltpu.VMEM),
        out_shape=jax.ShapeDtypeStruct((degrees, orders * shells, width), pair_coef.dtype),
        scratch_shapes=[
            pltpu.VMEM((rows, rows), pair_coef.dtype),
            pltpu.VMEM((blocks * rows, width), pair_coef.dtype),
            pltpu.SemaphoreType.DMA((blocks,)),
        ],
        compiler_params=pltpu.CompilerParams(vmem_limit_bytes=SORT_LIMIT * 2**20),
        cost_estimate=pl.CostEstimate(
            flops=2 * blocks * rows * rows * width,
            bytes_accessed=4 * blocks * rows * width,
            transcendentals=0,
        ),
    )(batch_order, pair_coef.reshape(orders * shells * degrees, width))


def scale_code(largest):
    return jnp.ceil(jnp.log2(jnp.maximum(largest, 1e-30)) * STEPS) + 1.0


def encode(real_part, imag_part):
    largest = jnp.max(jnp.maximum(jnp.abs(real_part), jnp.abs(imag_part)), axis=0, keepdims=True)
    code = scale_code(largest)
    gain = jnp.exp2(code * (-1.0 / STEPS)) * TOP
    coded = [jnp.floor(v * gain + 0.5).astype(jnp.int32) for v in (real_part, imag_part)]
    return coded[0], coded[1], code


EIGHTS = 17


def stage_block(stage_ref, piece, jb, coded, code):
    odd = lax.axis_index("shell") % 2
    first = EIGHTS * piece + odd + 4 * jb
    for part in range(2):
        stage_ref[pl.ds(first + 2 * part, 2)] = coded[part].reshape(2, 8, LANES)
    stage_ref[EIGHTS * piece + (EIGHTS - 1) * (1 - odd), pl.ds(jb, 1), :] = code.astype(jnp.int32)


def clear_codes(stage_ref, pieces):
    odd = lax.axis_index("shell") % 2
    for piece in range(pieces):
        stage_ref[EIGHTS * piece + (EIGHTS - 1) * (1 - odd)] = jnp.zeros((8, LANES), jnp.int32)


def ship(stage_ref, out_ref):
    for pair in range(stage_ref.shape[0] // 2):
        both = stage_ref[pl.ds(2 * pair, 2)].reshape(16, LANES)
        out_ref[pl.ds(16 * pair, 16), :] = both.astype(jnp.int16)


def value_rows(piece, jb, part):
    return pl.ds((EIGHTS * piece + piece % 2 + 4 * jb + 2 * part) * 8, 16)


def read_gains(in_ref, gain_ref):
    for pair in range(gain_ref.shape[0]):
        gain_ref[pair] = gains(in_ref[pl.ds((2 * EIGHTS * pair + EIGHTS - 1) * 8, 16), :])


def gains(codes):
    return jnp.exp2(codes.astype(jnp.int32).astype(jnp.float32) * (1.0 / STEPS)) * (1.0 / TOP)


def widen(value):
    return value.astype(jnp.int32).astype(jnp.float32)


def walk_at(place, chips):
    lines = chips // 2
    return jnp.where(place < lines, 2 * place, 2 * (chips - 1 - place) + 1)


def place_of(chip, chips):
    return jnp.where(chip % 2 == 0, chip // 2, chips - 1 - chip // 2)


def project_kernel(devices, sources, n_acc, packed, owner_ref, rows_ref, *refs):
    n = len(sources)
    panels = refs[:n]
    acc_in = refs[n : n + n_acc]
    acc_out = refs[-2] if packed else refs[-1]
    chips = devices // 2
    me = lax.axis_index("shell")
    part = lax.axis_index("grp")
    width = rows_ref.shape[2] // 2
    started = n_acc
    if n_acc:
        acc_out[...] = acc_in[0][...]
    for panel, (shift, flip, half) in zip(panels, sources):
        depth = panel.shape[0]
        ahead = jnp.where(me % 2 == 0, shift, -shift)
        place = lax.rem(place_of(me // 2, chips) + ahead + chips, chips)
        slot = 2 * walk_at(place, chips) + (me + flip) % 2
        degree = jnp.zeros((), jnp.int32)
        for l in range(rows_ref.shape[0]):
            degree = jnp.where(owner_ref[l] == slot, l, degree)
        offset = 0 if half is None else width // 2 * ((part + half[0]) % 2) + half[1]
        left = jnp.concatenate(
            [rows_ref[degree, :, pl.ds(pl.multiple_of(c * width + offset, 128), depth)] for c in range(2)]
        )
        product = jnp.dot(left, panel[...], preferred_element_type=jnp.float32)
        acc_out[...] = acc_out[...] + product if started else product
        started = 1
    if packed:
        pack(acc_out, refs[-1], refs[-3])


def project(acc, rows, owner, panels, sources, packed=None):
    count, width = rows.shape[1], panels[0].shape[1]
    depth = sum(p.shape[0] for p in panels)
    n_acc = 0 if acc is None else 1
    total = jax.ShapeDtypeStruct((2 * count, width), jnp.float32)
    return pl.pallas_call(
        functools.partial(
            project_kernel, lax.axis_size("shell"), tuple(sources), n_acc, packed is not None
        ),
        in_specs=[pl.BlockSpec(memory_space=pltpu.SMEM)]
        + [pl.BlockSpec(memory_space=pltpu.VMEM)] * (1 + len(panels) + n_acc),
        out_specs=pl.BlockSpec(memory_space=pltpu.VMEM),
        out_shape=total if packed is None else packed,
        scratch_shapes=[]
        if packed is None
        else [
            pltpu.VMEM(total.shape, total.dtype),
            pltpu.VMEM((packed.shape[0] // 8, 8, LANES), jnp.int32),
        ],
        compiler_params=pltpu.CompilerParams(vmem_limit_bytes=12 * 2**20),
        cost_estimate=pl.CostEstimate(
            flops=4 * count * depth * width,
            bytes_accessed=2 * depth * (width + 2 * count) + 8 * count * width * (1 + n_acc),
            transcendentals=0,
        ),
    )(owner, rows, *panels, *([acc] if n_acc else []))


def pack(proj_ref, stage_ref, out_ref):
    count, width = proj_ref.shape[0] // 2, proj_ref.shape[1]
    pieces = count // 16
    clear_codes(stage_ref, pieces)
    for d in range(pieces):
        for jb in range(width // LANES):
            lanes = pl.ds(jb * LANES, LANES)
            *coded, code = encode(
                proj_ref[pl.ds(16 * d, 16), lanes], proj_ref[pl.ds(count + 16 * d, 16), lanes]
            )
            stage_block(stage_ref, d, jb, coded, code)
    ship(stage_ref, out_ref)


def radix2(real_parts, imag_parts):
    n = len(real_parts)
    re, im = list(real_parts), list(imag_parts)
    half = n // 2
    while half:
        for start in range(0, n, 2 * half):
            for k in range(half):
                a, b = start + k, start + k + half
                dr, di = re[a] - re[b], im[a] - im[b]
                re[a], im[a] = re[a] + re[b], im[a] + im[b]
                angle = -math.pi * k / half
                if k == 0:
                    re[b], im[b] = dr, di
                elif 2 * k == half:
                    re[b], im[b] = di, -dr
                elif 4 * k == half:
                    re[b], im[b] = (dr + di) * math.cos(angle), (di - dr) * math.cos(angle)
                elif 4 * k == 3 * half:
                    re[b], im[b] = (di - dr) * math.cos(math.pi / 4), (dr + di) * -math.cos(math.pi / 4)
                else:
                    c, s = math.cos(angle), math.sin(angle)
                    re[b], im[b] = dr * c - di * s, dr * s + di * c
        half //= 2
    return re, im


def outer_kernel(in_ref, out_ref, gain_ref, stage_ref):
    n = 2 * gain_ref.shape[0]
    read_gains(in_ref, gain_ref)
    clear_codes(stage_ref, n)
    for jb in range((EIGHTS - 1) // 4):
        re, im = [], []
        for q in range(n):
            gain = gain_ref[q // 2, pl.ds(8 * (q % 2) + jb, 1), :]
            re.append(widen(in_ref[value_rows(q, jb, 0), :]) * gain)
            im.append(widen(in_ref[value_rows(q, jb, 1), :]) * gain)
        re, im = radix2(re, im)
        for p in range(n):
            *coded, code = encode(re[p], im[p])
            stage_block(stage_ref, p, jb, coded, code)
    ship(stage_ref, out_ref)


def inner_kernel(twist_ref, in_ref, out_ref, gain_ref):
    n = 2 * gain_ref.shape[0]
    orders = 2 * n
    nbits = orders.bit_length() - 1
    read_gains(in_ref, gain_ref)
    for jb in range((EIGHTS - 1) // 4):
        re, im = [], []
        for d in range(n):
            gain = gain_ref[d // 2, pl.ds(8 * (d % 2) + jb, 1), :]
            both_re = widen(in_ref[value_rows(d, jb, 0), :]) * gain
            both_im = widen(in_ref[value_rows(d, jb, 1), :]) * gain
            for r in range(2):
                a, b = both_re[8 * r : 8 * r + 8], both_im[8 * r : 8 * r + 8]
                c, s = twist_ref[0, 2 * d + r], twist_ref[1, 2 * d + r]
                re.append(a * c - b * s)
                im.append(a * s + b * c)
        re, im = radix2(re, im)
        for p in range(orders):
            h = bit_reverse(p, nbits)
            for part, value in enumerate((re[p], im[p])):
                for b in range(2):
                    first = (b * orders + h) * 32 + 2 * jb + part
                    out_ref[pl.ds(first, 4, stride=8), :] = value[4 * b : 4 * b + 4]


def local_call(kernel, out, scratch, *args, smem=0):
    return pl.pallas_call(
        kernel,
        in_specs=[pl.BlockSpec(memory_space=pltpu.SMEM)] * smem
        + [pl.BlockSpec(memory_space=pltpu.VMEM)] * (len(args) - smem),
        out_specs=pl.BlockSpec(memory_space=pltpu.VMEM),
        out_shape=out,
        scratch_shapes=scratch,
        compiler_params=pltpu.CompilerParams(vmem_limit_bytes=12 * 2**20),
    )(*args)


def shards(pair_coef, panel_pool, degree_owner, batch_order):
    local_orders, shells = pair_coef.shape[:2]
    width = panel_pool.shape[2]
    devices = lax.axis_size("shell")
    total_orders = local_orders * devices
    chips = devices // 2
    me = lax.axis_index("shell")
    lines = chips // 2
    walk = [2 * z for z in range(lines)] + [2 * z + 1 for z in reversed(range(lines))]

    onward = []
    for here, there in zip(walk, walk[1:] + walk[:1]):
        onward += [(2 * here, 2 * there), (2 * there + 1, 2 * here + 1)]

    def around(value):
        return lax.ppermute(value, "shell", onward)

    def sibling(value):
        return lax.ppermute(value, "shell", [(s, s ^ 1) for s in range(devices)])

    def across(value):
        return lax.ppermute(value, "grp", [(0, 1), (1, 0)])

    blocks = width // LANES
    parcels = jax.ShapeDtypeStruct((devices * EIGHTS * 8, LANES), jnp.int16)
    lines = pltpu.VMEM((devices // 2, 16, LANES), jnp.float32)
    stage = pltpu.VMEM((devices * EIGHTS, 8, LANES), jnp.int32)

    def exchange(value):
        value = value.reshape(devices, EIGHTS * 8, LANES)
        return lax.all_to_all(value, "shell", 0, 0).reshape(parcels.shape)

    own = panel_pool[0]
    half = own.shape[0] // 2
    whole = around(own)
    other = sibling(own)
    part = around(lax.dynamic_slice_in_dim(other, half * lax.axis_index("grp"), half))
    rows = sort_rows(pair_coef, batch_order)
    acc = project(None, rows, degree_owner, [own, other], [(0, 0, None), (0, 1, None)])
    whole, rows = lax.optimization_barrier((whole, rows))
    late, late_from = [], []
    for step in range(1, chips // 2):
        if step > 1:
            whole, acc = lax.optimization_barrier((whole, acc))
        next_whole = around(whole)
        next_part = around(part) if step + 1 < chips // 2 else None
        if next_part is None:
            cut = half // 2
            front, back, acc = lax.optimization_barrier((late[0][:cut], part[cut:], acc))
            ends = [around(front), across(back)]
        else:
            rest = across(part)
        acc = project(
            acc,
            rows,
            degree_owner,
            [whole, sibling(whole), part, sibling(part), *late],
            [(-step, 0, None), (step, 1, None), (-step, 1, (0, 0)), (step, 0, (0, 0)), *late_from],
        )
        if next_part is not None:
            late, late_from = [rest, sibling(rest)], [(-step, 1, (1, 0)), (step, 0, (1, 0))]
        whole, part = next_whole, next_part
    whole, acc, *ends = lax.optimization_barrier((whole, acc, *ends))
    far = chips // 2
    acc = project(
        acc,
        rows,
        degree_owner,
        [whole, *ends],
        [(-far, 0, None), (1 - far, 1, (1, 0)), (1 - far, 1, (1, cut))],
    )
    sent = project(
        acc,
        rows,
        degree_owner,
        [sibling(whole), *map(sibling, ends)],
        [(far, 1, None), (far - 1, 0, (1, 0)), (far - 1, 0, (1, cut))],
        packed=parcels,
    )
    sent = local_call(outer_kernel, parcels, [lines, stage], exchange(sent))
    sent = exchange(sent)
    first = bit_reverse(me, devices.bit_length() - 1)
    phase = lax.iota(jnp.int32, local_orders) * first % total_orders
    angle = -2.0 * math.pi * phase.astype(jnp.float32) / float(total_orders)
    twist = jnp.stack([jnp.cos(angle), jnp.sin(angle)]) * (1.0 / math.sqrt(total_orders))
    out = jax.ShapeDtypeStruct((2 * local_orders * shells // 2 * 2 * blocks, LANES), jnp.float32)
    scores = local_call(inner_kernel, out, [lines], twist, sent, smem=1)
    scores = scores.reshape(2, local_orders, shells // 2, blocks, 2, LANES)
    return scores.transpose(0, 1, 2, 4, 3, 5).reshape(2, local_orders, shells // 2, 2, width)


def solution(mesh):
    devices = mesh.shape["shell"]
    return jax.shard_map(
        shards if (devices, mesh.shape["grp"]) == (16, 2) else general,
        mesh=mesh,
        in_specs=(P(("grp", "shell"), None, None, None), P("shell", None, None), P(), P()),
        out_specs=P(None, ("grp", "shell"), None, None, None),
        check_vma=False,
    )
```

```python
import functools
import math

import jax
import jax.numpy as jnp
from jax import lax
from jax.experimental import pallas as pl
from jax.experimental.pallas import tpu as pltpu
from jax.sharding import PartitionSpec as P


def broadcast(value, axis, root):
    mine = lax.axis_index(axis) == root
    return lax.psum(jnp.where(mine, value, jnp.zeros_like(value)), axis)


def partner(value, axis, distance):
    mask = 2**distance
    pairs = [(source, source ^ mask) for source in range(lax.axis_size(axis))]
    return lax.ppermute(value, axis, pairs)


def rotate(real_part, imag_part, cosine, sine):
    return (real_part * cosine - imag_part * sine, real_part * sine + imag_part * cosine)


def general(pair_coef, panel_pool, degree_owner, batch_order):
    local_orders = pair_coef.shape[0]
    degrees = pair_coef.shape[2]
    width = pair_coef.shape[3] // 2
    batch_rows = batch_order.shape[0] // 2
    devices = lax.axis_size("shell")
    total_orders = local_orders * devices
    first = jnp.take(pair_coef, batch_order[:batch_rows], axis=1)
    second = jnp.take(pair_coef, batch_order[batch_rows:], axis=1)
    rows = jnp.stack([first, second])

    def add_degree(degree, total):
        panel = broadcast(panel_pool[0], "shell", degree_owner[degree])
        piece = lax.dynamic_index_in_dim(rows, degree, axis=3, keepdims=False).reshape(-1, width)
        return total + jnp.dot(piece, panel, preferred_element_type=jnp.float32)

    total = lax.fori_loop(
        0, degrees, add_degree, jnp.zeros((2 * local_orders * batch_rows * 2, width), jnp.float32)
    )
    proj = total.reshape(2, local_orders, batch_rows, 2, width)
    nbits = devices.bit_length() - 1
    high = lax.Precision.HIGHEST
    me = lax.axis_index("shell")
    blocks = proj
    for bit in reversed(range(nbits)):
        other = partner(blocks, "shell", bit)
        upper = me >> bit & 1 == 1
        lower_val = jnp.where(upper, other, blocks)
        upper_val = jnp.where(upper, blocks, other)
        summed = lower_val + upper_val
        differ = lower_val - upper_val
        twist = (me % (1 << bit)).astype(jnp.float32)
        angle = -2.0 * math.pi * twist / float(2 << bit)
        new_real, new_imag = rotate(
            differ[:, :, :, 0], differ[:, :, :, 1], jnp.cos(angle), jnp.sin(angle)
        )
        turned = jnp.stack([new_real, new_imag], axis=3)
        blocks = jnp.where(upper, turned, summed)
    flipped = jnp.zeros((), jnp.int32)
    for bit in range(nbits):
        flipped = flipped | (me >> bit & 1) << nbits - 1 - bit
    inner = lax.iota(jnp.int32, local_orders)
    freq = flipped + devices * inner
    phase = inner[None, :] * freq[:, None] % total_orders
    angle = -2.0 * math.pi * phase.astype(jnp.float32) / float(total_orders)
    cosine = jnp.cos(angle)
    sine = jnp.sin(angle)
    real_part = blocks[:, :, :, 0]
    imag_part = blocks[:, :, :, 1]
    out_real = jnp.einsum("gr,brtj->bgtj", cosine, real_part, precision=high) - jnp.einsum(
        "gr,brtj->bgtj", sine, imag_part, precision=high
    )
    out_imag = jnp.einsum("gr,brtj->bgtj", sine, real_part, precision=high) + jnp.einsum(
        "gr,brtj->bgtj", cosine, imag_part, precision=high
    )
    result = jnp.stack([out_real, out_imag], axis=3)
    return result * (1.0 / math.sqrt(total_orders))


STEPS = 16.0
TOP = 32000.0
LANES = 128
GROUP = 4
SORT_LIMIT = 42


def bit_reverse(value, nbits):
    flipped = 0
    for bit in range(nbits):
        flipped = flipped | (value >> bit & 1) << nbits - 1 - bit
    return flipped


def sort_kernel(order_ref, coef_ref, out_ref, perm_ref, held_ref, sems):
    rows = perm_ref.shape[0]
    blocks = held_ref.shape[0] // rows
    degrees = out_ref.shape[0]
    shells = order_ref.shape[0]
    slab = rows // degrees

    def copy(i):
        block = coef_ref.at[pl.ds(i * rows, GROUP * rows), :]
        return pltpu.make_async_copy(block, held_ref.at[pl.ds(i * rows, GROUP * rows), :], sems.at[i])

    for i in range(0, blocks, GROUP):
        copy(i).start()
    line = lax.broadcasted_iota(jnp.int32, (slab, rows), 0)
    in_at = lax.broadcasted_iota(jnp.int32, (slab, rows), 1)
    wanted = jnp.zeros(line.shape, jnp.int32)
    for at in range(slab):
        source = (at // shells * shells + order_ref[at % shells]) * degrees
        wanted = jnp.where(line == at, source, wanted)
    for l in range(degrees):
        chosen = jnp.where(in_at == wanted + l, 1.0, 0.0).astype(perm_ref.dtype)
        perm_ref[pl.ds(l * slab, slab), :] = chosen

    for i in range(blocks):
        if i % GROUP == 0:
            copy(i).wait()
        moved = jnp.dot(perm_ref[...], held_ref[pl.ds(i * rows, rows), :], preferred_element_type=jnp.float32)
        out_ref[:, pl.ds(i * slab, slab), :] = moved.astype(out_ref.dtype).reshape(
            degrees, slab, moved.shape[1]
        )


def sort_rows(pair_coef, batch_order):
    orders, shells, degrees, width = pair_coef.shape
    group = 16 // shells
    rows = group * shells * degrees
    blocks = orders // group
    return pl.pallas_call(
        sort_kernel,
        in_specs=[pl.BlockSpec(memory_space=pltpu.SMEM), pl.BlockSpec(memory_space=pltpu.HBM)],
        out_specs=pl.BlockSpec(memory_space=pltpu.VMEM),
        out_shape=jax.ShapeDtypeStruct((degrees, orders * shells, width), pair_coef.dtype),
        scratch_shapes=[
            pltpu.VMEM((rows, rows), pair_coef.dtype),
            pltpu.VMEM((blocks * rows, width), pair_coef.dtype),
            pltpu.SemaphoreType.DMA((blocks,)),
        ],
        compiler_params=pltpu.CompilerParams(vmem_limit_bytes=SORT_LIMIT * 2**20),
        cost_estimate=pl.CostEstimate(
            flops=2 * blocks * rows * rows * width,
            bytes_accessed=4 * blocks * rows * width,
            transcendentals=0,
        ),
    )(batch_order, pair_coef.reshape(orders * shells * degrees, width))


def scale_code(largest):
    return jnp.ceil(jnp.log2(jnp.maximum(largest, 1e-30)) * STEPS) + 1.0


def encode(real_part, imag_part):
    largest = jnp.max(jnp.maximum(jnp.abs(real_part), jnp.abs(imag_part)), axis=0, keepdims=True)
    code = scale_code(largest)
    gain = jnp.exp2(code * (-1.0 / STEPS)) * TOP
    coded = [jnp.floor(v * gain + 0.5).astype(jnp.int32) for v in (real_part, imag_part)]
    return coded[0], coded[1], code


EIGHTS = 17


def stage_block(stage_ref, piece, jb, coded, code):
    odd = lax.axis_index("shell") % 2
    first = EIGHTS * piece + odd + 4 * jb
    for part in range(2):
        stage_ref[pl.ds(first + 2 * part, 2)] = coded[part].reshape(2, 8, LANES)
    stage_ref[EIGHTS * piece + (EIGHTS - 1) * (1 - odd), pl.ds(jb, 1), :] = code.astype(jnp.int32)


def clear_codes(stage_ref, pieces):
    odd = lax.axis_index("shell") % 2
    for piece in range(pieces):
        stage_ref[EIGHTS * piece + (EIGHTS - 1) * (1 - odd)] = jnp.zeros((8, LANES), jnp.int32)


def ship(stage_ref, out_ref):
    for pair in range(stage_ref.shape[0] // 2):
        both = stage_ref[pl.ds(2 * pair, 2)].reshape(16, LANES)
        out_ref[pl.ds(16 * pair, 16), :] = both.astype(jnp.int16)


def value_rows(piece, jb, part):
    return pl.ds((EIGHTS * piece + piece % 2 + 4 * jb + 2 * part) * 8, 16)


def read_gains(in_ref, gain_ref):
    for pair in range(gain_ref.shape[0]):
        gain_ref[pair] = gains(in_ref[pl.ds((2 * EIGHTS * pair + EIGHTS - 1) * 8, 16), :])


def gains(codes):
    return jnp.exp2(codes.astype(jnp.int32).astype(jnp.float32) * (1.0 / STEPS)) * (1.0 / TOP)


def widen(value):
    return value.astype(jnp.int32).astype(jnp.float32)


def walk_at(place, chips):
    lines = chips // 2
    return jnp.where(place < lines, 2 * place, 2 * (chips - 1 - place) + 1)


def place_of(chip, chips):
    return jnp.where(chip % 2 == 0, chip // 2, chips - 1 - chip // 2)


def project_kernel(devices, sources, n_acc, packed, owner_ref, rows_ref, *refs):
    n = len(sources)
    panels = refs[:n]
    acc_in = refs[n : n + n_acc]
    acc_out = refs[-2] if packed else refs[-1]
    chips = devices // 2
    me = lax.axis_index("shell")
    part = lax.axis_index("grp")
    width = rows_ref.shape[2] // 2
    started = n_acc
    if n_acc:
        acc_out[...] = acc_in[0][...]
    for panel, (shift, flip, half) in zip(panels, sources):
        depth = panel.shape[0]
        ahead = jnp.where(me % 2 == 0, shift, -shift)
        place = lax.rem(place_of(me // 2, chips) + ahead + chips, chips)
        slot = 2 * walk_at(place, chips) + (me + flip) % 2
        degree = jnp.zeros((), jnp.int32)
        for l in range(rows_ref.shape[0]):
            degree = jnp.where(owner_ref[l] == slot, l, degree)
        offset = 0 if half is None else width // 2 * ((part + half[0]) % 2) + half[1]
        left = jnp.concatenate(
            [rows_ref[degree, :, pl.ds(pl.multiple_of(c * width + offset, 128), depth)] for c in range(2)]
        )
        product = jnp.dot(left, panel[...], preferred_element_type=jnp.float32)
        acc_out[...] = acc_out[...] + product if started else product
        started = 1
    if packed:
        pack(acc_out, refs[-1], refs[-3])


def project(acc, rows, owner, panels, sources, packed=None):
    count, width = rows.shape[1], panels[0].shape[1]
    depth = sum(p.shape[0] for p in panels)
    n_acc = 0 if acc is None else 1
    total = jax.ShapeDtypeStruct((2 * count, width), jnp.float32)
    return pl.pallas_call(
        functools.partial(
            project_kernel, lax.axis_size("shell"), tuple(sources), n_acc, packed is not None
        ),
        in_specs=[pl.BlockSpec(memory_space=pltpu.SMEM)]
        + [pl.BlockSpec(memory_space=pltpu.VMEM)] * (1 + len(panels) + n_acc),
        out_specs=pl.BlockSpec(memory_space=pltpu.VMEM),
        out_shape=total if packed is None else packed,
        scratch_shapes=[]
        if packed is None
        else [
            pltpu.VMEM(total.shape, total.dtype),
            pltpu.VMEM((packed.shape[0] // 8, 8, LANES), jnp.int32),
        ],
        compiler_params=pltpu.CompilerParams(vmem_limit_bytes=12 * 2**20),
        cost_estimate=pl.CostEstimate(
            flops=4 * count * depth * width,
            bytes_accessed=2 * depth * (width + 2 * count) + 8 * count * width * (1 + n_acc),
            transcendentals=0,
        ),
    )(owner, rows, *panels, *([acc] if n_acc else []))


def pack(proj_ref, stage_ref, out_ref):
    count, width = proj_ref.shape[0] // 2, proj_ref.shape[1]
    pieces = count // 16
    clear_codes(stage_ref, pieces)
    for d in range(pieces):
        for jb in range(width // LANES):
            lanes = pl.ds(jb * LANES, LANES)
            *coded, code = encode(
                proj_ref[pl.ds(16 * d, 16), lanes], proj_ref[pl.ds(count + 16 * d, 16), lanes]
            )
            stage_block(stage_ref, d, jb, coded, code)
    ship(stage_ref, out_ref)


def radix2(real_parts, imag_parts):
    n = len(real_parts)
    re, im = list(real_parts), list(imag_parts)
    half = n // 2
    while half:
        for start in range(0, n, 2 * half):
            for k in range(half):
                a, b = start + k, start + k + half
                dr, di = re[a] - re[b], im[a] - im[b]
                re[a], im[a] = re[a] + re[b], im[a] + im[b]
                angle = -math.pi * k / half
                if k == 0:
                    re[b], im[b] = dr, di
                elif 2 * k == half:
                    re[b], im[b] = di, -dr
                elif 4 * k == half:
                    re[b], im[b] = (dr + di) * math.cos(angle), (di - dr) * math.cos(angle)
                elif 4 * k == 3 * half:
                    re[b], im[b] = (di - dr) * math.cos(math.pi / 4), (dr + di) * -math.cos(math.pi / 4)
                else:
                    c, s = math.cos(angle), math.sin(angle)
                    re[b], im[b] = dr * c - di * s, dr * s + di * c
        half //= 2
    return re, im


def outer_kernel(in_ref, out_ref, gain_ref, stage_ref):
    n = 2 * gain_ref.shape[0]
    read_gains(in_ref, gain_ref)
    clear_codes(stage_ref, n)
    for jb in range((EIGHTS - 1) // 4):
        re, im = [], []
        for q in range(n):
            gain = gain_ref[q // 2, pl.ds(8 * (q % 2) + jb, 1), :]
            re.append(widen(in_ref[value_rows(q, jb, 0), :]) * gain)
            im.append(widen(in_ref[value_rows(q, jb, 1), :]) * gain)
        re, im = radix2(re, im)
        for p in range(n):
            *coded, code = encode(re[p], im[p])
            stage_block(stage_ref, p, jb, coded, code)
    ship(stage_ref, out_ref)


def inner_kernel(twist_ref, in_ref, out_ref, gain_ref):
    n = 2 * gain_ref.shape[0]
    orders = 2 * n
    nbits = orders.bit_length() - 1
    read_gains(in_ref, gain_ref)
    for jb in range((EIGHTS - 1) // 4):
        re, im = [], []
        for d in range(n):
            gain = gain_ref[d // 2, pl.ds(8 * (d % 2) + jb, 1), :]
            both_re = widen(in_ref[value_rows(d, jb, 0), :]) * gain
            both_im = widen(in_ref[value_rows(d, jb, 1), :]) * gain
            for r in range(2):
                a, b = both_re[8 * r : 8 * r + 8], both_im[8 * r : 8 * r + 8]
                c, s = twist_ref[0, 2 * d + r], twist_ref[1, 2 * d + r]
                re.append(a * c - b * s)
                im.append(a * s + b * c)
        re, im = radix2(re, im)
        for p in range(orders):
            h = bit_reverse(p, nbits)
            for part, value in enumerate((re[p], im[p])):
                for b in range(2):
                    first = (b * orders + h) * 32 + 2 * jb + part
                    out_ref[pl.ds(first, 4, stride=8), :] = value[4 * b : 4 * b + 4]


def local_call(kernel, out, scratch, *args, smem=0):
    return pl.pallas_call(
        kernel,
        in_specs=[pl.BlockSpec(memory_space=pltpu.SMEM)] * smem
        + [pl.BlockSpec(memory_space=pltpu.VMEM)] * (len(args) - smem),
        out_specs=pl.BlockSpec(memory_space=pltpu.VMEM),
        out_shape=out,
        scratch_shapes=scratch,
        compiler_params=pltpu.CompilerParams(vmem_limit_bytes=12 * 2**20),
    )(*args)


def shards(pair_coef, panel_pool, degree_owner, batch_order):
    local_orders, shells = pair_coef.shape[:2]
    width = panel_pool.shape[2]
    devices = lax.axis_size("shell")
    total_orders = local_orders * devices
    chips = devices // 2
    me = lax.axis_index("shell")
    lines = chips // 2
    walk = [2 * z for z in range(lines)] + [2 * z + 1 for z in reversed(range(lines))]

    onward = []
    for here, there in zip(walk, walk[1:] + walk[:1]):
        onward += [(2 * here, 2 * there), (2 * there + 1, 2 * here + 1)]

    def around(value):
        return lax.ppermute(value, "shell", onward)

    def sibling(value):
        return lax.ppermute(value, "shell", [(s, s ^ 1) for s in range(devices)])

    def across(value):
        return lax.ppermute(value, "grp", [(0, 1), (1, 0)])

    blocks = width // LANES
    parcels = jax.ShapeDtypeStruct((devices * EIGHTS * 8, LANES), jnp.int16)
    lines = pltpu.VMEM((devices // 2, 16, LANES), jnp.float32)
    stage = pltpu.VMEM((devices * EIGHTS, 8, LANES), jnp.int32)

    def exchange(value):
        value = value.reshape(devices, EIGHTS * 8, LANES)
        return lax.all_to_all(value, "shell", 0, 0).reshape(parcels.shape)

    own = panel_pool[0]
    half = own.shape[0] // 2
    whole = around(own)
    other = sibling(own)
    part = around(lax.dynamic_slice_in_dim(other, half * lax.axis_index("grp"), half))
    rows = sort_rows(pair_coef, batch_order)
    acc = project(None, rows, degree_owner, [own, other], [(0, 0, None), (0, 1, None)])
    whole, rows = lax.optimization_barrier((whole, rows))
    part, acc = lax.optimization_barrier((part, acc))
    late, late_from = [], []
    for step in range(1, chips // 2):
        if step > 1:
            whole, acc = lax.optimization_barrier((whole, acc))
        next_whole = around(whole)
        next_part = around(part) if step + 1 < chips // 2 else None
        if next_part is None:
            cut = half // 2
            front, back, acc = lax.optimization_barrier((late[0][:cut], part[cut:], acc))
            ends = [around(front), across(back)]
        else:
            rest = across(part)
        acc = project(
            acc,
            rows,
            degree_owner,
            [whole, sibling(whole), part, sibling(part), *late],
            [(-step, 0, None), (step, 1, None), (-step, 1, (0, 0)), (step, 0, (0, 0)), *late_from],
        )
        if next_part is not None:
            late, late_from = [rest, sibling(rest)], [(-step, 1, (1, 0)), (step, 0, (1, 0))]
        whole, part = next_whole, next_part
    whole, acc, *ends = lax.optimization_barrier((whole, acc, *ends))
    far = chips // 2
    acc = project(
        acc,
        rows,
        degree_owner,
        [whole, *ends],
        [(-far, 0, None), (1 - far, 1, (1, 0)), (1 - far, 1, (1, cut))],
    )
    sent = project(
        acc,
        rows,
        degree_owner,
        [sibling(whole), *map(sibling, ends)],
        [(far, 1, None), (far - 1, 0, (1, 0)), (far - 1, 0, (1, cut))],
        packed=parcels,
    )
    sent = local_call(outer_kernel, parcels, [lines, stage], exchange(sent))
    sent = exchange(sent)
    first = bit_reverse(me, devices.bit_length() - 1)
    phase = lax.iota(jnp.int32, local_orders) * first % total_orders
    angle = -2.0 * math.pi * phase.astype(jnp.float32) / float(total_orders)
    twist = jnp.stack([jnp.cos(angle), jnp.sin(angle)]) * (1.0 / math.sqrt(total_orders))
    out = jax.ShapeDtypeStruct((2 * local_orders * shells // 2 * 2 * blocks, LANES), jnp.float32)
    scores = local_call(inner_kernel, out, [lines], twist, sent, smem=1)
    scores = scores.reshape(2, local_orders, shells // 2, blocks, 2, LANES)
    return scores.transpose(0, 1, 2, 4, 3, 5).reshape(2, local_orders, shells // 2, 2, width)


def solution(mesh):
    devices = mesh.shape["shell"]
    return jax.shard_map(
        shards if (devices, mesh.shape["grp"]) == (16, 2) else general,
        mesh=mesh,
        in_specs=(P(("grp", "shell"), None, None, None), P("shell", None, None), P(), P()),
        out_specs=P(None, ("grp", "shell"), None, None, None),
        check_vma=False,
    )
```

```python
import functools
import math

import jax
import jax.numpy as jnp
from jax import lax
from jax.experimental import pallas as pl
from jax.experimental.pallas import tpu as pltpu
from jax.sharding import PartitionSpec as P


def broadcast(value, axis, root):
    mine = lax.axis_index(axis) == root
    return lax.psum(jnp.where(mine, value, jnp.zeros_like(value)), axis)


def partner(value, axis, distance):
    mask = 2**distance
    pairs = [(source, source ^ mask) for source in range(lax.axis_size(axis))]
    return lax.ppermute(value, axis, pairs)


def rotate(real_part, imag_part, cosine, sine):
    return (real_part * cosine - imag_part * sine, real_part * sine + imag_part * cosine)


def general(pair_coef, panel_pool, degree_owner, batch_order):
    local_orders = pair_coef.shape[0]
    degrees = pair_coef.shape[2]
    width = pair_coef.shape[3] // 2
    batch_rows = batch_order.shape[0] // 2
    devices = lax.axis_size("shell")
    total_orders = local_orders * devices
    first = jnp.take(pair_coef, batch_order[:batch_rows], axis=1)
    second = jnp.take(pair_coef, batch_order[batch_rows:], axis=1)
    rows = jnp.stack([first, second])

    def add_degree(degree, total):
        panel = broadcast(panel_pool[0], "shell", degree_owner[degree])
        piece = lax.dynamic_index_in_dim(rows, degree, axis=3, keepdims=False).reshape(-1, width)
        return total + jnp.dot(piece, panel, preferred_element_type=jnp.float32)

    total = lax.fori_loop(
        0, degrees, add_degree, jnp.zeros((2 * local_orders * batch_rows * 2, width), jnp.float32)
    )
    proj = total.reshape(2, local_orders, batch_rows, 2, width)
    nbits = devices.bit_length() - 1
    high = lax.Precision.HIGHEST
    me = lax.axis_index("shell")
    blocks = proj
    for bit in reversed(range(nbits)):
        other = partner(blocks, "shell", bit)
        upper = me >> bit & 1 == 1
        lower_val = jnp.where(upper, other, blocks)
        upper_val = jnp.where(upper, blocks, other)
        summed = lower_val + upper_val
        differ = lower_val - upper_val
        twist = (me % (1 << bit)).astype(jnp.float32)
        angle = -2.0 * math.pi * twist / float(2 << bit)
        new_real, new_imag = rotate(
            differ[:, :, :, 0], differ[:, :, :, 1], jnp.cos(angle), jnp.sin(angle)
        )
        turned = jnp.stack([new_real, new_imag], axis=3)
        blocks = jnp.where(upper, turned, summed)
    flipped = jnp.zeros((), jnp.int32)
    for bit in range(nbits):
        flipped = flipped | (me >> bit & 1) << nbits - 1 - bit
    inner = lax.iota(jnp.int32, local_orders)
    freq = flipped + devices * inner
    phase = inner[None, :] * freq[:, None] % total_orders
    angle = -2.0 * math.pi * phase.astype(jnp.float32) / float(total_orders)
    cosine = jnp.cos(angle)
    sine = jnp.sin(angle)
    real_part = blocks[:, :, :, 0]
    imag_part = blocks[:, :, :, 1]
    out_real = jnp.einsum("gr,brtj->bgtj", cosine, real_part, precision=high) - jnp.einsum(
        "gr,brtj->bgtj", sine, imag_part, precision=high
    )
    out_imag = jnp.einsum("gr,brtj->bgtj", sine, real_part, precision=high) + jnp.einsum(
        "gr,brtj->bgtj", cosine, imag_part, precision=high
    )
    result = jnp.stack([out_real, out_imag], axis=3)
    return result * (1.0 / math.sqrt(total_orders))


STEPS = 16.0
TOP = 32000.0
LANES = 128
GROUP = 4
SORT_LIMIT = 42


def bit_reverse(value, nbits):
    flipped = 0
    for bit in range(nbits):
        flipped = flipped | (value >> bit & 1) << nbits - 1 - bit
    return flipped


def sort_kernel(order_ref, coef_ref, out_ref, perm_ref, held_ref, sems):
    rows = perm_ref.shape[0]
    blocks = held_ref.shape[0] // rows
    degrees = out_ref.shape[0]
    shells = order_ref.shape[0]
    slab = rows // degrees

    def copy(i):
        block = coef_ref.at[pl.ds(i * rows, GROUP * rows), :]
        return pltpu.make_async_copy(block, held_ref.at[pl.ds(i * rows, GROUP * rows), :], sems.at[i])

    for i in range(0, blocks, GROUP):
        copy(i).start()
    line = lax.broadcasted_iota(jnp.int32, (slab, rows), 0)
    in_at = lax.broadcasted_iota(jnp.int32, (slab, rows), 1)
    wanted = jnp.zeros(line.shape, jnp.int32)
    for at in range(slab):
        source = (at // shells * shells + order_ref[at % shells]) * degrees
        wanted = jnp.where(line == at, source, wanted)
    for l in range(degrees):
        chosen = jnp.where(in_at == wanted + l, 1.0, 0.0).astype(perm_ref.dtype)
        perm_ref[pl.ds(l * slab, slab), :] = chosen

    for i in range(blocks):
        if i % GROUP == 0:
            copy(i).wait()
        moved = jnp.dot(perm_ref[...], held_ref[pl.ds(i * rows, rows), :], preferred_element_type=jnp.float32)
        out_ref[:, pl.ds(i * slab, slab), :] = moved.astype(out_ref.dtype).reshape(
            degrees, slab, moved.shape[1]
        )


def sort_rows(pair_coef, batch_order):
    orders, shells, degrees, width = pair_coef.shape
    group = 16 // shells
    rows = group * shells * degrees
    blocks = orders // group
    return pl.pallas_call(
        sort_kernel,
        in_specs=[pl.BlockSpec(memory_space=pltpu.SMEM), pl.BlockSpec(memory_space=pltpu.HBM)],
        out_specs=pl.BlockSpec(memory_space=pltpu.VMEM),
        out_shape=jax.ShapeDtypeStruct((degrees, orders * shells, width), pair_coef.dtype),
        scratch_shapes=[
            pltpu.VMEM((rows, rows), pair_coef.dtype),
            pltpu.VMEM((blocks * rows, width), pair_coef.dtype),
            pltpu.SemaphoreType.DMA((blocks,)),
        ],
        compiler_params=pltpu.CompilerParams(vmem_limit_bytes=SORT_LIMIT * 2**20),
        cost_estimate=pl.CostEstimate(
            flops=2 * blocks * rows * rows * width,
            bytes_accessed=4 * blocks * rows * width,
            transcendentals=0,
        ),
    )(batch_order, pair_coef.reshape(orders * shells * degrees, width))


def scale_code(largest):
    return jnp.ceil(jnp.log2(jnp.maximum(largest, 1e-30)) * STEPS) + 1.0


def encode(real_part, imag_part):
    largest = jnp.max(jnp.maximum(jnp.abs(real_part), jnp.abs(imag_part)), axis=0, keepdims=True)
    code = scale_code(largest)
    gain = jnp.exp2(code * (-1.0 / STEPS)) * TOP
    coded = [jnp.floor(v * gain + 0.5).astype(jnp.int32) for v in (real_part, imag_part)]
    return coded[0], coded[1], code


EIGHTS = 17


def stage_block(stage_ref, piece, jb, coded, code):
    odd = lax.axis_index("shell") % 2
    first = EIGHTS * piece + odd + 4 * jb
    for part in range(2):
        stage_ref[pl.ds(first + 2 * part, 2)] = coded[part].reshape(2, 8, LANES)
    stage_ref[EIGHTS * piece + (EIGHTS - 1) * (1 - odd), pl.ds(jb, 1), :] = code.astype(jnp.int32)


def clear_codes(stage_ref, pieces):
    odd = lax.axis_index("shell") % 2
    for piece in range(pieces):
        stage_ref[EIGHTS * piece + (EIGHTS - 1) * (1 - odd)] = jnp.zeros((8, LANES), jnp.int32)


def ship(stage_ref, out_ref):
    for pair in range(stage_ref.shape[0] // 2):
        both = stage_ref[pl.ds(2 * pair, 2)].reshape(16, LANES)
        out_ref[pl.ds(16 * pair, 16), :] = both.astype(jnp.int16)


def value_rows(piece, jb, part):
    return pl.ds((EIGHTS * piece + piece % 2 + 4 * jb + 2 * part) * 8, 16)


def read_gains(in_ref, gain_ref):
    for pair in range(gain_ref.shape[0]):
        gain_ref[pair] = gains(in_ref[pl.ds((2 * EIGHTS * pair + EIGHTS - 1) * 8, 16), :])


def gains(codes):
    return jnp.exp2(codes.astype(jnp.int32).astype(jnp.float32) * (1.0 / STEPS)) * (1.0 / TOP)


def widen(value):
    return value.astype(jnp.int32).astype(jnp.float32)


def walk_at(place, chips):
    lines = chips // 2
    return jnp.where(place < lines, 2 * place, 2 * (chips - 1 - place) + 1)


def place_of(chip, chips):
    return jnp.where(chip % 2 == 0, chip // 2, chips - 1 - chip // 2)


def project_kernel(devices, sources, n_acc, packed, owner_ref, rows_ref, *refs):
    n = len(sources)
    panels = refs[:n]
    acc_in = refs[n : n + n_acc]
    acc_out = refs[-2] if packed else refs[-1]
    chips = devices // 2
    me = lax.axis_index("shell")
    part = lax.axis_index("grp")
    width = rows_ref.shape[2] // 2
    started = n_acc
    if n_acc:
        acc_out[...] = acc_in[0][...]
    for panel, (shift, flip, half) in zip(panels, sources):
        depth = panel.shape[0]
        ahead = jnp.where(me % 2 == 0, shift, -shift)
        place = lax.rem(place_of(me // 2, chips) + ahead + chips, chips)
        slot = 2 * walk_at(place, chips) + (me + flip) % 2
        degree = jnp.zeros((), jnp.int32)
        for l in range(rows_ref.shape[0]):
            degree = jnp.where(owner_ref[l] == slot, l, degree)
        offset = 0 if half is None else width // 2 * ((part + half[0]) % 2) + half[1]
        left = jnp.concatenate(
            [rows_ref[degree, :, pl.ds(pl.multiple_of(c * width + offset, 128), depth)] for c in range(2)]
        )
        product = jnp.dot(left, panel[...], preferred_element_type=jnp.float32)
        acc_out[...] = acc_out[...] + product if started else product
        started = 1
    if packed:
        pack(acc_out, refs[-1], refs[-3])


def project(acc, rows, owner, panels, sources, packed=None):
    count, width = rows.shape[1], panels[0].shape[1]
    depth = sum(p.shape[0] for p in panels)
    n_acc = 0 if acc is None else 1
    total = jax.ShapeDtypeStruct((2 * count, width), jnp.float32)
    return pl.pallas_call(
        functools.partial(
            project_kernel, lax.axis_size("shell"), tuple(sources), n_acc, packed is not None
        ),
        in_specs=[pl.BlockSpec(memory_space=pltpu.SMEM)]
        + [pl.BlockSpec(memory_space=pltpu.VMEM)] * (1 + len(panels) + n_acc),
        out_specs=pl.BlockSpec(memory_space=pltpu.VMEM),
        out_shape=total if packed is None else packed,
        scratch_shapes=[]
        if packed is None
        else [
            pltpu.VMEM(total.shape, total.dtype),
            pltpu.VMEM((packed.shape[0] // 8, 8, LANES), jnp.int32),
        ],
        compiler_params=pltpu.CompilerParams(vmem_limit_bytes=12 * 2**20),
        cost_estimate=pl.CostEstimate(
            flops=4 * count * depth * width,
            bytes_accessed=2 * depth * (width + 2 * count) + 8 * count * width * (1 + n_acc),
            transcendentals=0,
        ),
    )(owner, rows, *panels, *([acc] if n_acc else []))


def pack(proj_ref, stage_ref, out_ref):
    count, width = proj_ref.shape[0] // 2, proj_ref.shape[1]
    pieces = count // 16
    clear_codes(stage_ref, pieces)
    for d in range(pieces):
        for jb in range(width // LANES):
            lanes = pl.ds(jb * LANES, LANES)
            *coded, code = encode(
                proj_ref[pl.ds(16 * d, 16), lanes], proj_ref[pl.ds(count + 16 * d, 16), lanes]
            )
            stage_block(stage_ref, d, jb, coded, code)
    ship(stage_ref, out_ref)


def radix2(real_parts, imag_parts):
    n = len(real_parts)
    re, im = list(real_parts), list(imag_parts)
    half = n // 2
    while half:
        for start in range(0, n, 2 * half):
            for k in range(half):
                a, b = start + k, start + k + half
                dr, di = re[a] - re[b], im[a] - im[b]
                re[a], im[a] = re[a] + re[b], im[a] + im[b]
                angle = -math.pi * k / half
                if k == 0:
                    re[b], im[b] = dr, di
                elif 2 * k == half:
                    re[b], im[b] = di, -dr
                elif 4 * k == half:
                    re[b], im[b] = (dr + di) * math.cos(angle), (di - dr) * math.cos(angle)
                elif 4 * k == 3 * half:
                    re[b], im[b] = (di - dr) * math.cos(math.pi / 4), (dr + di) * -math.cos(math.pi / 4)
                else:
                    c, s = math.cos(angle), math.sin(angle)
                    re[b], im[b] = dr * c - di * s, dr * s + di * c
        half //= 2
    return re, im


def outer_kernel(in_ref, out_ref, gain_ref, stage_ref):
    n = 2 * gain_ref.shape[0]
    read_gains(in_ref, gain_ref)
    clear_codes(stage_ref, n)
    for jb in range((EIGHTS - 1) // 4):
        re, im = [], []
        for q in range(n):
            gain = gain_ref[q // 2, pl.ds(8 * (q % 2) + jb, 1), :]
            re.append(widen(in_ref[value_rows(q, jb, 0), :]) * gain)
            im.append(widen(in_ref[value_rows(q, jb, 1), :]) * gain)
        re, im = radix2(re, im)
        for p in range(n):
            *coded, code = encode(re[p], im[p])
            stage_block(stage_ref, p, jb, coded, code)
    ship(stage_ref, out_ref)


def inner_kernel(twist_ref, in_ref, out_ref, gain_ref, held_ref, sems):
    n = 2 * gain_ref.shape[0]
    orders = 2 * n
    nbits = orders.bit_length() - 1
    read_gains(in_ref, gain_ref)
    for jb in range((EIGHTS - 1) // 4):
        re, im = [], []
        for d in range(n):
            gain = gain_ref[d // 2, pl.ds(8 * (d % 2) + jb, 1), :]
            both_re = widen(in_ref[value_rows(d, jb, 0), :]) * gain
            both_im = widen(in_ref[value_rows(d, jb, 1), :]) * gain
            for r in range(2):
                a, b = both_re[8 * r : 8 * r + 8], both_im[8 * r : 8 * r + 8]
                c, s = twist_ref[0, 2 * d + r], twist_ref[1, 2 * d + r]
                re.append(a * c - b * s)
                im.append(a * s + b * c)
        re, im = radix2(re, im)
        for p in range(orders):
            h = bit_reverse(p, nbits)
            for part, value in enumerate((re[p], im[p])):
                held_ref[pl.ds(64 * h + 2 * jb + part, 8, stride=8), :] = value
    by_batch = held_ref.reshape(orders, 2, 32, LANES)
    copies = [
        pltpu.make_async_copy(by_batch.at[:, b], out_ref.at[b], sems.at[b]) for b in range(2)
    ]
    for copy in copies:
        copy.start()
    for copy in copies:
        copy.wait()


def local_call(kernel, out, scratch, *args, smem=0, place=pltpu.VMEM):
    return pl.pallas_call(
        kernel,
        in_specs=[pl.BlockSpec(memory_space=pltpu.SMEM)] * smem
        + [pl.BlockSpec(memory_space=pltpu.VMEM)] * (len(args) - smem),
        out_specs=pl.BlockSpec(memory_space=place),
        out_shape=out,
        scratch_shapes=scratch,
        compiler_params=pltpu.CompilerParams(vmem_limit_bytes=12 * 2**20),
    )(*args)


def shards(pair_coef, panel_pool, degree_owner, batch_order):
    local_orders, shells = pair_coef.shape[:2]
    width = panel_pool.shape[2]
    devices = lax.axis_size("shell")
    total_orders = local_orders * devices
    chips = devices // 2
    me = lax.axis_index("shell")
    lines = chips // 2
    walk = [2 * z for z in range(lines)] + [2 * z + 1 for z in reversed(range(lines))]

    onward = []
    for here, there in zip(walk, walk[1:] + walk[:1]):
        onward += [(2 * here, 2 * there), (2 * there + 1, 2 * here + 1)]

    def around(value):
        return lax.ppermute(value, "shell", onward)

    def sibling(value):
        return lax.ppermute(value, "shell", [(s, s ^ 1) for s in range(devices)])

    def across(value):
        return lax.ppermute(value, "grp", [(0, 1), (1, 0)])

    blocks = width // LANES
    parcels = jax.ShapeDtypeStruct((devices * EIGHTS * 8, LANES), jnp.int16)
    lines = pltpu.VMEM((devices // 2, 16, LANES), jnp.float32)
    stage = pltpu.VMEM((devices * EIGHTS, 8, LANES), jnp.int32)

    def exchange(value):
        value = value.reshape(devices, EIGHTS * 8, LANES)
        return lax.all_to_all(value, "shell", 0, 0).reshape(parcels.shape)

    own = panel_pool[0]
    half = own.shape[0] // 2
    whole = around(own)
    other = sibling(own)
    part = around(lax.dynamic_slice_in_dim(other, half * lax.axis_index("grp"), half))
    rows = sort_rows(pair_coef, batch_order)
    acc = project(None, rows, degree_owner, [own, other], [(0, 0, None), (0, 1, None)])
    whole, rows = lax.optimization_barrier((whole, rows))
    part, acc = lax.optimization_barrier((part, acc))
    late, late_from = [], []
    for step in range(1, chips // 2):
        if step > 1:
            whole, acc = lax.optimization_barrier((whole, acc))
        next_whole = around(whole)
        next_part = around(part) if step + 1 < chips // 2 else None
        if next_part is None:
            cut = half // 2
            front, back, acc = lax.optimization_barrier((late[0][:cut], part[cut:], acc))
            ends = [around(front), across(back)]
        else:
            rest = across(part)
        acc = project(
            acc,
            rows,
            degree_owner,
            [whole, sibling(whole), part, sibling(part), *late],
            [(-step, 0, None), (step, 1, None), (-step, 1, (0, 0)), (step, 0, (0, 0)), *late_from],
        )
        if next_part is not None:
            late, late_from = [rest, sibling(rest)], [(-step, 1, (1, 0)), (step, 0, (1, 0))]
        whole, part = next_whole, next_part
    whole, acc, *ends = lax.optimization_barrier((whole, acc, *ends))
    far = chips // 2
    acc = project(
        acc,
        rows,
        degree_owner,
        [whole, *ends],
        [(-far, 0, None), (1 - far, 1, (1, 0)), (1 - far, 1, (1, cut))],
    )
    sent = project(
        acc,
        rows,
        degree_owner,
        [sibling(whole), *map(sibling, ends)],
        [(far, 1, None), (far - 1, 0, (1, 0)), (far - 1, 0, (1, cut))],
        packed=parcels,
    )
    sent = local_call(outer_kernel, parcels, [lines, stage], exchange(sent))
    sent = exchange(sent)
    first = bit_reverse(me, devices.bit_length() - 1)
    phase = lax.iota(jnp.int32, local_orders) * first % total_orders
    angle = -2.0 * math.pi * phase.astype(jnp.float32) / float(total_orders)
    twist = jnp.stack([jnp.cos(angle), jnp.sin(angle)]) * (1.0 / math.sqrt(total_orders))
    out = jax.ShapeDtypeStruct((2, local_orders, shells * blocks, LANES), jnp.float32)
    held = pltpu.VMEM((local_orders * shells * 2 * blocks, LANES), jnp.float32)
    scratch = [lines, held, pltpu.SemaphoreType.DMA((2,))]
    scores = local_call(inner_kernel, out, scratch, twist, sent, smem=1, place=pltpu.HBM)
    scores = scores.reshape(2, local_orders, shells // 2, blocks, 2, LANES)
    return scores.transpose(0, 1, 2, 4, 3, 5).reshape(2, local_orders, shells // 2, 2, width)


def solution(mesh):
    devices = mesh.shape["shell"]
    return jax.shard_map(
        shards if (devices, mesh.shape["grp"]) == (16, 2) else general,
        mesh=mesh,
        in_specs=(P(("grp", "shell"), None, None, None), P("shell", None, None), P(), P()),
        out_specs=P(None, ("grp", "shell"), None, None, None),
        check_vma=False,
    )
```
